32 devices in a mesh: dp: 4 (over y, x), mp: 8 (over z, core).
Axes of the slice: x: 2, y: 2, z: 4, core: 2. Of those that a mesh axis runs over, the one named last changes fastest.
Arguments:
- tokens: bfloat16 [1536, 2048], P('dp'), may hold values from -6 to 6
- cotangent: bfloat16 [1536, 2048], P('dp'), may hold values from -6 to 6
- norm_gains: float32 [2, 2048], replicated, may hold values from 0.1 to 1.9
- w_attn: bfloat16 [4, 2048, 2048], P(None, 'mp'), may hold values from -0.125 to 0.125
- w_in: bfloat16 [2, 2048, 5632], P(None, 'mp'), may hold values from -0.125 to 0.125
- w_down: bfloat16 [5632, 2048], P('mp'), may hold values from -0.078125 to 0.078125
- segments: int32 [4, 384], P('dp'), may hold values from 0 to 5, never falling along the last dimension, each value on 1 to 288 neighbouring positions
- owners: int32 [637], replicated, may hold values from 0 to 31, as said below
- master: float32 [1280, 1024], P(('dp', 'mp'))
- first_moment: float32 [1280, 1024], P(('dp', 'mp'))
- second_moment: float32 [1280, 1024], P(('dp', 'mp'))
Outputs:
- layer_out: bfloat16 [1536, 2048], P('dp')
- input_grad: float32 [1536, 2048], P('dp')
- new_master: float32 [1280, 1024], P(('dp', 'mp'))
- new_first: float32 [1280, 1024], P(('dp', 'mp'))
- new_second: float32 [1280, 1024], P(('dp', 'mp'))
The draws below stay inside these ranges and needn't reach their ends.
Inputs may be any that keep to these rules, and one draw needn't show every extreme that they name: `segments`: segment numbers never fall along a row. `owners`: no device keeps more than 40 blocks, and some device keeps exactly 40.
All inputs are finite; a program needn't handle non-finite values.
Results may differ from the reference program's by a relative error of at most 0.014.
The reference program's roundings to bfloat16 on the way count: a program that leaves them out, or rounds other values in their place, can miss the bound.
Values may be sent and summed in bfloat16 or wider, within the bound.
No kernel may reach another device: no remote copies, remote signals or barrier semaphores. Data moves between devices by JAX's collectives and lax.ppermute only.
A program may use at most 320 MiB of HBM per device.

```python
import math
import jax
import jax.numpy as jnp
import numpy as np
from jax import lax

D = 2048
FF = 5632
HEADS = 16
HEAD_DIM = 128
RANK = 16
ROW_TOKENS = 384
BLOCK = 1024
STEP = 5
TOKENS = 1536
BLOCKS = 637
CAPACITY = 40
SLOT_ROWS = 1280
N_DP = 4
N_MP = 8


def owner_list(key):
    devices = N_DP * N_MP
    key_full, key_order, key_mix = jax.random.split(key, 3)
    full_device = jax.random.randint(key_full, (), 0, devices)
    shuffled = jax.random.permutation(key_order, SLOT_ROWS)
    slot_ids = jnp.arange(SLOT_ROWS)
    scores = jnp.where(slot_ids // CAPACITY == full_device, slot_ids - SLOT_ROWS, shuffled)
    order = jnp.argsort(scores, stable=True)
    chosen = order[:BLOCKS] // CAPACITY
    return jax.random.permutation(key_mix, chosen).astype(jnp.int32)


def slot_blocks(owners):
    order = jnp.arange(BLOCKS, dtype=jnp.int32)
    same = (owners[:, None] == owners[None, :]) & (order[None, :] < order[:, None])
    ranks = jnp.sum(same.astype(jnp.int32), axis=1)
    slot_index = owners * CAPACITY + ranks
    return jnp.full((SLOT_ROWS,), -1, jnp.int32).at[slot_index].set(order)


def static_tables():
    dims = [(D, D)] * 4 + [(D, FF)] * 2 + [(FF, D)]
    means = [1.0, 1.0, 1.0, 4.0, 1.0, 1.0, 2.0]
    root = float(TOKENS) ** 0.5
    spread = []
    marks = []
    estimate = []
    for inner, outer in dims:
        spread.append(np.full(inner * RANK, inner ** (-0.5), np.float32))
        marks.append(np.zeros(inner * RANK, np.float32))
        estimate.append(np.full(inner * RANK, 3.0 * root, np.float32))
    for inner, outer in dims:
        spread.append(np.full(outer * RANK, 0.1, np.float32))
        marks.append(np.zeros(outer * RANK, np.float32))
        estimate.append(np.full(outer * RANK, root, np.float32))
    for position in range(7):
        outer = dims[position][1]
        spread.append(np.full(outer, means[position], np.float32))
        marks.append(np.ones(outer, np.float32))
        estimate.append(np.full(outer, 0.5 * root, np.float32))
    return [jnp.asarray(np.concatenate(part).reshape(BLOCKS, BLOCK)) for part in (spread, marks, estimate)]


def slot_tables(owners):
    safe = jnp.maximum(slot_blocks(owners), 0)
    tables = static_tables()
    return (tables[0][safe], tables[1][safe], tables[2][safe])


def draw_owners(key, part):
    return owner_list(key)


def draw_master(key, part):
    owners = owner_list(key)
    key = jax.random.fold_in(key, 11)
    spread, marks, estimate = slot_tables(owners)
    key_base, key_shake = jax.random.split(key)
    shape = (SLOT_ROWS, BLOCK)
    base = jnp.clip(jax.random.normal(key_base, shape, jnp.float32), -4.0, 4.0)
    shake = jax.random.uniform(key_shake, shape, jnp.float32, -1.0, 1.0)
    return jnp.where(marks > 0.5, spread * (1.0 + 0.5 * shake), spread * base)


def draw_first_moment(key, part):
    owners = owner_list(key)
    key = jax.random.fold_in(key, 23)
    spread, marks, estimate = slot_tables(owners)
    shape = (SLOT_ROWS, BLOCK)
    base = jnp.clip(jax.random.normal(key, shape, jnp.float32), -4.0, 4.0)
    return estimate * base


def draw_second_moment(key, part):
    owners = owner_list(key)
    key = jax.random.fold_in(key, 37)
    spread, marks, estimate = slot_tables(owners)
    factor = jax.random.uniform(key, (SLOT_ROWS, BLOCK), jnp.float32, 1.0, 4.0)
    return estimate * estimate * factor


def block_scale(own_key, shape, pieces, smallest, high):
    loudness = 1.0
    for dim, parts in pieces:
        draws = jax.random.uniform(jax.random.fold_in(jax.random.fold_in(own_key, 6), dim), (parts,), jnp.float32, smallest / len(pieces), high / len(pieces))
        loudness = loudness * jnp.repeat(jnp.exp(draws), shape[dim] // parts).reshape((-1,) + (1,) * (len(shape) - 1 - dim))
    return loudness


def length_profile(count, total, reach, slope):
    weights = [(1 << 20) // math.isqrt(grade ** slope) + 1 for grade in range(2, count + 1)]
    surplus, given = total - reach - (count - 1), [1] * (count - 1)
    while surplus > 0:
        candidates = [i for i in range(count - 1) if given[i] < reach]
        whole, left = sum([weights[i] for i in candidates]), surplus
        for i in candidates:
            addition = min(reach - given[i], max(1, left * weights[i] // whole), surplus)
            given[i] = given[i] + addition
            surplus = surplus - addition
    return np.array([reach] + given)


def uneven(key, amount, total, limit, lean):
    if amount == 2:
        one = jax.random.randint(key, (), max(1, total - limit), min(limit, total - 1) + 1)
        return jnp.stack([one, total - one])
    sizes = jnp.asarray(length_profile(amount, total, limit, lean), jnp.int32)
    couples = (amount - 1) // 2
    giver, taker = sizes[1:1 + 2 * couples:2], sizes[2:2 + 2 * couples:2]
    margin = jnp.minimum(giver - 1, limit - taker)
    passed = jax.random.randint(jax.random.fold_in(key, 1), (couples,), 0, 1 << 20) % (margin + 1)
    sizes = sizes.at[1:1 + 2 * couples:2].set(giver - passed).at[2:2 + 2 * couples:2].set(taker + passed)
    return sizes[jax.random.permutation(jax.random.fold_in(key, 2), amount)]


def centred(stream_key, shape, deviation, bound, pieces=(), kind=jnp.bfloat16):
    values = jax.random.normal(stream_key, shape, jnp.float32) * deviation
    if len(pieces) > 0:
        values = block_scale(stream_key, shape, pieces, -0.22, 0.18) * values
    return jnp.clip(values, min=-bound, max=bound).astype(kind)


def setup_inputs(seed: int = 0) -> dict:
    key_of = jax.random.split(jax.random.key(seed), 12)
    tokens = centred(key_of[0], (TOKENS, D), 1.0, 6.0, ((0, 4),))
    cotangent = centred(key_of[1], (TOKENS, D), 1.0, 6.0, ((0, 4),))
    norm_gains = jnp.clip(1.0 + 0.18 * jax.random.normal(key_of[2], (2, D), jnp.float32), 0.1, 1.9)
    w_attn = centred(key_of[3], (4, D, D), D ** -0.5, 0.125, ((1, 8),))
    w_in = centred(key_of[4], (2, D, FF), D ** -0.5, 0.125, ((1, 8),))
    w_down = centred(key_of[5], (FF, D), FF ** -0.5, 0.078125, ((0, 8),))
    segments = jax.vmap(lambda own: jnp.searchsorted(jnp.cumsum(uneven(own, max(2, ROW_TOKENS // 64), ROW_TOKENS, ROW_TOKENS // 2 + ROW_TOKENS // 4, 1)), jnp.arange(ROW_TOKENS), side="right"))(jax.random.split(key_of[6], N_DP)).reshape((N_DP, ROW_TOKENS)).astype(jnp.int32)
    owners = draw_owners(jax.random.fold_in(key_of[11], 71), 0)
    master = draw_master(jax.random.fold_in(key_of[11], 71), 0)
    first_moment = draw_first_moment(jax.random.fold_in(key_of[11], 71), 0)
    second_moment = draw_second_moment(jax.random.fold_in(key_of[11], 71), 0)
    return {"tokens": tokens, "cotangent": cotangent, "norm_gains": norm_gains, "w_attn": w_attn, "w_in": w_in, "w_down": w_down, "segments": segments, "owners": owners, "master": master, "first_moment": first_moment, "second_moment": second_moment}


dora_scale = 2.0
rope_base = 10000.0
norm_eps = 1e-05
column_eps = 1e-06
beta_one = 0.5
beta_two = 0.5
adam_eps = 1e-08
weight_decay = 0.01
rate_lower = 0.02
rate_upper = 0.1
rate_magnitude = 1.0
highest = lax.Precision.HIGHEST

@jax.custom_vjp
def low(v):
    return lax.optimization_barrier(v.astype(jnp.bfloat16)).astype(jnp.float32)

@jax.custom_vjp
def low_back(v):
    return v

def low_keep(v):
    return (low(v), None)

def low_pass(kept, grad):
    return (grad,)

def back_keep(v):
    return (v, None)

def back_low(kept, grad):
    return (low(grad),)
low.defvjp(low_keep, low_pass)
low_back.defvjp(back_keep, back_low)

def proj_dims():
    return [(D, D), (D, D), (D, D), (D, D), (D, FF), (D, FF), (FF, D)]

def unpack(flat):
    offset = 0
    lowers = []
    for inner, outer in proj_dims():
        lowers.append(flat[offset:offset + inner * RANK].reshape(inner, RANK))
        offset += inner * RANK
    uppers = []
    for inner, outer in proj_dims():
        uppers.append(flat[offset:offset + outer * RANK].reshape(outer, RANK))
        offset += outer * RANK
    magnitudes = []
    for inner, outer in proj_dims():
        magnitudes.append(flat[offset:offset + outer])
        offset += outer
    return (lowers, uppers, magnitudes)

def slot_positions(owners, capacity):
    order = jnp.arange(owners.shape[0], dtype=jnp.int32)
    same = (owners[:, None] == owners[None, :]) & (order[None, :] < order[:, None])
    ranks = lax.optimization_barrier(jnp.sum(same.astype(jnp.int32), axis=1))
    return (owners * capacity + ranks).astype(jnp.int32)

def block_rates(block_ids):
    count_lower = RANK * (6 * D + FF) // BLOCK
    count_upper = RANK * (5 * D + 2 * FF) // BLOCK
    rates = jnp.where(block_ids < count_lower + count_upper, rate_upper, rate_magnitude)
    rates = jnp.where(block_ids < count_lower, rate_lower, rates)
    return jnp.where(block_ids < 0, 0.0, rates).astype(jnp.float32)

def adam_update(weight, grad, first, second, rates):
    first_new = beta_one * first + (1.0 - beta_one) * grad
    second_new = beta_two * second + (1.0 - beta_two) * grad * grad
    first_hat = first_new / (1.0 - beta_one ** STEP)
    second_hat = second_new / (1.0 - beta_two ** STEP)
    weight_new = weight - rates[:, None] * (first_hat / (jnp.sqrt(second_hat) + adam_eps) + weight_decay * weight)
    return (weight_new, first_new, second_new)

def rms_norm(values, gain):
    return values * lax.rsqrt(lax.optimization_barrier(jnp.mean(values * values, axis=-1, keepdims=True)) + norm_eps) * gain

def segment_positions(row):
    order = jnp.arange(row.shape[0], dtype=jnp.int32)
    change = jnp.concatenate([jnp.ones((1,), dtype=bool), row[1:] != row[:-1]])
    starts = lax.cummax(jnp.where(change, order, 0), axis=0)
    return (order - starts).astype(jnp.int32)

def rotary_tables(positions):
    half = HEAD_DIM // 2
    freqs = rope_base ** (-(jnp.arange(half).astype(jnp.float32) * 2.0 / HEAD_DIM))
    angles = positions.astype(jnp.float32)[:, None] * freqs[None, :]
    return (jnp.cos(angles)[:, None, :], jnp.sin(angles)[:, None, :])

def rotate(values, cosine, sine):
    half = values.shape[-1] // 2
    first_half = values[..., :half]
    second_half = values[..., half:]
    return jnp.concatenate([first_half * cosine - second_half * sine, second_half * cosine + first_half * sine], axis=-1)

def attend(query, keys_in, value, row):
    scale = HEAD_DIM ** (-0.5)
    scores = jnp.einsum('thd,shd->hts', query, keys_in, precision=highest) * scale
    scores = low_back(scores)
    order = jnp.arange(row.shape[0])
    allowed = (row[:, None] == row[None, :]) & (order[None, :] <= order[:, None])
    scores = jnp.where(allowed[None], scores, -1e+30)
    top = lax.optimization_barrier(jnp.max(scores, axis=-1, keepdims=True))
    expd = jnp.exp(scores - top)
    weights = low(expd / lax.optimization_barrier(jnp.sum(expd, axis=-1, keepdims=True)))
    return jnp.einsum('hts,shd->thd', weights, value, precision=highest)

def reference(tokens, cotangent, norm_gains, w_attn, w_in, w_down, segments, owners, master, first_moment, second_moment):
    slot_index = slot_positions(owners, CAPACITY)
    flat = lax.optimization_barrier(master[slot_index].astype(jnp.bfloat16)).astype(jnp.float32).reshape(-1)
    frozen = [w_attn[0].astype(jnp.float32), w_attn[1].astype(jnp.float32), w_attn[2].astype(jnp.float32), w_attn[3].astype(jnp.float32), w_in[0].astype(jnp.float32), w_in[1].astype(jnp.float32), w_down.astype(jnp.float32)]
    gains = norm_gains.astype(jnp.float32)
    positions = jax.vmap(segment_positions)(segments).reshape(-1)
    cosine, sine = rotary_tables(positions)

    def forward(inputs, params):
        lowers, uppers, magnitudes = unpack(params)

        def dora(values, index):
            weight = frozen[index]
            lower = lowers[index]
            upper = uppers[index].T
            combined = weight + dora_scale * jnp.dot(lower, upper, precision=highest)
            norm = jnp.sqrt(lax.optimization_barrier(jnp.sum(combined * combined, axis=0)) + column_eps)
            mixed = jnp.dot(values, weight, precision=highest) + dora_scale * jnp.dot(jnp.dot(values, lower, precision=highest), upper, precision=highest)
            mixed = low_back(mixed)
            return mixed * (magnitudes[index] / norm)
        h_one = low(rms_norm(inputs, gains[0]))
        query = low(rotate(dora(h_one, 0).reshape(TOKENS, HEADS, HEAD_DIM), cosine, sine))
        keys_in = low(rotate(dora(h_one, 1).reshape(TOKENS, HEADS, HEAD_DIM), cosine, sine))
        value = low(dora(h_one, 2).reshape(TOKENS, HEADS, HEAD_DIM))
        shape_rows = (N_DP, ROW_TOKENS, HEADS, HEAD_DIM)
        attended = jax.vmap(attend)(query.reshape(shape_rows), keys_in.reshape(shape_rows), value.reshape(shape_rows), segments).reshape(TOKENS, D)
        attended = low_back(low(attended))
        x_two = inputs + dora(attended, 3)
        h_two = low(rms_norm(x_two, gains[1]))
        act = low(jax.nn.silu(dora(h_two, 4)) * dora(h_two, 5))
        return x_two + dora(act, 6)
    result, pullback = jax.vjp(forward, tokens.astype(jnp.float32), flat)
    grad_input, grad_flat = pullback(cotangent.astype(jnp.float32))
    grad_slots = jnp.zeros((SLOT_ROWS, BLOCK), jnp.float32).at[slot_index].set(grad_flat.reshape(BLOCKS, BLOCK))
    slot_block = jnp.full((SLOT_ROWS,), -1, jnp.int32).at[slot_index].set(jnp.arange(BLOCKS, dtype=jnp.int32))
    new_master, new_first, new_second = adam_update(master, grad_slots, first_moment, second_moment, block_rates(slot_block))
    return (result.astype(jnp.bfloat16), grad_input, new_master, new_first, new_second)
```

```python
import jax
import jax.numpy as jnp
import numpy as np
from jax import lax
from jax.sharding import PartitionSpec as P

D = 2048
FF = 5632
HEADS = 16
HEAD_DIM = 128
RANK = 16
BLOCK = 1024
STEP = 5


dora_scale = 2.0
rope_base = 10000.0
norm_eps = 1e-05
column_eps = 1e-06
beta_one = 0.5
beta_two = 0.5
adam_eps = 1e-08
weight_decay = 0.01
rate_lower = 0.02
rate_upper = 0.1
rate_magnitude = 1.0
highest = lax.Precision.HIGHEST


def proj_dims():
    return [(D, D), (D, D), (D, D), (D, D), (D, FF), (D, FF), (FF, D)]


def unpack(flat):
    offset = 0
    lowers = []
    for inner, outer in proj_dims():
        lowers.append(flat[offset : offset + inner * RANK].reshape(inner, RANK))
        offset += inner * RANK
    uppers = []
    for inner, outer in proj_dims():
        uppers.append(flat[offset : offset + outer * RANK].reshape(outer, RANK))
        offset += outer * RANK
    magnitudes = []
    for inner, outer in proj_dims():
        magnitudes.append(flat[offset : offset + outer])
        offset += outer
    return (lowers, uppers, magnitudes)


def slot_positions(owners, capacity):
    order = jnp.arange(owners.shape[0], dtype=jnp.int32)
    same = (owners[:, None] == owners[None, :]) & (order[None, :] < order[:, None])
    ranks = jnp.sum(same.astype(jnp.int32), axis=1)
    return owners * capacity + ranks


def block_rates(block_ids):
    count_lower = RANK * (6 * D + FF) // BLOCK
    count_upper = RANK * (5 * D + 2 * FF) // BLOCK
    rates = jnp.where(block_ids < count_lower + count_upper, rate_upper, rate_magnitude)
    rates = jnp.where(block_ids < count_lower, rate_lower, rates)
    return jnp.where(block_ids < 0, 0.0, rates).astype(jnp.float32)


def adam_update(weight, grad, first, second, rates):
    first_new = beta_one * first + (1.0 - beta_one) * grad
    second_new = beta_two * second + (1.0 - beta_two) * grad * grad
    first_hat = first_new / (1.0 - beta_one**STEP)
    second_hat = second_new / (1.0 - beta_two**STEP)
    weight_new = weight - rates[:, None] * (
        first_hat / (jnp.sqrt(second_hat) + adam_eps) + weight_decay * weight
    )
    return (weight_new, first_new, second_new)


def rms_norm(values, gain):
    return values * lax.rsqrt(jnp.mean(values * values, axis=-1, keepdims=True) + norm_eps) * gain


def rms_back(values, grad, gain):
    inverse = lax.rsqrt(jnp.mean(values * values, axis=-1, keepdims=True) + norm_eps)
    scaled = grad * gain
    return inverse * (
        scaled - values * inverse * inverse * jnp.mean(scaled * values, axis=-1, keepdims=True)
    )


def segment_positions(row):
    order = jnp.arange(row.shape[0], dtype=jnp.int32)
    change = jnp.concatenate([jnp.ones((1,), dtype=bool), row[1:] != row[:-1]])
    starts = lax.cummax(jnp.where(change, order, 0), axis=0)
    return order - starts


def rotary_tables(positions):
    half = HEAD_DIM // 2
    freqs = rope_base ** (-(jnp.arange(half).astype(jnp.float32) * 2.0 / HEAD_DIM))
    angles = positions.astype(jnp.float32)[:, None] * freqs[None, :]
    return (jnp.cos(angles)[:, None, :], jnp.sin(angles)[:, None, :])


def rotate(values, cosine, sine):
    half = values.shape[-1] // 2
    first_half = values[..., :half]
    second_half = values[..., half:]
    return jnp.concatenate(
        [first_half * cosine - second_half * sine, second_half * cosine + first_half * sine],
        axis=-1,
    )


def unrotate(values, cosine, sine):
    half = values.shape[-1] // 2
    first_half = values[..., :half]
    second_half = values[..., half:]
    return jnp.concatenate(
        [first_half * cosine + second_half * sine, second_half * cosine - first_half * sine],
        axis=-1,
    )


def body(
    tokens,
    cotangent,
    norm_gains,
    w_attn,
    w_in,
    w_down,
    segments,
    owners,
    master,
    first_moment,
    second_moment,
):
    group_rows = tokens.shape[0]
    model_size = lax.axis_size("mp")
    model_index = lax.axis_index("mp")
    share = group_rows // model_size
    share_start = model_index * share
    capacity = master.shape[0]
    everyone = lax.axis_size(("dp", "mp"))
    score_scale = HEAD_DIM ** (-0.5)
    widths = [outer for inner, outer in proj_dims()]
    slot_index = slot_positions(owners, capacity)
    copies = lax.all_gather(master.astype(jnp.bfloat16), ("dp", "mp"), axis=0, tiled=True)
    lowers, uppers, magnitudes = unpack(jnp.take(copies, slot_index, axis=0).reshape(-1))
    frozen = [w_attn[0], w_attn[1], w_attn[2], w_attn[3], w_in[0], w_in[1], w_down]
    lower_local = []
    combined = []
    square_parts = []
    for index in range(7):
        rows_here = frozen[index].shape[0]
        piece = lax.dynamic_slice_in_dim(lowers[index], model_index * rows_here, rows_here, 0)
        lower_local.append(piece)
        joined = frozen[index].astype(jnp.float32) + dora_scale * jnp.dot(
            piece.astype(jnp.float32), uppers[index].astype(jnp.float32).T, precision=highest
        )
        combined.append(joined)
        square_parts.append(jnp.sum(joined * joined, axis=0))

    def rows_of(values):
        return lax.dynamic_slice_in_dim(values, share_start, share, 0)

    def split_parts(values, indices, axis):
        pieces = []
        offset = 0
        for index in indices:
            pieces.append(lax.slice_in_dim(values, offset, offset + widths[index], axis=axis))
            offset += widths[index]
        return pieces

    norms = [None] * 7
    mixed_share = [None] * 7
    low_share = [None] * 7
    mixed_full = [None] * 7
    grads = [None] * 7

    def set_scales(indices):
        summed = lax.psum(jnp.concatenate([square_parts[index] for index in indices]), "mp")
        squares = split_parts(summed, indices, 0)
        for index, value in zip(indices, squares):
            norms[index] = jnp.sqrt(value + column_eps)

    def scale(index):
        return magnitudes[index].astype(jnp.float32) / norms[index]

    def local_partials(inputs_local, indices):
        mixed_list = []
        low_list = []
        for index in indices:
            low_part = jnp.dot(inputs_local, lower_local[index], preferred_element_type=jnp.float32)
            mixed = jnp.dot(
                inputs_local, frozen[index], preferred_element_type=jnp.float32
            ) + dora_scale * jnp.dot(
                low_part, uppers[index].astype(jnp.float32).T, precision=highest
            )
            mixed_list.append(mixed)
            low_list.append(low_part)
        return (
            inputs_local,
            jnp.concatenate(mixed_list, axis=1),
            jnp.concatenate(low_list, axis=1),
        )

    def group_partials(inputs_b, indices):
        rows_here = frozen[indices[0]].shape[0]
        inputs_local = lax.dynamic_slice_in_dim(inputs_b, model_index * rows_here, rows_here, 1)
        return local_partials(inputs_local, indices)

    def finish(indices, local_mixed, local_low):
        summed_mixed, summed_low = lax.psum((local_mixed, local_low), "mp")
        pieces = split_parts(summed_mixed, indices, 1)
        for position, index in enumerate(indices):
            mixed_full[index] = pieces[position]
            mixed_share[index] = rows_of(pieces[position])
            low_share[index] = rows_of(summed_low[:, position * RANK : (position + 1) * RANK])
        return pieces

    def gather_inputs(local):
        return lax.all_gather(local, "mp", axis=1, tiled=True)

    xf = tokens.astype(jnp.float32)
    row = segments[0]
    cosine, sine = rotary_tables(segment_positions(row))
    order = jnp.arange(group_rows)
    allowed = (row[:, None] == row[None, :]) & (order[None, :] <= order[:, None])
    features = rms_norm(xf, norm_gains[0]).astype(jnp.bfloat16)
    first_local, first_mixed, first_low = group_partials(features, (0, 1, 2))
    set_scales((0, 1, 2))
    summed_mixed, summed_low = lax.psum((first_mixed, first_low), "mp")
    pieces = split_parts(summed_mixed, (0, 1, 2), 1)
    heads_in = []
    for index in range(3):
        mixed_full[index] = pieces[index]
        mixed_share[index] = rows_of(pieces[index])
        low_share[index] = rows_of(summed_low[:, index * RANK : (index + 1) * RANK])
        projected = (pieces[index] * scale(index)).reshape(group_rows, HEADS, HEAD_DIM)
        if index < 2:
            projected = rotate(projected, cosine, sine)
        heads_in.append(projected.astype(jnp.bfloat16))
    query_b, key_b, value_b = heads_in

    def attention_scores(query_h, key_h):
        scores = (
            jnp.einsum("thd,shd->hts", query_h, key_h, preferred_element_type=jnp.float32)
            * score_scale
        )
        return jnp.where(allowed[None], scores, -1e30)

    scores = attention_scores(query_b, key_b)
    top = jnp.max(scores, axis=-1, keepdims=True)
    expd = jnp.exp(scores - top)
    total = jnp.sum(expd, axis=-1, keepdims=True)
    probs = (expd / total).astype(jnp.bfloat16)
    attended_h = jnp.einsum("hts,shd->thd", probs, value_b, preferred_element_type=jnp.float32)
    attended_h, log_total = (attended_h, top + jnp.log(total))
    attended = attended_h.reshape(group_rows, D).astype(jnp.bfloat16)
    out_local, out_mixed, out_low = group_partials(attended, (3,))
    set_scales((3,))
    x_two = xf + finish((3,), out_mixed, out_low)[0] * scale(3)
    second_features = rms_norm(x_two, norm_gains[1]).astype(jnp.bfloat16)
    ffn_local, ffn_mixed, ffn_low = group_partials(second_features, (4, 5))
    set_scales((4, 5))
    gate_pre, up_pre = finish((4, 5), ffn_mixed, ffn_low)
    gate = gate_pre * scale(4)
    upward = up_pre * scale(5)
    sigmoid_gate = jax.nn.sigmoid(gate)
    act = (gate * sigmoid_gate * upward).astype(jnp.bfloat16)
    down_local, down_mixed, down_low = group_partials(act, (6,))
    set_scales((6,))
    down_pre = finish((6,), down_mixed, down_low)[0]
    layer_out = (x_two + down_pre * scale(6)).astype(jnp.bfloat16)

    def whole_dot(index, grad):
        return jnp.sum(grad * mixed_full[index], axis=0)

    def project_back(index, grad, inputs_local, group_dot):
        norm = norms[index]
        magnitude = magnitudes[index].astype(jnp.float32)
        grad_b = (grad * (magnitude / norm)).astype(jnp.bfloat16)
        share_dot = jnp.sum(rows_of(grad) * mixed_share[index], axis=0)
        grad_full = combined[index] * (-group_dot * magnitude / (norm * norm * norm))[None, :]
        upper_f = uppers[index].astype(jnp.float32)
        lower_f = lower_local[index].astype(jnp.float32)
        through = dora_scale * jnp.dot(grad_b, uppers[index], preferred_element_type=jnp.float32)
        grad_lower = jnp.dot(
            inputs_local.astype(jnp.float32).T, through, precision=highest
        ) + dora_scale * jnp.dot(grad_full, upper_f, precision=highest)
        grad_upper = dora_scale * jnp.dot(
            rows_of(grad_b).astype(jnp.float32).T, low_share[index], precision=highest
        ) + dora_scale * jnp.dot(grad_full.T, lower_f, precision=highest)
        grads[index] = (grad_lower, grad_upper, share_dot / norm)
        return jnp.dot(grad_b, frozen[index].T, preferred_element_type=jnp.float32) + jnp.dot(
            through, lower_f.T, precision=highest
        )

    grad_out = cotangent.astype(jnp.float32)
    grad_act = gather_inputs(project_back(6, grad_out, down_local, whole_dot(6, grad_out)))
    grad_gate = grad_act * upward * sigmoid_gate * (1.0 + gate * (1.0 - sigmoid_gate))
    grad_up = grad_act * gate * sigmoid_gate
    ffn_back = project_back(4, grad_gate, ffn_local, whole_dot(4, grad_gate)) + project_back(
        5, grad_up, ffn_local, whole_dot(5, grad_up)
    )
    grad_two = grad_out + rms_back(x_two, gather_inputs(ffn_back), norm_gains[1])
    grad_att = gather_inputs(project_back(3, grad_two, out_local, whole_dot(3, grad_two)))
    grad_att = grad_att.astype(jnp.bfloat16).reshape(group_rows, HEADS, HEAD_DIM)
    weights = jnp.exp(attention_scores(query_b, key_b) - log_total)
    weights_b = weights.astype(jnp.bfloat16)
    grad_weights = jnp.einsum("thd,shd->hts", grad_att, value_b, preferred_element_type=jnp.float32)
    grad_value = jnp.einsum("hts,thd->shd", weights_b, grad_att, preferred_element_type=jnp.float32)
    centred = jnp.sum(weights * grad_weights, axis=-1, keepdims=True)
    grad_scores = (weights * (grad_weights - centred)).astype(jnp.bfloat16)
    grad_query = (
        jnp.einsum("hts,shd->thd", grad_scores, key_b, preferred_element_type=jnp.float32)
        * score_scale
    )
    grad_key = (
        jnp.einsum("hts,thd->shd", grad_scores, query_b, preferred_element_type=jnp.float32)
        * score_scale
    )
    grad_query, grad_key, grad_value = (
        unrotate(grad_query, cosine, sine),
        unrotate(grad_key, cosine, sine),
        grad_value,
    )
    incoming = [
        grad_query.reshape(group_rows, D),
        grad_key.reshape(group_rows, D),
        grad_value.reshape(group_rows, D),
    ]
    group_dots = [whole_dot(index, incoming[index]) for index in range(3)]
    first_back = project_back(0, incoming[0], first_local, group_dots[0])
    first_back = first_back + project_back(1, incoming[1], first_local, group_dots[1])
    first_back = first_back + project_back(2, incoming[2], first_local, group_dots[2])
    input_grad = grad_two + rms_back(xf, gather_inputs(first_back), norm_gains[0])
    pieces = []
    for index in range(7):
        rows_total = proj_dims()[index][0]
        grad_lower = grads[index][0]
        placed = lax.dynamic_update_slice_in_dim(
            jnp.zeros((rows_total, RANK), jnp.float32),
            grad_lower,
            model_index * grad_lower.shape[0],
            0,
        )
        pieces.append(placed.reshape(-1))
    for index in range(7):
        pieces.append(grads[index][1].reshape(-1))
    for index in range(7):
        pieces.append(grads[index][2])
    blocks = jnp.concatenate(pieces).reshape(-1, BLOCK)
    buffer = jnp.zeros((capacity * everyone, BLOCK), jnp.float32).at[slot_index].set(blocks)
    owned = lax.psum_scatter(buffer, ("dp", "mp"), scatter_dimension=0, tiled=True)
    slot_block = (
        jnp.full((capacity * everyone,), -1, jnp.int32)
        .at[slot_index]
        .set(jnp.arange(blocks.shape[0], dtype=jnp.int32))
    )
    local_blocks = lax.dynamic_slice_in_dim(
        slot_block, lax.axis_index(("dp", "mp")) * capacity, capacity, 0
    )
    new_master, new_first, new_second = adam_update(
        master, owned, first_moment, second_moment, block_rates(local_blocks)
    )
    return (layer_out, input_grad, new_master, new_first, new_second)


def swap_halves(values):
    half = values.shape[-1] // 2
    return jnp.concatenate([values[..., half:], values[..., :half]], axis=-1)


def dot_t(left, right, **kwargs):
    return lax.dot_general(
        left, right, (((1,), (1,)), ((), ())), preferred_element_type=jnp.float32, **kwargs
    )


def dot_first(left, right, **kwargs):
    return lax.dot_general(
        left, right, (((0,), (0,)), ((), ())), preferred_element_type=jnp.float32, **kwargs
    )


def dot(left, right, **kwargs):
    return jnp.dot(left, right, preferred_element_type=jnp.float32, **kwargs)


def wide(left, right):
    return dot(left.astype(jnp.float32), right.astype(jnp.float32), precision=highest)


def wide_t(left, right):
    return dot_t(left.astype(jnp.float32), right.astype(jnp.float32), precision=highest)


def wide_first(left, right):
    return dot_first(left.astype(jnp.float32), right.astype(jnp.float32), precision=highest)


def block_order():
    rows = lax.broadcasted_iota(jnp.int32, (BLOCK, BLOCK), 0)
    cols = lax.broadcasted_iota(jnp.int32, (BLOCK, BLOCK), 1)
    return (cols == (rows % RANK) * (BLOCK // RANK) + rows // RANK).astype(jnp.bfloat16)


def fast_body(
    tokens,
    cotangent,
    norm_gains,
    w_attn,
    w_in,
    w_down,
    segments,
    owners,
    master,
    first_moment,
    second_moment,
):
    group_rows = tokens.shape[0]
    n_mp = lax.axis_size("mp")
    n_dp = lax.axis_size("dp")
    n_z = n_mp // 2
    mi = lax.axis_index("mp")
    di = lax.axis_index("dp")
    core = mi % 2
    zi = mi // 2
    share = group_rows // n_mp
    capacity = master.shape[0]
    n_blocks = owners.shape[0]
    n_heads = HEADS // n_mp
    width_a = D // n_mp
    width_f = FF // n_mp
    score_scale = HEAD_DIM ** (-0.5)
    f32 = jnp.float32
    bf16 = jnp.bfloat16

    def mp_swap(values, step):
        return lax.ppermute(values, "mp", [(i, i ^ step) for i in range(n_mp)])

    def dp_swap(values, step):
        return lax.ppermute(values, "dp", [(i, i ^ step) for i in range(n_dp)])

    def plane(values):
        half = values.shape[0] // 2
        a, b = values[:half], values[half:]
        ax, by = dp_swap(a, 1), dp_swap(b, 2)
        ay, bx = dp_swap(a, 2), dp_swap(b, 1)
        axy, bxy = dp_swap(ax, 2), dp_swap(by, 1)
        return jnp.stack([jnp.stack([a, ax, ay, axy]), jnp.stack([b, bx, by, bxy])], axis=1)

    def scatter_rows(values):
        rows = values.shape[0] // n_mp
        split = values.reshape(n_z, 2, rows, values.shape[1])
        keep = lax.dynamic_index_in_dim(split, core, 1, keepdims=False)
        send = lax.dynamic_index_in_dim(split, 1 - core, 1, keepdims=False).astype(bf16)
        pair = (keep.astype(f32) + mp_swap(send, 1).astype(f32)).astype(bf16)
        total = lax.dynamic_index_in_dim(pair, zi, 0, keepdims=False).astype(f32)
        for step in range(1, n_z):
            piece = lax.dynamic_index_in_dim(pair, zi ^ step, 0, keepdims=False)
            total = total + mp_swap(piece, 2 * step).astype(f32)
        return total

    def gather_rows(values):
        return lax.all_gather(values, "mp", axis=0, tiled=True)

    ranks = slot_positions(owners, 0)
    own_slots = owners * capacity + ranks
    me = di * n_mp + mi
    hits = own_slots[None, :] == me * capacity + jnp.arange(capacity)[:, None]
    mine = jnp.sum(jnp.where(hits, jnp.arange(n_blocks)[None, :] + 1, 0), axis=1) - 1
    count_flat = RANK * (11 * D + 3 * FF) // BLOCK
    in_order = mine >= count_flat
    order_matrix = block_order()
    master_b = master.astype(bf16)
    ordered = dot(master_b, order_matrix).astype(bf16)
    to_send = jnp.where(in_order[:, None], master_b, ordered)

    line = jnp.stack([to_send] + [mp_swap(to_send, 2 * step) for step in range(1, n_z)])
    sheet = plane(line)
    adapters = jnp.stack([sheet, mp_swap(sheet, 1)])
    adapters = adapters.reshape(-1, 8, 128)
    owner_d, owner_m = owners // n_mp, owners % n_mp
    place = (((owner_m % 2) ^ core) * n_dp + (owner_d ^ di)) * n_z + ((owner_m // 2) ^ zi)
    place = place * capacity + ranks

    def reshard_line(weights, width):
        count, rows = weights.shape[0], weights.shape[1]
        quarter = rows // n_dp
        part = lax.dynamic_slice_in_dim(weights, di * quarter, quarter, 1)
        part = part.reshape(count, quarter, n_mp, width).transpose(2, 0, 1, 3)
        pieces = []
        for step in range(n_mp):
            piece = lax.dynamic_index_in_dim(part, mi ^ step, 0, keepdims=False)
            pieces.append(mp_swap(piece, step) if step else piece)
        return pieces

    def reshard_plane(pieces):
        block = jnp.take(jnp.stack(pieces), mi ^ jnp.arange(n_mp), axis=0)
        whole = plane(block)
        whole = jnp.take(whole, di ^ jnp.arange(n_dp), axis=0)
        count, quarter, width = block.shape[1:]
        whole = whole.reshape(n_dp, n_mp, count, quarter, width).transpose(2, 1, 0, 3, 4)
        whole = whole.reshape(count, n_mp * n_dp * quarter, width)
        return [whole[index] for index in range(count)]

    line_a = reshard_line(w_attn[:3], width_a)
    line_a, w_in_late = lax.optimization_barrier((line_a, w_in))
    columns_a = reshard_plane(line_a)
    line_f = reshard_line(w_in_late, width_f)
    columns_a, line_f = lax.optimization_barrier((columns_a, line_f))
    columns_f = reshard_plane(line_f)
    columns = {0: columns_a[0], 1: columns_a[1], 2: columns_a[2], 4: columns_f[0], 5: columns_f[1]}
    rows_w = {3: w_attn[3], 6: w_down}

    starts = []
    total_blocks = 0
    for inner, outer in proj_dims():
        starts.append(total_blocks)
        total_blocks += inner * RANK // BLOCK
    upper_starts = []
    for inner, outer in proj_dims():
        upper_starts.append(total_blocks)
        total_blocks += outer * RANK // BLOCK
    wanted = []
    spans = {}

    def want(name, base, count):
        even = (count + 1) // 2 * 2
        spans[name] = (sum(w.shape[0] for w in wanted) * 64, count * 64)
        steps = jnp.minimum(jnp.arange(even), count - 1)
        wanted.append(base + steps)

    per_a, per_f = width_a * RANK // BLOCK, width_f * RANK // BLOCK
    for index in (0, 1, 2, 4, 5):
        per = per_a if index < 3 else per_f
        want(("A", index), starts[index], D * RANK // BLOCK)
        want(("B", index), upper_starts[index] + mi * per, per)
    for index in (3, 6):
        per = per_a if index == 3 else per_f
        want(("A", index), starts[index] + mi * per, per)
        want(("B", index), upper_starts[index], D * RANK // BLOCK)
    chosen = jnp.take(place, jnp.concatenate(wanted))
    pairs = jnp.take(adapters, chosen, axis=0).reshape(-1, 2, 8, 128)
    even, odd = pairs[:, 0], pairs[:, 1]
    tiles = jnp.concatenate(
        [
            jnp.concatenate([even[..., :64], odd[..., :64]], axis=-1),
            jnp.concatenate([even[..., 64:], odd[..., 64:]], axis=-1),
        ],
        axis=1,
    )
    flat = tiles.transpose(1, 0, 2).reshape(RANK, -1)

    def adapter(kind, index):
        start, size = spans[(kind, index)]
        return flat[:, start : start + size]

    lower = {index: adapter("A", index) for index in range(7)}
    upper = {index: adapter("B", index) for index in range(7)}
    magnitude_rows = jnp.take(adapters, place[count_flat:], axis=0).reshape(-1).astype(f32)
    magnitudes = {}
    offset = 0
    for index, (inner, outer) in enumerate(proj_dims()):
        values = magnitude_rows[offset : offset + outer]
        if index in columns:
            width = outer // n_mp
            values = lax.dynamic_slice_in_dim(values, mi * width, width, 0)
        magnitudes[index] = values
        offset += outer

    def squares(weights, index):
        joined = weights.astype(f32) + dora_scale * dot_first(lower[index], upper[index])
        return jnp.sum(joined * joined, axis=0)

    norms, scales = {}, {}
    for index in (0, 1, 2, 4, 5):
        norms[index] = jnp.sqrt(squares(columns[index], index) + column_eps)
    both = lax.psum(jnp.stack([squares(rows_w[3], 3), squares(rows_w[6], 6)]), "mp")
    norms[3] = jnp.sqrt(both[0] + column_eps)
    norms[6] = jnp.sqrt(both[1] + column_eps)
    for index in range(7):
        scales[index] = magnitudes[index] / norms[index]

    def low_rank(inputs, index):
        return dot_t(inputs, lower[index])

    def project(inputs, weights, index):
        low = low_rank(inputs, index)
        return dot(inputs, weights) + dora_scale * wide(low, upper[index]), low

    row = segments[0]
    positions = segment_positions(row)
    cosine, sine = rotary_tables(positions)
    cosine, sine = cosine[:, 0], sine[:, 0]
    cos_full = jnp.concatenate([cosine, cosine], axis=-1)[:, None, :]
    sin_full = jnp.concatenate([-sine, sine], axis=-1)[:, None, :]
    order = jnp.arange(group_rows)
    allowed = (row[:, None] == row[None, :]) & (order[None, :] <= order[:, None])

    xf = tokens.astype(f32)
    features = rms_norm(xf, norm_gains[0]).astype(bf16)
    mixed, lows, heads = {}, {}, {}
    for index in range(3):
        mixed[index], lows[index] = project(features, columns[index], index)
        value = (mixed[index] * scales[index]).reshape(group_rows, n_heads, HEAD_DIM)
        if index < 2:
            value = value * cos_full + swap_halves(value) * sin_full
        heads[index] = value.astype(bf16)
    query, keys, value = heads[0], heads[1], heads[2]
    scores = jnp.einsum("thd,shd->hts", query, keys, preferred_element_type=f32) * score_scale
    scores = jnp.where(allowed[None], scores, -1e30)
    top = jnp.max(scores, axis=-1, keepdims=True)
    expd = jnp.exp(scores - top)
    weights = expd / jnp.sum(expd, axis=-1, keepdims=True)
    weights_b = weights.astype(bf16)
    attended = jnp.einsum("hts,shd->thd", weights_b, value, preferred_element_type=f32)
    attended = attended.reshape(group_rows, width_a).astype(bf16)

    def rows_here(values):
        return lax.dynamic_slice_in_dim(values, mi * share, share, 0)

    partial, lows[3] = project(attended, rows_w[3], 3)
    mixed[3] = scatter_rows(partial)
    x_two = rows_here(tokens).astype(f32) + mixed[3] * scales[3]
    features_two = gather_rows(rms_norm(x_two, norm_gains[1]).astype(bf16))
    for index in (4, 5):
        mixed[index], lows[index] = project(features_two, columns[index], index)
    gate = mixed[4] * scales[4]
    upward = mixed[5] * scales[5]
    sigmoid_gate = jax.nn.sigmoid(gate)
    act = (gate * sigmoid_gate * upward).astype(bf16)
    partial, lows[6] = project(act, rows_w[6], 6)
    mixed[6] = scatter_rows(partial)
    layer_out = gather_rows((x_two + mixed[6] * scales[6]).astype(bf16))

    def send_back(grad, index):
        grad_b = (grad * scales[index]).astype(bf16)
        through = dora_scale * dot_t(grad_b, upper[index])
        return grad_b, through

    def to_inputs(grad_b, through, weights, index):
        return dot_t(grad_b, weights) + wide(through, lower[index])

    def dots_of(grad, index):
        return jnp.sum(grad * mixed[index], axis=0)

    grad_out = cotangent.astype(f32)
    grads_b, throughs, dots = {}, {}, {}
    grads_b[6], throughs[6] = send_back(grad_out, 6)
    grad_act = to_inputs(grads_b[6], throughs[6], rows_w[6], 6)
    grad_gate = grad_act * upward * sigmoid_gate * (1.0 + gate * (1.0 - sigmoid_gate))
    grad_up = grad_act * gate * sigmoid_gate
    back = 0.0
    for index, grad in ((4, grad_gate), (5, grad_up)):
        dots[index] = dots_of(grad, index)
        grads_b[index], throughs[index] = send_back(grad, index)
        back = back + to_inputs(grads_b[index], throughs[index], columns[index], index)
    out_here = rows_here(cotangent).astype(f32)
    grad_two = out_here + rms_back(x_two, scatter_rows(back), norm_gains[1])
    grads_b[3] = gather_rows((grad_two * scales[3]).astype(bf16))
    throughs[3] = dora_scale * dot_t(grads_b[3], upper[3])
    grad_att = to_inputs(grads_b[3], throughs[3], rows_w[3], 3).astype(bf16)
    grad_att = grad_att.reshape(group_rows, n_heads, HEAD_DIM)
    grad_weights = jnp.einsum("thd,shd->hts", grad_att, value, preferred_element_type=f32)
    grad_value = jnp.einsum("hts,thd->shd", weights_b, grad_att, preferred_element_type=f32)
    centred = jnp.sum(weights * grad_weights, axis=-1, keepdims=True)
    grad_scores = (weights * (grad_weights - centred)).astype(bf16)
    grad_query = jnp.einsum("hts,shd->thd", grad_scores, keys, preferred_element_type=f32)
    grad_key = jnp.einsum("hts,thd->shd", grad_scores, query, preferred_element_type=f32)
    incoming = []
    for grad in (grad_query, grad_key):
        grad = grad * score_scale
        incoming.append((grad * cos_full - swap_halves(grad) * sin_full).reshape(group_rows, width_a))
    incoming.append(grad_value.reshape(group_rows, width_a))
    back = 0.0
    for index, grad in enumerate(incoming):
        dots[index] = dots_of(grad, index)
        grads_b[index], throughs[index] = send_back(grad, index)
        back = back + to_inputs(grads_b[index], throughs[index], columns[index], index)
    grad_in = grad_two + rms_back(rows_here(tokens).astype(f32), scatter_rows(back), norm_gains[0])
    input_grad = gather_rows(grad_in.astype(bf16)).astype(f32)

    here = jnp.stack([dots_of(grad_two, 3), dots_of(out_here, 6)])
    both = lax.psum(here, "mp")
    dots[3], dots[6] = both[0], both[1]
    inputs = {0: features, 1: features, 2: features, 3: attended, 4: features_two, 5: features_two, 6: act}
    grad_lower, grad_upper = {}, {}
    for index in range(7):
        weights_p = columns[index] if index in columns else rows_w[index]
        norm = norms[index]
        ratio = -dots[index] * magnitudes[index] / (norm * norm * norm)
        upper_f = upper[index].astype(f32)
        scaled = dora_scale * upper_f * ratio[None, :]
        grad_lower[index] = (
            wide_first(throughs[index], inputs[index])
            + wide_t(scaled, weights_p)
            + wide(dora_scale * wide_t(scaled, upper_f), lower[index])
        )
        crossed = dot(lower[index], weights_p) + dora_scale * wide(
            dot_t(lower[index], lower[index]), upper[index]
        )
        grad_upper[index] = dora_scale * (
            wide_first(lows[index], grads_b[index]) + crossed * ratio[None, :]
        )
    grad_magnitude = []
    for index, (inner, outer) in enumerate(proj_dims()):
        if index in columns:
            width = outer // n_mp
            full = jnp.zeros((outer,), f32)
            full = lax.dynamic_update_slice_in_dim(full, dots[index] / norms[index], mi * width, 0)
        else:
            full = here[0 if index == 3 else 1] / norms[index]
        grad_magnitude.append(full)

    def to_blocks(values):
        extra = -values.shape[1] % 128
        if extra:
            values = jnp.pad(values, ((0, 0), (0, extra)))
        parts = values.reshape(2, 8, -1, 128).transpose(2, 0, 1, 3)
        low, high = parts[:, 0], parts[:, 1]
        even = jnp.concatenate([low[..., :64], high[..., :64]], axis=-1)
        odd = jnp.concatenate([low[..., 64:], high[..., 64:]], axis=-1)
        return jnp.stack([even, odd], axis=1).reshape(-1, BLOCK)

    shared = []
    where = {}
    shared_rows = 0

    def add_shared(name, blocks):
        nonlocal shared_rows
        where[name] = ("shared", shared_rows)
        shared.append(blocks)
        shared_rows += blocks.shape[0]

    for index in (0, 1, 2, 4, 5):
        add_shared(("A", index), to_blocks(grad_lower[index]))
    for index in (3, 6):
        add_shared(("B", index), to_blocks(grad_upper[index]))
    add_shared("m", jnp.concatenate(grad_magnitude).reshape(-1, BLOCK))
    unit = -(-shared_rows // n_mp)
    shared.append(jnp.zeros((unit * n_mp - shared_rows, BLOCK), f32))
    summed = scatter_rows(jnp.concatenate(shared))
    local = [summed]
    local_rows = unit

    for index in (3, 6):
        blocks = to_blocks(grad_lower[index])
        where[("A", index)] = ("local", local_rows)
        local.append(blocks)
        local_rows += blocks.shape[0]
    for index in (0, 1, 2, 4, 5):
        blocks = to_blocks(grad_upper[index])
        where[("B", index)] = ("local", local_rows)
        local.append(blocks)
        local_rows += blocks.shape[0]
    part = -(-local_rows // n_dp)
    local.append(jnp.zeros((part * n_dp - local_rows, BLOCK), f32))
    local = jnp.concatenate(local).reshape(n_dp, part, BLOCK).astype(bf16)
    total = lax.dynamic_index_in_dim(local, di, 0, keepdims=False).astype(f32)
    for step in range(1, n_dp):
        piece = lax.dynamic_index_in_dim(local, di ^ step, 0, keepdims=False)
        total = total + dp_swap(piece, step).astype(f32)
    reduced = lax.all_gather(total.astype(bf16), ("dp", "mp"), axis=0, tiled=True)

    table = np.zeros((n_blocks,), np.int32)

    def set_row(block, m, local_row):
        table[block] = ((local_row // part) * n_mp + m) * part + local_row % part

    for index, (inner, outer) in enumerate(proj_dims()):
        for kind, base, size in (("A", starts[index], inner), ("B", upper_starts[index], outer)):
            count = size * RANK // BLOCK
            space, begin = where[(kind, index)]
            for k in range(count):
                if space == "shared":
                    set_row(base + k, (begin + k) // unit, (begin + k) % unit)
                else:
                    per = count // n_mp
                    set_row(base + k, k // per, begin + k % per)
    begin = where["m"][1]
    for k in range(n_blocks - count_flat):
        set_row(count_flat + k, (begin + k) // unit, (begin + k) % unit)
    picked = jnp.take(reduced, jnp.take(jnp.asarray(table), jnp.maximum(mine, 0)), axis=0)
    unordered = dot_t(picked, order_matrix)
    grad = jnp.where(in_order[:, None], picked.astype(f32), unordered)
    grad = jnp.where((mine >= 0)[:, None], grad, 0.0)
    new_master, new_first, new_second = adam_update(
        master, grad, first_moment, second_moment, block_rates(mine)
    )
    return (layer_out, input_grad, new_master, new_first, new_second)


def solution(mesh):
    fast = mesh.shape["dp"] == 4 and mesh.shape["mp"] == 8
    return jax.shard_map(
        fast_body if fast else body,
        mesh=mesh,
        in_specs=(
            P("dp", None),
            P("dp", None),
            P(),
            P(None, "mp", None),
            P(None, "mp", None),
            P("mp", None),
            P("dp", None),
            P(),
            P(("dp", "mp"), None),
            P(("dp", "mp"), None),
            P(("dp", "mp"), None),
        ),
        out_specs=(
            P("dp", None),
            P("dp", None),
            P(("dp", "mp"), None),
            P(("dp", "mp"), None),
            P(("dp", "mp"), None),
        ),
        check_vma=False,
    )
```

```python
import functools

import jax
import jax.numpy as jnp
import numpy as np
from jax import lax
from jax.experimental import pallas as pl
from jax.experimental.pallas import tpu as pltpu
from jax.sharding import PartitionSpec as P

D = 2048
FF = 5632
HEADS = 16
HEAD_DIM = 128
RANK = 16
BLOCK = 1024
STEP = 5


dora_scale = 2.0
rope_base = 10000.0
norm_eps = 1e-05
column_eps = 1e-06
beta_one = 0.5
beta_two = 0.5
adam_eps = 1e-08
weight_decay = 0.01
rate_lower = 0.02
rate_upper = 0.1
rate_magnitude = 1.0
highest = lax.Precision.HIGHEST


def proj_dims():
    return [(D, D), (D, D), (D, D), (D, D), (D, FF), (D, FF), (FF, D)]


def unpack(flat):
    offset = 0
    lowers = []
    for inner, outer in proj_dims():
        lowers.append(flat[offset : offset + inner * RANK].reshape(inner, RANK))
        offset += inner * RANK
    uppers = []
    for inner, outer in proj_dims():
        uppers.append(flat[offset : offset + outer * RANK].reshape(outer, RANK))
        offset += outer * RANK
    magnitudes = []
    for inner, outer in proj_dims():
        magnitudes.append(flat[offset : offset + outer])
        offset += outer
    return (lowers, uppers, magnitudes)


def slot_positions(owners, capacity):
    order = jnp.arange(owners.shape[0], dtype=jnp.int32)
    same = (owners[:, None] == owners[None, :]) & (order[None, :] < order[:, None])
    ranks = jnp.sum(same.astype(jnp.int32), axis=1)
    return owners * capacity + ranks


def block_rates(block_ids):
    count_lower = RANK * (6 * D + FF) // BLOCK
    count_upper = RANK * (5 * D + 2 * FF) // BLOCK
    rates = jnp.where(block_ids < count_lower + count_upper, rate_upper, rate_magnitude)
    rates = jnp.where(block_ids < count_lower, rate_lower, rates)
    return jnp.where(block_ids < 0, 0.0, rates).astype(jnp.float32)


def adam_update(weight, grad, first, second, rates):
    first_new = beta_one * first + (1.0 - beta_one) * grad
    second_new = beta_two * second + (1.0 - beta_two) * grad * grad
    first_hat = first_new / (1.0 - beta_one**STEP)
    second_hat = second_new / (1.0 - beta_two**STEP)
    weight_new = weight - rates[:, None] * (
        first_hat / (jnp.sqrt(second_hat) + adam_eps) + weight_decay * weight
    )
    return (weight_new, first_new, second_new)


def rms_norm(values, gain):
    return values * lax.rsqrt(jnp.mean(values * values, axis=-1, keepdims=True) + norm_eps) * gain


def rms_back(values, grad, gain):
    inverse = lax.rsqrt(jnp.mean(values * values, axis=-1, keepdims=True) + norm_eps)
    scaled = grad * gain
    return inverse * (
        scaled - values * inverse * inverse * jnp.mean(scaled * values, axis=-1, keepdims=True)
    )


def segment_positions(row):
    order = jnp.arange(row.shape[0], dtype=jnp.int32)
    change = jnp.concatenate([jnp.ones((1,), dtype=bool), row[1:] != row[:-1]])
    starts = lax.cummax(jnp.where(change, order, 0), axis=0)
    return order - starts


def rotary_tables(positions):
    half = HEAD_DIM // 2
    freqs = rope_base ** (-(jnp.arange(half).astype(jnp.float32) * 2.0 / HEAD_DIM))
    angles = positions.astype(jnp.float32)[:, None] * freqs[None, :]
    return (jnp.cos(angles)[:, None, :], jnp.sin(angles)[:, None, :])


def rotate(values, cosine, sine):
    half = values.shape[-1] // 2
    first_half = values[..., :half]
    second_half = values[..., half:]
    return jnp.concatenate(
        [first_half * cosine - second_half * sine, second_half * cosine + first_half * sine],
        axis=-1,
    )


def unrotate(values, cosine, sine):
    half = values.shape[-1] // 2
    first_half = values[..., :half]
    second_half = values[..., half:]
    return jnp.concatenate(
        [first_half * cosine + second_half * sine, second_half * cosine - first_half * sine],
        axis=-1,
    )


def body(
    tokens,
    cotangent,
    norm_gains,
    w_attn,
    w_in,
    w_down,
    segments,
    owners,
    master,
    first_moment,
    second_moment,
):
    group_rows = tokens.shape[0]
    model_size = lax.axis_size("mp")
    model_index = lax.axis_index("mp")
    share = group_rows // model_size
    share_start = model_index * share
    capacity = master.shape[0]
    everyone = lax.axis_size(("dp", "mp"))
    score_scale = HEAD_DIM ** (-0.5)
    widths = [outer for inner, outer in proj_dims()]
    slot_index = slot_positions(owners, capacity)
    copies = lax.all_gather(master.astype(jnp.bfloat16), ("dp", "mp"), axis=0, tiled=True)
    lowers, uppers, magnitudes = unpack(jnp.take(copies, slot_index, axis=0).reshape(-1))
    frozen = [w_attn[0], w_attn[1], w_attn[2], w_attn[3], w_in[0], w_in[1], w_down]
    lower_local = []
    combined = []
    square_parts = []
    for index in range(7):
        rows_here = frozen[index].shape[0]
        piece = lax.dynamic_slice_in_dim(lowers[index], model_index * rows_here, rows_here, 0)
        lower_local.append(piece)
        joined = frozen[index].astype(jnp.float32) + dora_scale * jnp.dot(
            piece.astype(jnp.float32), uppers[index].astype(jnp.float32).T, precision=highest
        )
        combined.append(joined)
        square_parts.append(jnp.sum(joined * joined, axis=0))

    def rows_of(values):
        return lax.dynamic_slice_in_dim(values, share_start, share, 0)

    def split_parts(values, indices, axis):
        pieces = []
        offset = 0
        for index in indices:
            pieces.append(lax.slice_in_dim(values, offset, offset + widths[index], axis=axis))
            offset += widths[index]
        return pieces

    norms = [None] * 7
    mixed_share = [None] * 7
    low_share = [None] * 7
    mixed_full = [None] * 7
    grads = [None] * 7

    def set_scales(indices):
        summed = lax.psum(jnp.concatenate([square_parts[index] for index in indices]), "mp")
        squares = split_parts(summed, indices, 0)
        for index, value in zip(indices, squares):
            norms[index] = jnp.sqrt(value + column_eps)

    def scale(index):
        return magnitudes[index].astype(jnp.float32) / norms[index]

    def local_partials(inputs_local, indices):
        mixed_list = []
        low_list = []
        for index in indices:
            low_part = jnp.dot(inputs_local, lower_local[index], preferred_element_type=jnp.float32)
            mixed = jnp.dot(
                inputs_local, frozen[index], preferred_element_type=jnp.float32
            ) + dora_scale * jnp.dot(
                low_part, uppers[index].astype(jnp.float32).T, precision=highest
            )
            mixed_list.append(mixed)
            low_list.append(low_part)
        return (
            inputs_local,
            jnp.concatenate(mixed_list, axis=1),
            jnp.concatenate(low_list, axis=1),
        )

    def group_partials(inputs_b, indices):
        rows_here = frozen[indices[0]].shape[0]
        inputs_local = lax.dynamic_slice_in_dim(inputs_b, model_index * rows_here, rows_here, 1)
        return local_partials(inputs_local, indices)

    def finish(indices, local_mixed, local_low):
        summed_mixed, summed_low = lax.psum((local_mixed, local_low), "mp")
        pieces = split_parts(summed_mixed, indices, 1)
        for position, index in enumerate(indices):
            mixed_full[index] = pieces[position]
            mixed_share[index] = rows_of(pieces[position])
            low_share[index] = rows_of(summed_low[:, position * RANK : (position + 1) * RANK])
        return pieces

    def gather_inputs(local):
        return lax.all_gather(local, "mp", axis=1, tiled=True)

    xf = tokens.astype(jnp.float32)
    row = segments[0]
    cosine, sine = rotary_tables(segment_positions(row))
    order = jnp.arange(group_rows)
    allowed = (row[:, None] == row[None, :]) & (order[None, :] <= order[:, None])
    features = rms_norm(xf, norm_gains[0]).astype(jnp.bfloat16)
    first_local, first_mixed, first_low = group_partials(features, (0, 1, 2))
    set_scales((0, 1, 2))
    summed_mixed, summed_low = lax.psum((first_mixed, first_low), "mp")
    pieces = split_parts(summed_mixed, (0, 1, 2), 1)
    heads_in = []
    for index in range(3):
        mixed_full[index] = pieces[index]
        mixed_share[index] = rows_of(pieces[index])
        low_share[index] = rows_of(summed_low[:, index * RANK : (index + 1) * RANK])
        projected = (pieces[index] * scale(index)).reshape(group_rows, HEADS, HEAD_DIM)
        if index < 2:
            projected = rotate(projected, cosine, sine)
        heads_in.append(projected.astype(jnp.bfloat16))
    query_b, key_b, value_b = heads_in

    def attention_scores(query_h, key_h):
        scores = (
            jnp.einsum("thd,shd->hts", query_h, key_h, preferred_element_type=jnp.float32)
            * score_scale
        )
        return jnp.where(allowed[None], scores, -1e30)

    scores = attention_scores(query_b, key_b)
    top = jnp.max(scores, axis=-1, keepdims=True)
    expd = jnp.exp(scores - top)
    total = jnp.sum(expd, axis=-1, keepdims=True)
    probs = (expd / total).astype(jnp.bfloat16)
    attended_h = jnp.einsum("hts,shd->thd", probs, value_b, preferred_element_type=jnp.float32)
    attended_h, log_total = (attended_h, top + jnp.log(total))
    attended = attended_h.reshape(group_rows, D).astype(jnp.bfloat16)
    out_local, out_mixed, out_low = group_partials(attended, (3,))
    set_scales((3,))
    x_two = xf + finish((3,), out_mixed, out_low)[0] * scale(3)
    second_features = rms_norm(x_two, norm_gains[1]).astype(jnp.bfloat16)
    ffn_local, ffn_mixed, ffn_low = group_partials(second_features, (4, 5))
    set_scales((4, 5))
    gate_pre, up_pre = finish((4, 5), ffn_mixed, ffn_low)
    gate = gate_pre * scale(4)
    upward = up_pre * scale(5)
    sigmoid_gate = jax.nn.sigmoid(gate)
    act = (gate * sigmoid_gate * upward).astype(jnp.bfloat16)
    down_local, down_mixed, down_low = group_partials(act, (6,))
    set_scales((6,))
    down_pre = finish((6,), down_mixed, down_low)[0]
    layer_out = (x_two + down_pre * scale(6)).astype(jnp.bfloat16)

    def whole_dot(index, grad):
        return jnp.sum(grad * mixed_full[index], axis=0)

    def project_back(index, grad, inputs_local, group_dot):
        norm = norms[index]
        magnitude = magnitudes[index].astype(jnp.float32)
        grad_b = (grad * (magnitude / norm)).astype(jnp.bfloat16)
        share_dot = jnp.sum(rows_of(grad) * mixed_share[index], axis=0)
        grad_full = combined[index] * (-group_dot * magnitude / (norm * norm * norm))[None, :]
        upper_f = uppers[index].astype(jnp.float32)
        lower_f = lower_local[index].astype(jnp.float32)
        through = dora_scale * jnp.dot(grad_b, uppers[index], preferred_element_type=jnp.float32)
        grad_lower = jnp.dot(
            inputs_local.astype(jnp.float32).T, through, precision=highest
        ) + dora_scale * jnp.dot(grad_full, upper_f, precision=highest)
        grad_upper = dora_scale * jnp.dot(
            rows_of(grad_b).astype(jnp.float32).T, low_share[index], precision=highest
        ) + dora_scale * jnp.dot(grad_full.T, lower_f, precision=highest)
        grads[index] = (grad_lower, grad_upper, share_dot / norm)
        return jnp.dot(grad_b, frozen[index].T, preferred_element_type=jnp.float32) + jnp.dot(
            through, lower_f.T, precision=highest
        )

    grad_out = cotangent.astype(jnp.float32)
    grad_act = gather_inputs(project_back(6, grad_out, down_local, whole_dot(6, grad_out)))
    grad_gate = grad_act * upward * sigmoid_gate * (1.0 + gate * (1.0 - sigmoid_gate))
    grad_up = grad_act * gate * sigmoid_gate
    ffn_back = project_back(4, grad_gate, ffn_local, whole_dot(4, grad_gate)) + project_back(
        5, grad_up, ffn_local, whole_dot(5, grad_up)
    )
    grad_two = grad_out + rms_back(x_two, gather_inputs(ffn_back), norm_gains[1])
    grad_att = gather_inputs(project_back(3, grad_two, out_local, whole_dot(3, grad_two)))
    grad_att = grad_att.astype(jnp.bfloat16).reshape(group_rows, HEADS, HEAD_DIM)
    weights = jnp.exp(attention_scores(query_b, key_b) - log_total)
    weights_b = weights.astype(jnp.bfloat16)
    grad_weights = jnp.einsum("thd,shd->hts", grad_att, value_b, preferred_element_type=jnp.float32)
    grad_value = jnp.einsum("hts,thd->shd", weights_b, grad_att, preferred_element_type=jnp.float32)
    centred = jnp.sum(weights * grad_weights, axis=-1, keepdims=True)
    grad_scores = (weights * (grad_weights - centred)).astype(jnp.bfloat16)
    grad_query = (
        jnp.einsum("hts,shd->thd", grad_scores, key_b, preferred_element_type=jnp.float32)
        * score_scale
    )
    grad_key = (
        jnp.einsum("hts,thd->shd", grad_scores, query_b, preferred_element_type=jnp.float32)
        * score_scale
    )
    grad_query, grad_key, grad_value = (
        unrotate(grad_query, cosine, sine),
        unrotate(grad_key, cosine, sine),
        grad_value,
    )
    incoming = [
        grad_query.reshape(group_rows, D),
        grad_key.reshape(group_rows, D),
        grad_value.reshape(group_rows, D),
    ]
    group_dots = [whole_dot(index, incoming[index]) for index in range(3)]
    first_back = project_back(0, incoming[0], first_local, group_dots[0])
    first_back = first_back + project_back(1, incoming[1], first_local, group_dots[1])
    first_back = first_back + project_back(2, incoming[2], first_local, group_dots[2])
    input_grad = grad_two + rms_back(xf, gather_inputs(first_back), norm_gains[0])
    pieces = []
    for index in range(7):
        rows_total = proj_dims()[index][0]
        grad_lower = grads[index][0]
        placed = lax.dynamic_update_slice_in_dim(
            jnp.zeros((rows_total, RANK), jnp.float32),
            grad_lower,
            model_index * grad_lower.shape[0],
            0,
        )
        pieces.append(placed.reshape(-1))
    for index in range(7):
        pieces.append(grads[index][1].reshape(-1))
    for index in range(7):
        pieces.append(grads[index][2])
    blocks = jnp.concatenate(pieces).reshape(-1, BLOCK)
    buffer = jnp.zeros((capacity * everyone, BLOCK), jnp.float32).at[slot_index].set(blocks)
    owned = lax.psum_scatter(buffer, ("dp", "mp"), scatter_dimension=0, tiled=True)
    slot_block = (
        jnp.full((capacity * everyone,), -1, jnp.int32)
        .at[slot_index]
        .set(jnp.arange(blocks.shape[0], dtype=jnp.int32))
    )
    local_blocks = lax.dynamic_slice_in_dim(
        slot_block, lax.axis_index(("dp", "mp")) * capacity, capacity, 0
    )
    new_master, new_first, new_second = adam_update(
        master, owned, first_moment, second_moment, block_rates(local_blocks)
    )
    return (layer_out, input_grad, new_master, new_first, new_second)


f32 = jnp.float32
bf16 = jnp.bfloat16
VM = pl.BlockSpec(memory_space=pltpu.VMEM)
SM = pl.BlockSpec(memory_space=pltpu.SMEM)
ANY = pl.BlockSpec(memory_space=pl.ANY)
HBM = pl.BlockSpec(memory_space=pltpu.HBM)
TILE = 128
CHUNK = 256
N_DP = 4
N_MP = 8
N_Z = 4
WIDE = 768
FILL = 64


def mm(left, right):
    return lax.dot_general(left, right, (((1,), (0,)), ((), ())), preferred_element_type=f32)


def mm_t(left, right):
    return lax.dot_general(left, right, (((1,), (1,)), ((), ())), preferred_element_type=f32)


def mm_f(left, right):
    return lax.dot_general(left, right, (((0,), (0,)), ((), ())), preferred_element_type=f32)


def halves(value):
    high = value.astype(bf16)
    return high, (value - high.astype(f32)).astype(bf16)


def mm2(left, right):
    high, low = halves(left)
    return mm(high, right) + mm(low, right)


def mm2_t(left, right):
    high, low = halves(left)
    return mm_t(high, right) + mm_t(low, right)


def mm2_f(left, right):
    high, low = halves(left)
    return mm_f(high, right) + mm_f(low, right)


def swap64(value):
    return pltpu.roll(value, 64, 1)


def low_lanes(rows):
    return lax.broadcasted_iota(jnp.int32, (rows, TILE), 1) < 64


def merge(first, second):
    low = low_lanes(first.shape[0])
    return (
        jnp.where(low, first, swap64(second)),
        jnp.where(low, swap64(first), second),
    )


def tile(value, index):
    return value[:, index * TILE : (index + 1) * TILE]


def to_dp_order(value):
    out = [None] * 16
    for core in range(2):
        for pair in range(2):
            for part in range(2):
                first = 8 * pair + 2 * core + part
                low, high = merge(tile(value, first), tile(value, first + 4))
                out[8 * part + 2 * core + pair] = low
                out[8 * part + 4 + 2 * core + pair] = high
    return jnp.concatenate(out, axis=1)


def to_mp_order(value):
    out = [None] * 16
    for core in range(2):
        for pair in range(2):
            for part in range(2):
                first = 8 * part + 2 * core + pair
                low, high = merge(tile(value, first), tile(value, first + 4))
                out[8 * pair + 2 * core + part] = low
                out[8 * pair + 2 * core + part + 4] = high
    return jnp.concatenate(out, axis=1)


def shape_of(shape, dtype):
    return jax.ShapeDtypeStruct(shape, dtype)


def run(kernel, ins, specs, outs, scratch=(), name=None, after=(), megabytes=4, us=1.0):
    n_in, n_after = len(ins), len(after)

    def body(*refs):
        kernel(*refs[:n_in], *refs[n_in + n_after :])

    kinds = {"s": SM, "v": VM, "h": VM, "r": ANY}
    return pl.pallas_call(
        body,
        out_shape=list(outs),
        in_specs=[kinds[kind] for kind in specs] + [ANY] * n_after,
        out_specs=[VM] * len(outs),
        scratch_shapes=list(scratch),
        compiler_params=pltpu.CompilerParams(vmem_limit_bytes=megabytes * 2**20),
        cost_estimate=pl.CostEstimate(flops=int(us * 10**9), bytes_accessed=int(us * 10**6), transcendentals=0),
        name=name,
    )(*ins, *after)


def at(index, unit):
    return pl.ds(pl.multiple_of(index * unit, unit), unit)


def first_norm_kernel(tokens, gains, out):
    value = tokens[...].astype(f32)
    inverse = lax.rsqrt(jnp.mean(value * value, axis=-1, keepdims=True) + norm_eps)
    out[...] = to_dp_order(value * inverse * gains[0:1, :]).astype(bf16)


def line_kernel(step, where, p0, p1, p2, p3, out, forward):
    width = out.shape[2]
    for index, piece in enumerate((p0, p1, p2, p3)):
        rows = at(jnp.bitwise_xor(where[2], index), 64)
        for result, core in ((out, where[3]), (forward, 1 - where[3])):
            lanes = pl.ds(pl.multiple_of(core * step, TILE), width)
            result[:, rows, :] = piece[:, :, lanes]


def stack_kernel(first, second, out):
    out[0] = first[...]
    out[1] = second[...]


def join_all_kernel(*refs):
    begin = 0
    for piece in refs[:-1]:
        refs[-1][begin : begin + piece.shape[0]] = piece[...]
        begin += piece.shape[0]


def eight(a, ax, y2, b, by, x2):
    return [
        lambda p: a[p],
        lambda p: ax[p],
        lambda p: y2[0, p],
        lambda p: y2[1, p],
        lambda p: b[p],
        lambda p: by[p],
        lambda p: x2[0, p],
        lambda p: x2[1, p],
    ]


def order_matrix():
    rows = lax.broadcasted_iota(jnp.int32, (BLOCK, BLOCK), 0)
    cols = lax.broadcasted_iota(jnp.int32, (BLOCK, BLOCK), 1)
    target = jnp.bitwise_and(rows, RANK - 1) * (BLOCK // RANK) + jnp.right_shift(rows, 4)
    return jnp.where(cols == target, 1.0, 0.0).astype(bf16)


def pick(indices, pieces):
    total = None
    first = 0
    for piece in pieces:
        rows = piece.shape[0]
        lanes = lax.broadcasted_iota(jnp.int32, (indices.shape[0], rows), 1) + first
        part = mm(jnp.where(lanes == indices, 1.0, 0.0).astype(bf16), piece[...])
        total = part if total is None else total + part
        first += rows
    return total


def adapters_kernel(even_at, odd_at, flat_at, *rest):
    pieces, (out, out_m, tiles) = rest[:-3], rest[-3:]
    order = order_matrix()
    even = mm(pick(even_at[...], pieces).astype(bf16), order)
    odd = mm(pick(odd_at[...], pieces).astype(bf16), order)
    for part in range(8):
        low, high = merge(tile(even, part), tile(odd, part))
        tiles[:, part, :] = low
        tiles[:, 8 + part, :] = high
    for index in range(out.shape[1] // TILE):
        out[:, index * TILE : (index + 1) * TILE] = tiles[index].astype(bf16)
    flat = pick(flat_at[...], pieces)
    for index in range(out_m.shape[1] // BLOCK):
        out_m[0:1, index * BLOCK : (index + 1) * BLOCK] = flat[index : index + 1, :]


def column_norm(weights, lowers, uppers):
    joined = weights.astype(f32) + dora_scale * mm_f(lowers, uppers)
    return jnp.sum(joined * joined, axis=0, keepdims=True)


def split_rows(where, part, send, keep, share):
    core = where[3]
    for line in range(N_Z):
        send[line * share : (line + 1) * share] = part[at(2 * line + 1 - core, share)].astype(bf16)
    for line in range(N_Z):
        keep[line * share : (line + 1) * share] = part[at(2 * line + core, share)]


def attention_kernel(spans, where, x, b0, b1, b2, b3, b4, b5, w_out, flat, mags, cos, sin, seg_row, seg_col,
                     send, keep, mixed, qkv, probs, att, low_qkv, low_out, stats, part):
    blocks = eight(b0, b1, b2, b3, b4, b5)
    width = CHUNK
    rows = x.shape[0]
    la = [spans[("A", p)][0] for p in range(3)]
    lb = [spans[("B", p)][0] for p in range(3)]
    allowed = seg_col[...] == seg_row[...]
    t_index = lax.broadcasted_iota(jnp.int32, (rows, rows), 0)
    s_index = lax.broadcasted_iota(jnp.int32, (rows, rows), 1)
    allowed = jnp.logical_and(allowed, s_index <= t_index)
    for p in range(3):
        upper = flat[:, lb[p] : lb[p] + width]
        low = mm_t(x[...], flat[:, la[p] : la[p] + D])
        total = dora_scale * mm2(low, upper)
        square = jnp.zeros((1, width), f32)
        for index, block in enumerate(blocks):
            chunk = where[4 + index]
            weights = block(p)
            total += mm(x[:, at(chunk, CHUNK)], weights)
            lowers = flat[:, pl.ds(pl.multiple_of(la[p] + chunk * CHUNK, TILE), CHUNK)]
            square += column_norm(weights, lowers, upper)
        norm = jnp.sqrt(square + column_eps)
        magnitude = mags[:, pl.ds(pl.multiple_of(p * D + where[1] * width, TILE), width)]
        scale = magnitude / norm
        lanes = slice(p * width, (p + 1) * width)
        mixed[:, lanes] = total
        low_qkv[:, p * RANK : (p + 1) * RANK] = low
        stats[0:1, lanes] = scale
        stats[1:2, lanes] = norm
        stats[2:3, lanes] = magnitude
        value = total * scale
        for head in range(width // HEAD_DIM):
            one = value[:, head * HEAD_DIM : (head + 1) * HEAD_DIM]
            if p < 2:
                one = one * cos[...] + swap64(one) * sin[...]
            begin = p * width + head * HEAD_DIM
            qkv[:, begin : begin + HEAD_DIM] = one.astype(bf16)
    for head in range(width // HEAD_DIM):
        lanes = slice(head * HEAD_DIM, (head + 1) * HEAD_DIM)
        query = qkv[:, lanes]
        keys = qkv[:, width + head * HEAD_DIM : width + (head + 1) * HEAD_DIM]
        value = qkv[:, 2 * width + head * HEAD_DIM : 2 * width + (head + 1) * HEAD_DIM]
        scores = mm_t(query, keys) * HEAD_DIM ** (-0.5)
        scores = jnp.where(allowed, scores, -1e30)
        expd = jnp.exp(scores - jnp.max(scores, axis=-1, keepdims=True))
        weights = expd / jnp.sum(expd, axis=-1, keepdims=True)
        probs[head] = weights
        att[:, lanes] = mm(weights.astype(bf16), value).astype(bf16)
    a_out, b_out = spans[("A", 3)][0], spans[("B", 3)][0]
    low = mm_t(att[...], flat[:, a_out : a_out + width])
    low_out[...] = low
    part[...] = mm(att[...], w_out[...]) + dora_scale * mm2(low, flat[:, b_out : b_out + D])
    split_rows(where, part, send, keep, send.shape[0] // N_Z)


def pair_kernel(where, keep, received, p1, p2, p3, own):
    share = own.shape[0]

    def line(index):
        rows = at(index, share)
        return keep[rows] + received[rows].astype(f32)

    own[...] = line(where[2])
    for step, piece in ((1, p1), (2, p2), (3, p3)):
        piece[...] = line(jnp.bitwise_xor(where[2], step)).astype(bf16)


def total_of(own, r1, r2, r3):
    return own[...] + r1[...].astype(f32) + r2[...].astype(f32) + r3[...].astype(f32)


def second_norm_kernel(own, r1, r2, r3, tokens, gains, scale, x_two, mixed, out):
    total = total_of(own, r1, r2, r3)
    mixed[...] = total
    value = tokens[...].astype(f32) + total * scale[...]
    x_two[...] = value
    inverse = lax.rsqrt(jnp.mean(value * value, axis=-1, keepdims=True) + norm_eps)
    out[...] = to_dp_order(value * inverse * gains[1:2, :]).astype(bf16)


def join_rows(where, pieces, out):
    share = pieces[0].shape[0]
    for index, piece in enumerate(pieces):
        line = jnp.bitwise_xor(where[2], index % N_Z)
        core = where[3] if index < N_Z else 1 - where[3]
        out[at(2 * line + core, share)] = piece[...].astype(out.dtype)


def join_kernel(where, p0, p1, p2, p3, p4, p5, p6, p7, out):
    join_rows(where, (p0, p1, p2, p3, p4, p5, p6, p7), out)


def wide_squares(spans, where, blocks, chunks, flat):
    squares = []
    for p in range(2):
        a, b = spans[("A", 4 + p)][0], spans[("B", 4 + p)][0]
        square = jnp.zeros((1, WIDE), f32)
        for index, block in zip(chunks, blocks):
            begin = pl.multiple_of(a + where[4 + index] * CHUNK, TILE)
            square += column_norm(block(p), flat[:, pl.ds(begin, CHUNK)], flat[:, b : b + WIDE])
        squares.append(square)
    return jnp.concatenate(squares, axis=1)


def wide_first_kernel(spans, where, a, ax, b, by, flat, squares):
    blocks = eight(a, ax, None, b, by, None)
    squares[...] = wide_squares(spans, where, [blocks[k] for k in (0, 1, 4, 5)], (0, 1, 4, 5), flat)


def wide_norm_kernel(spans, where, y2, x2, flat, mags, squares, stats):
    blocks = eight(None, None, y2, None, None, x2)
    total = squares[...] + wide_squares(spans, where, [blocks[k] for k in (2, 3, 6, 7)], (2, 3, 6, 7), flat)
    for p in range(2):
        lanes = slice(p * WIDE, (p + 1) * WIDE)
        norm = jnp.sqrt(total[:, lanes] + column_eps)
        first = 4 * D + p * FF + where[2] * (2 * FF // N_MP) + where[3] * (WIDE - TILE)
        magnitude = mags[:, pl.ds(pl.multiple_of(first, TILE), WIDE)]
        stats[0:1, lanes] = magnitude / norm
        stats[1:2, lanes] = norm
        stats[2:3, lanes] = magnitude


def row_norm_kernel(spans, w_out, w_down, flat, squares):
    for row, (p, weights) in enumerate(((3, w_out[...]), (6, w_down[...]))):
        a, size = spans[("A", p)]
        b = spans[("B", p)][0]
        squares[row : row + 1, :] = column_norm(weights, flat[:, a : a + size], flat[:, b : b + D])


def down_back_kernel(spans, where, cotangent, scale, w_down, flat, d_act, grad_b, through, padded):
    a, size = spans[("A", 6)]
    b = spans[("B", 6)][0]
    grad = (cotangent[...].astype(f32) * scale[...]).astype(bf16)
    grad_b[...] = grad
    low = dora_scale * mm_t(grad, flat[:, b : b + D])
    through[...] = low
    padded[...] = jnp.zeros_like(padded)
    padded[:, 0:size] = mm_t(grad, w_down[...]) + mm2(low, flat[:, a : a + size])
    value = padded[...]
    d_act[...] = jnp.where(where[3] == 0, value, pltpu.roll(value, FILL, 1))


def middle_kernel(spans, where, p0, p1, p2, p3, p4, p5, p6, p7, b0, b1, b2, b3, b4, b5, d_act, flat, stats,
                  send, keep, x, act, grads, throughs, lows, dots, part, mixed):
    blocks = eight(b0, b1, b2, b3, b4, b5)
    join_rows(where, (p0, p1, p2, p3, p4, p5, p6, p7), x)
    for p in range(2):
        a, b = spans[("A", 4 + p)][0], spans[("B", 4 + p)][0]
        low = mm_t(x[...], flat[:, a : a + D])
        lows[:, p * RANK : (p + 1) * RANK] = low
        total = dora_scale * mm2(low, flat[:, b : b + WIDE])
        for index, block in enumerate(blocks):
            total += mm(x[:, at(where[4 + index], CHUNK)], block(p))
        mixed[:, p * WIDE : (p + 1) * WIDE] = total
    lanes = lax.broadcasted_iota(jnp.int32, d_act.shape, 1) - where[3] * FILL
    used = jnp.logical_and(lanes >= 0, lanes < WIDE - FILL)
    gate = mixed[:, :WIDE] * stats[0:1, :WIDE]
    upward = mixed[:, WIDE:] * stats[0:1, WIDE:]
    sigmoid_gate = jax.nn.sigmoid(gate)
    silu = gate * sigmoid_gate
    act[...] = jnp.where(used, silu * upward, 0.0).astype(bf16)
    back = jnp.where(used, d_act[...], 0.0)
    grad = back * upward * sigmoid_gate * (1.0 + gate * (1.0 - sigmoid_gate))
    dots[0:1, :WIDE] = jnp.sum(grad * mixed[:, :WIDE], axis=0, keepdims=True)
    grads[:, :WIDE] = (grad * stats[0:1, :WIDE]).astype(bf16)
    grad = back * silu
    dots[0:1, WIDE:] = jnp.sum(grad * mixed[:, WIDE:], axis=0, keepdims=True)
    grads[:, WIDE:] = (grad * stats[0:1, WIDE:]).astype(bf16)
    through = []
    for p in range(2):
        b = spans[("B", 4 + p)][0]
        low = dora_scale * mm_t(grads[:, p * WIDE : (p + 1) * WIDE], flat[:, b : b + WIDE])
        throughs[:, p * RANK : (p + 1) * RANK] = low
        through.append(halves(low))
    for index, block in enumerate(blocks):
        chunk = where[4 + index]
        total = None
        for p in range(2):
            a = spans[("A", 4 + p)][0]
            lowers = flat[:, pl.ds(pl.multiple_of(a + chunk * CHUNK, TILE), CHUNK)]
            one = mm_t(grads[:, p * WIDE : (p + 1) * WIDE], block(p))
            one += mm(through[p][0], lowers) + mm(through[p][1], lowers)
            total = one if total is None else total + one
        part[:, at(chunk, CHUNK)] = total
    split_rows(where, part, send, keep, send.shape[0] // N_Z)


def down_kernel(spans, where, act, w_down, flat, cotangent, send, keep, low_out, dots, part, local):
    a, size = spans[("A", 6)]
    b = spans[("B", 6)][0]
    value = act[...].astype(f32)
    value = jnp.where(where[3] == 0, value, pltpu.roll(value, WIDE - FILL, 1))
    local[...] = value.astype(bf16)
    inputs = local[:, 0:size]
    low = mm_t(inputs, flat[:, a : a + size])
    low_out[...] = low
    part[...] = mm(inputs, w_down[...]) + dora_scale * mm2(low, flat[:, b : b + D])
    split_rows(where, part, send, keep, send.shape[0] // N_Z)
    dots[...] = jnp.sum(cotangent[...].astype(f32) * part[...], axis=0, keepdims=True)


def out_kernel(own, r1, r2, r3, x_two, scale, out):
    out[...] = (x_two[...] + total_of(own, r1, r2, r3) * scale[...]).astype(bf16)


def norm_back(value, grad, gain):
    inverse = lax.rsqrt(jnp.mean(value * value, axis=-1, keepdims=True) + norm_eps)
    scaled = grad * gain
    inner = jnp.mean(scaled * value, axis=-1, keepdims=True)
    return inverse * (scaled - value * inverse * inverse * inner)


def second_back_kernel(own, r1, r2, r3, x_two, mixed, cotangent, gains, scale, dots_d, grad_two, grad_b, dots):
    total = to_mp_order(total_of(own, r1, r2, r3))
    grad = cotangent[...].astype(f32) + norm_back(x_two[...], total, gains[1:2, :])
    grad_two[...] = grad
    grad_b[...] = (grad * scale[...]).astype(bf16)
    dots[0:1] = jnp.sum(grad * mixed[...], axis=0, keepdims=True)
    dots[1:2] = dots_d[...]


def first_back_kernel(own, r1, r2, r3, tokens, grad_two, gains, out):
    total = to_mp_order(total_of(own, r1, r2, r3))
    value = tokens[...].astype(f32)
    out[...] = (grad_two[...] + norm_back(value, total, gains[0:1, :])).astype(bf16)


def attention_back_kernel(spans, where, p0, p1, p2, p3, p4, p5, p6, p7, b0, b1, b2, b3, b4, b5, w_out, flat,
                          cos, sin, mixed, qkv, probs, stats,
                          send, keep, grad_out, grads, throughs, through_out, dots, part, incoming):
    blocks = eight(b0, b1, b2, b3, b4, b5)
    width = CHUNK
    join_rows(where, (p0, p1, p2, p3, p4, p5, p6, p7), grad_out)
    a, b = spans[("A", 3)][0], spans[("B", 3)][0]
    low = dora_scale * mm_t(grad_out[...], flat[:, b : b + D])
    through_out[...] = low
    grad_att = (mm_t(grad_out[...], w_out[...]) + mm2(low, flat[:, a : a + width])).astype(bf16)
    for head in range(width // HEAD_DIM):
        lanes = [slice(p * width + head * HEAD_DIM, p * width + (head + 1) * HEAD_DIM) for p in range(3)]
        query, keys, value = [qkv[:, one] for one in lanes]
        grad = grad_att[:, head * HEAD_DIM : (head + 1) * HEAD_DIM]
        weights = probs[head]
        grad_weights = mm_t(grad, value)
        incoming[:, lanes[2]] = mm_f(weights.astype(bf16), grad)
        centred = jnp.sum(weights * grad_weights, axis=-1, keepdims=True)
        grad_scores = (weights * (grad_weights - centred)).astype(bf16)
        grad_query = mm(grad_scores, keys) * HEAD_DIM ** (-0.5)
        grad_key = mm_f(grad_scores, query) * HEAD_DIM ** (-0.5)
        incoming[:, lanes[0]] = grad_query * cos[...] - swap64(grad_query) * sin[...]
        incoming[:, lanes[1]] = grad_key * cos[...] - swap64(grad_key) * sin[...]
    dots[...] = jnp.sum(incoming[...] * mixed[...], axis=0, keepdims=True)
    grads[...] = (incoming[...] * stats[0:1, :]).astype(bf16)
    through = []
    for p in range(3):
        b = spans[("B", p)][0]
        low = dora_scale * mm_t(grads[:, p * width : (p + 1) * width], flat[:, b : b + width])
        throughs[:, p * RANK : (p + 1) * RANK] = low
        through.append(halves(low))
    for index, block in enumerate(blocks):
        chunk = where[4 + index]
        total = None
        for p in range(3):
            a = spans[("A", p)][0]
            lowers = flat[:, pl.ds(pl.multiple_of(a + chunk * CHUNK, TILE), CHUNK)]
            one = mm_t(grads[:, p * width : (p + 1) * width], block(p))
            one += mm(through[p][0], lowers) + mm(through[p][1], lowers)
            total = one if total is None else total + one
        part[:, at(chunk, CHUNK)] = total
    split_rows(where, part, send, keep, send.shape[0] // N_Z)


def to_blocks(value, tiles, out, begin):
    pairs = value.shape[1] // TILE
    for index in range(pairs):
        tiles[index] = tile(value, index)
    for part in range(8):
        even, odd = merge(tiles[0:pairs, part, :], tiles[0:pairs, 8 + part, :])
        lanes = slice(part * TILE, (part + 1) * TILE)
        out[begin : begin + pairs, lanes] = even
        out[begin + pairs : begin + 2 * pairs, lanes] = odd


def column_grads_kernel(spans, projections, width, where, x, b0, b1, b2, b3, b4, b5, flat, stats, grads, throughs,
                        lows, dots, out_a, out_b, out_m, tiles, whole):
    blocks = eight(b0, b1, b2, b3, b4, b5)
    for position, p in enumerate(projections):
        a, b = spans[("A", p)][0], spans[("B", p)][0]
        lanes = slice(position * width, (position + 1) * width)
        ranks = slice(position * RANK, (position + 1) * RANK)
        upper = flat[:, b : b + width]
        norm = stats[1:2, lanes]
        inverse = 1.0 / norm
        e = dots[0:1, lanes]
        out_m[0:1, lanes] = e * inverse
        ratio = -e * stats[2:3, lanes] * inverse * inverse * inverse
        scaled = halves(dora_scale * upper.astype(f32) * ratio)
        through = halves(throughs[:, ranks])
        square = dora_scale * (mm_t(scaled[0], upper) + mm_t(scaled[1], upper))
        lower = flat[:, a : a + D]
        whole[...] = mm2(square, lower) + mm_f(through[0], x[...]) + mm_f(through[1], x[...])
        crossed = dora_scale * mm2(mm_t(lower, lower), upper)
        for index, block in enumerate(blocks):
            chunk = where[4 + index]
            weights = block(position)
            whole[:, at(chunk, CHUNK)] += mm_t(scaled[0], weights) + mm_t(scaled[1], weights)
            crossed += mm(flat[:, pl.ds(pl.multiple_of(a + chunk * CHUNK, TILE), CHUNK)], weights)
        to_blocks(whole[...], tiles, out_a, position * D * RANK // BLOCK)
        upper_grad = dora_scale * (mm2_f(lows[:, ranks], grads[:, lanes]) + crossed * ratio)
        to_blocks(upper_grad, tiles, out_b, position * width * RANK // BLOCK)


def row_grads_kernel(spans, p, where, x, weights_ref, flat, scale_row, norm_row, mag_row, grads, through_in, low, dots,
                     out_a, out_b, tiles, local):
    a, size = spans[("A", p)]
    b = spans[("B", p)][0]
    weights = weights_ref[...]
    inputs = x[...]
    if p == 6:
        value = inputs.astype(f32)
        value = jnp.where(where[3] == 0, value, pltpu.roll(value, WIDE - FILL, 1))
        local[...] = value.astype(bf16)
        inputs = local[:, 0:size]
    lower = flat[:, a : a + size]
    upper = flat[:, b : b + D]
    inverse = 1.0 / norm_row[...]
    ratio = -dots[...] * mag_row[...] * inverse * inverse * inverse
    scaled = halves(dora_scale * upper.astype(f32) * ratio)
    square = dora_scale * (mm_t(scaled[0], upper) + mm_t(scaled[1], upper))
    grad = mm2(square, lower) + mm2_f(through_in[...], inputs)
    grad += mm_t(scaled[0], weights) + mm_t(scaled[1], weights)
    if size % TILE:
        grad = jnp.concatenate([grad, jnp.zeros((RANK, TILE - size % TILE), f32)], axis=1)
    to_blocks(grad, tiles, out_a, 0)
    crossed = mm(lower, weights) + dora_scale * mm2(mm_t(lower, lower), upper)
    to_blocks(dora_scale * (mm2_f(low[...], grads[...]) + crossed * ratio), tiles, out_b, 0)


def pack_kernel(where, a_f, a_a, b_d, b_o, m_f, m_a, dots_o, norm_o, dots_d, norm_d, give, keep, rows, flat):
    begin = 0
    for array in (a_f, a_a, b_d, b_o):
        rows[begin : begin + array.shape[0]] = array[...]
        begin += array.shape[0]
    flat[...] = jnp.zeros_like(flat)
    for p in range(3):
        lanes = pl.ds(pl.multiple_of(p * D + where[1] * CHUNK, TILE), CHUNK)
        flat[:, lanes] = m_a[:, p * CHUNK : (p + 1) * CHUNK]
    flat[:, 3 * D : 4 * D] = dots_o[...] / norm_o[...]
    for p in range(2):
        first = 4 * D + p * FF + where[2] * (2 * FF // N_MP) + where[3] * (WIDE - TILE)
        flat[:, pl.ds(pl.multiple_of(first, TILE), WIDE)] = m_f[:, p * WIDE : (p + 1) * WIDE]
    flat[:, 4 * D + 2 * FF :] = dots_d[...] / norm_d[...]
    rows[begin:] = jnp.zeros((rows.shape[0] - begin, BLOCK), f32)
    for index in range(flat.shape[1] // BLOCK):
        rows[begin + index : begin + index + 1] = flat[:, index * BLOCK : (index + 1) * BLOCK]
    unit = rows.shape[0] // N_MP
    for line in range(N_Z):
        give[line * unit : (line + 1) * unit] = rows[at(2 * line + 1 - where[3], unit)].astype(bf16)
        keep[line * unit : (line + 1) * unit] = rows[at(2 * line + where[3], unit)]


def local_kernel(where, own, r1, r2, r3, b_f, b_a, a_d, a_o, mine, p1, p2, p3, rows):
    begin = own.shape[0]
    rows[0:begin] = total_of(own, r1, r2, r3)
    for array in (b_f, b_a, a_d, a_o):
        rows[begin : begin + array.shape[0]] = array[...]
        begin += array.shape[0]
    rows[begin:] = jnp.zeros((rows.shape[0] - begin, BLOCK), f32)
    part = mine.shape[0]
    mine[...] = rows[at(where[0], part)]
    for step, piece in ((1, p1), (2, p2), (3, p3)):
        piece[...] = rows[at(jnp.bitwise_xor(where[0], step), part)].astype(bf16)


def last_sum_kernel(own, r1, r2, r3, out):
    out[...] = total_of(own, r1, r2, r3).astype(bf16)


def update_kernel(index, mine, s0, s1, s2, s3, s4, s5, s6, s7, master, first, second, new_master, new_first, new_second):
    picked = pick(index[...], (s0, s1, s2, s3, s4, s5, s6, s7)).astype(bf16)
    grad = jnp.where(mine[...] >= COUNT_FLAT, picked.astype(f32), mm_t(picked, order_matrix()))
    grad = jnp.where(mine[...] >= 0, grad, 0.0)
    rates = jnp.where(mine[...] < COUNT_FLAT, rate_upper, rate_magnitude)
    rates = jnp.where(mine[...] < COUNT_LOWER, rate_lower, rates)
    rates = jnp.where(mine[...] < 0, 0.0, rates)
    weight = master[...]
    first_new = beta_one * first[...] + (1.0 - beta_one) * grad
    second_new = beta_two * second[...] + (1.0 - beta_two) * grad * grad
    first_hat = first_new / (1.0 - beta_one**STEP)
    second_hat = second_new / (1.0 - beta_two**STEP)
    new_master[...] = weight - rates * (
        first_hat / (jnp.sqrt(second_hat) + adam_eps) + weight_decay * weight
    )
    new_first[...] = first_new
    new_second[...] = second_new


COUNT_LOWER = RANK * (6 * D + FF) // BLOCK
COUNT_FLAT = COUNT_LOWER + RANK * (5 * D + 2 * FF) // BLOCK


def block_starts():
    starts = {}
    total = 0
    for kind, side in (("A", 0), ("B", 1)):
        for index, sizes in enumerate(proj_dims()):
            starts[(kind, index)] = total
            total += sizes[side] * RANK // BLOCK
    return starts


def fast_body(
    tokens,
    cotangent,
    norm_gains,
    w_attn,
    w_in,
    w_down,
    segments,
    owners,
    master,
    first_moment,
    second_moment,
):
    rows = tokens.shape[0]
    mi = lax.axis_index("mp")
    di = lax.axis_index("dp")
    core = mi % 2
    zi = mi // 2
    share = rows // N_MP
    capacity = master.shape[0]
    n_blocks = owners.shape[0]
    width = D // N_MP
    starts = block_starts()

    def mp_swap(values, step):
        return lax.ppermute(values, "mp", [(i, i ^ step) for i in range(N_MP)])

    def dp_swap(values, step):
        return lax.ppermute(values, "dp", [(i, i ^ step) for i in range(N_DP)])

    order = [(0, 0), (1, 0), (2, 0), (3, 0), (0, 1), (2, 1), (1, 1), (3, 1)]
    chunks = [(di ^ t) * 2 + (core ^ h) for t, h in order]
    where = jnp.stack([di, mi, zi, core] + chunks).astype(jnp.int32)

    def stack(first, second, after=()):
        shape = (2,) + first.shape
        return run(
            stack_kernel, [first, second], "hh", [shape_of(shape, bf16)], name="stack", after=after, us=0.6
        )[0]

    def plane_first(a, b):
        return a, dp_swap(a, 1), b, dp_swap(b, 2)

    def plane_second(a, ax, b, by, after=()):
        return [a, ax, dp_swap(stack(a, ax, after), 2), b, by, dp_swap(stack(b, by, after), 1)]

    def plane(a, b):
        return plane_second(*plane_first(a, b))

    features = run(
        first_norm_kernel,
        [tokens, norm_gains],
        "hh",
        [shape_of((rows, D), bf16)],
        name="first_norm",
        megabytes=6,
        us=1.2,
    )[0]

    sent = master.astype(bf16)
    line = [sent] + [mp_swap(sent, 2 * step) for step in range(1, N_Z)]
    sheet = plane(jnp.concatenate(line[:2]), jnp.concatenate(line[2:]))
    sheet = [one.reshape(-1, BLOCK) for one in sheet]
    def cut(weights, count, chip):
        pieces = []
        for index in range(N_Z):
            piece = lax.dynamic_slice(weights, (0, di * 64, (zi ^ index) * chip), (count, 64, chip))
            pieces.append(mp_swap(piece, 2 * index) if index else piece)
        return pieces

    def columns_of(pieces, size, step, name, after=()):
        count = pieces[0].shape[0]
        a, forward = run(
            functools.partial(line_kernel, step),
            [where] + pieces,
            "shhhh",
            [shape_of((count, CHUNK, size), bf16)] * 2,
            name=name,
            after=after,
        )
        return plane_first(a, mp_swap(forward, 1))

    first_a = columns_of(cut(w_attn, 3, 2 * width), width, width, "line_a", [features])
    blocks_a = plane_second(*first_a)
    sheet = run(
        join_all_kernel, sheet, "h" * 6, [shape_of((16 * capacity, BLOCK), bf16)], name="adapter_rows", us=1.0, after=[first_a[2]]
    )[0]
    stacked = [sheet, mp_swap(sheet, 1)]
    w_in_late, stacked[1] = lax.optimization_barrier((w_in, stacked[1]))
    pieces_f = cut(w_in_late, 2, 2 * FF // N_MP)
    w_out = w_attn[3]

    ranks = slot_positions(owners, 0)
    owner_d, owner_m = owners // N_MP, owners % N_MP
    piece_at = (owner_d ^ di) * N_Z + ((owner_m // 2) ^ zi)
    listed = np.array([0, 1, 8, 9, 2, 3, 12, 13, 4, 5, 10, 11, 6, 7, 14, 15], np.int32)
    piece_at = jnp.sum(jnp.where(piece_at[:, None] == np.arange(16), listed, 0), axis=1)
    slot = (((owner_m % 2) ^ core) * 16 + piece_at) * capacity + ranks
    wanted = []
    spans = {}

    def want(name, blocks, size):
        spans[name] = (sum(w.shape[0] for w in wanted) * 64, size)
        wanted.append(blocks)

    by_dp = np.array(
        [(2 * z + c) * 4 + d for d in range(N_DP) for c in range(2) for z in range(N_Z)], np.int32
    )
    all_blocks = np.arange(D * RANK // BLOCK, dtype=np.int32)
    for index in (0, 1, 2, 4, 5):
        want(("A", index), starts[("A", index)] + by_dp, D)
        if index < 3:
            want(("B", index), starts[("B", index)] + mi * 4 + np.arange(4), width)
        else:
            first_block = starts[("B", index)] + zi * 22 + core * 10
            want(("B", index), first_block + np.arange(12), WIDE)
    want(("A", 3), starts[("A", 3)] + mi * 4 + np.arange(4), width)
    want(("B", 3), starts[("B", 3)] + all_blocks, D)
    want(("A", 6), starts[("A", 6)] + mi * 11 + np.minimum(np.arange(12), 10), FF // N_MP)
    want(("B", 6), starts[("B", 6)] + all_blocks, D)
    chosen = jnp.take(slot, jnp.concatenate([jnp.asarray(w, jnp.int32) for w in wanted]))
    n_pairs = chosen.shape[0] // 2
    pairs = chosen.reshape(n_pairs, 2)
    flat, mags = run(
        adapters_kernel,
        [pairs[:, :1], pairs[:, 1:], slot[COUNT_FLAT:, None]] + stacked,
        "vvv" + "h" * len(stacked),
        [shape_of((RANK, n_pairs * TILE), bf16), shape_of((1, (n_blocks - COUNT_FLAT) * BLOCK), f32)],
        [pltpu.VMEM((n_pairs, RANK, TILE), f32)],
        name="adapters", megabytes=13, us=5,
    )

    def bind(kernel, *args):
        return functools.partial(kernel, spans, *args)

    def mp_sum(value):
        for step in (1, 2, 4):
            value = value + mp_swap(value, step)
        return value

    def column_grads(projections, size, x, blocks, flat, stats, grads, throughs, lows, dots, after):
        count = len(projections)
        return run(
            bind(column_grads_kernel, projections, size),
            [where, x] + blocks + [flat, stats, grads, throughs, lows, dots],
            "s" + "h" * 13,
            [
                shape_of((count * D * RANK // BLOCK, BLOCK), f32),
                shape_of((count * size * RANK // BLOCK, BLOCK), f32),
                shape_of((1, count * size), f32),
            ],
            [pltpu.VMEM((D // TILE, RANK, TILE), f32), pltpu.VMEM((RANK, D), f32)],
            name="column_grads", megabytes=9, us=8,
            after=after,
        )

    def row_grads(p, x, weights, flat, scale, norm, mag, grads, through, low, dots, after):
        size = spans[("A", p)][1]
        return run(
            bind(row_grads_kernel, p),
            [where, x, weights, flat, scale, norm, mag, grads, through, low, dots],
            "s" + "h" * 10,
            [
                shape_of((-(-size // TILE) * 2, BLOCK), f32),
                shape_of((D * RANK // BLOCK, BLOCK), f32),
            ],
            [pltpu.VMEM((D // TILE, RANK, TILE), f32), pltpu.VMEM((rows, WIDE), bf16)],
            name="row_grads", megabytes=6, us=3,
            after=after,
        )

    row = segments[0]
    cosine, sine = rotary_tables(segment_positions(row))
    cosine, sine = cosine[:, 0], sine[:, 0]
    cos_full = jnp.concatenate([cosine, cosine], axis=-1)
    sin_full = jnp.concatenate([-sine, sine], axis=-1)
    tokens_here = lax.dynamic_slice_in_dim(tokens, mi * share, share, 0)
    cotangent_here = lax.dynamic_slice_in_dim(cotangent, mi * share, share, 0)
    half_rows = [shape_of((rows // 2, D), bf16), shape_of((rows // 2, D), f32)]

    def finish_rows(send, keep, after):
        received = mp_swap(send, 1)
        p1, p2, p3, own = run(
            pair_kernel,
            [where, keep, received],
            "shh",
            [shape_of((share, D), bf16)] * 3 + [shape_of((share, D), f32)],
            name="pair_sums", megabytes=4, us=1.2,
            after=after,
        )
        return [own, mp_swap(p1, 2), mp_swap(p2, 4), mp_swap(p3, 6)]

    def gather_rows(value):
        mine = [value] + [mp_swap(value, 2 * step) for step in range(1, N_Z)]
        return mine + [mp_swap(one, 1) for one in mine]

    n_heads = width // HEAD_DIM
    send, keep, mixed_a, qkv, probs, att, low_a, low_o, stats_a = run(
        bind(attention_kernel),
        [where, features] + blocks_a + [w_out, flat, mags, cos_full, sin_full, segments, row[:, None]],
        "s" + "h" * 14,
        half_rows
        + [
            shape_of((rows, 3 * width), f32),
            shape_of((rows, 3 * width), bf16),
            shape_of((n_heads, rows, rows), f32),
            shape_of((rows, width), bf16),
            shape_of((rows, 3 * RANK), f32),
            shape_of((rows, RANK), f32),
            shape_of((8, 3 * width), f32),
        ],
        [pltpu.VMEM((rows, D), f32)],
        name="attention", megabytes=13, us=10,
    )

    sums_o = finish_rows(send, keep, [])
    squares = run(
        bind(row_norm_kernel), [w_out, w_down, flat], "hhh", [shape_of((2, D), f32)], name="row_norms", megabytes=3, us=1.6, after=[sums_o[1]]
    )[0]
    first_f = columns_of(pieces_f, WIDE, WIDE - TILE, "line_f", [send])
    blocks_f = plane_second(*first_f, after=[sums_o[1]])
    squares = mp_sum(squares)
    norm_o = jnp.sqrt(squares[:1] + column_eps)
    norm_d = jnp.sqrt(squares[1:] + column_eps)
    mag_o = mags[:, 3 * D : 4 * D]
    mag_d = mags[:, 4 * D + 2 * FF :]
    scale_o, scale_d = mag_o / norm_o, mag_d / norm_d
    squares_f = run(
        bind(wide_first_kernel),
        [where] + [blocks_f[k] for k in (0, 1, 3, 4)] + [flat],
        "s" + "h" * 5,
        [shape_of((1, 2 * WIDE), f32)],
        name="wide_squares", megabytes=8, us=3,
        after=[scale_o],
    )[0]
    x_two, mixed_o, features_two = run(
        second_norm_kernel,
        sums_o + [tokens_here, norm_gains, scale_o],
        "h" * 7,
        [shape_of((share, D), f32)] * 2 + [shape_of((share, D), bf16)],
        name="second_norm", megabytes=3, us=0.5,
        after=[squares_f],
    )
    pieces = gather_rows(features_two)
    d_act, grad_d, through_d = run(
        bind(down_back_kernel),
        [where, cotangent, scale_d, w_down, flat],
        "shhhh",
        [shape_of((rows, WIDE), f32), shape_of((rows, D), bf16), shape_of((rows, RANK), f32)],
        [pltpu.VMEM((rows, WIDE), f32)],
        name="down_back", megabytes=7, us=3.5,
        after=[features_two],
    )
    stats_f = run(
        bind(wide_norm_kernel),
        [where] + [blocks_f[k] for k in (2, 5)] + [flat, mags, squares_f],
        "s" + "h" * 5,
        [shape_of((8, 2 * WIDE), f32)],
        name="wide_norms", megabytes=8, us=3,
        after=[through_d],
    )[0]
    send, keep, x_f, act, grads_f, through_f, low_f, dots_f = run(
        bind(middle_kernel),
        [where] + pieces + blocks_f + [d_act, flat, stats_f],
        "s" + "h" * 17,
        half_rows
        + [
            shape_of((rows, D), bf16),
            shape_of((rows, WIDE), bf16),
            shape_of((rows, 2 * WIDE), bf16),
            shape_of((rows, 2 * RANK), f32),
            shape_of((rows, 2 * RANK), f32),
            shape_of((1, 2 * WIDE), f32),
        ],
        [pltpu.VMEM((rows, D), f32), pltpu.VMEM((rows, 2 * WIDE), f32)],
        name="feed_forward", megabytes=22, us=14,
    )
    send_d, keep_d, low_d, dots_d = run(
        bind(down_kernel),
        [where, act, w_down, flat, cotangent],
        "shhhh",
        half_rows + [shape_of((rows, RANK), f32), shape_of((1, D), f32)],
        [pltpu.VMEM((rows, D), f32), pltpu.VMEM((rows, WIDE), bf16)],
        name="down", megabytes=9, us=3.5,
    )
    sums = finish_rows(send, keep, [low_d])
    a_f, b_f, m_f = column_grads(
        (4, 5), WIDE, x_f, blocks_f, flat, stats_f, grads_f, through_f, low_f, dots_f, [sums[1]]
    )
    grad_two, grad_o_piece, dots_o = run(
        second_back_kernel,
        sums + [x_two, mixed_o, cotangent_here, norm_gains, scale_o, dots_d],
        "h" * 10,
        [shape_of((share, D), f32), shape_of((share, D), bf16), shape_of((2, D), f32)],
        name="second_norm_back", megabytes=3, us=0.5,
        after=[m_f],
    )
    pieces_o = gather_rows(grad_o_piece)
    dots_here = dots_o
    dots_o, dots_d = dots_here[:1], dots_here[1:]
    dots_all = mp_sum(dots_here)
    a_d, b_d = row_grads(
        6, act, w_down, flat, scale_d, norm_d, mag_d, grad_d, through_d, low_d, dots_all[1:], []
    )
    sums_d = finish_rows(send_d, keep_d, pieces_o + [a_d])
    send, keep, grad_o, grads_a, through_a, through_o, dots_a = run(
        bind(attention_back_kernel),
        [where] + pieces_o + blocks_a + [w_out, flat, cos_full, sin_full, mixed_a, qkv, probs, stats_a],
        "s" + "h" * 22,
        half_rows
        + [
            shape_of((rows, D), bf16),
            shape_of((rows, 3 * width), bf16),
            shape_of((rows, 3 * RANK), f32),
            shape_of((rows, RANK), f32),
            shape_of((1, 3 * width), f32),
        ],
        [pltpu.VMEM((rows, D), f32), pltpu.VMEM((rows, 3 * width), f32)],
        name="attention_back", megabytes=10, us=9.5,
        after=[sums_d[0]],
    )
    a_o, b_o = row_grads(
        3, att, w_out, flat, scale_o, norm_o, mag_o, grad_o, through_o, low_o, dots_all[:1], [send]
    )
    sums = finish_rows(send, keep, [a_o])
    a_a, b_a, m_a = column_grads(
        (0, 1, 2), width, features, blocks_a, flat, stats_a, grads_a, through_a, low_a, dots_a, [sums[1]]
    )
    out_piece = run(
        out_kernel,
        sums_d + [x_two, scale_d],
        "h" * 6,
        [shape_of((share, D), bf16)],
        name="layer_out",
        after=[m_a],
    )[0]
    grad_in = run(
        first_back_kernel,
        sums + [tokens_here, grad_two, norm_gains],
        "h" * 7,
        [shape_of((share, D), bf16)],
        name="first_norm_back", megabytes=3, us=0.5,
        after=[out_piece],
    )[0]

    def join(pieces, kind):
        return run(
            join_kernel, [where] + pieces, "s" + "h" * 8, [shape_of((rows, D), kind)], name="join_rows", megabytes=6, us=1.5
        )[0]

    input_grad = join(gather_rows(grad_in), f32)
    layer_out = join(gather_rows(out_piece), bf16)

    unit, part = 32, 24
    give, kept = run(
        pack_kernel,
        [where, a_f, a_a, b_d, b_o, m_f, m_a, dots_o, norm_o, dots_d, norm_d],
        "s" + "h" * 10,
        [shape_of((N_Z * unit, BLOCK), bf16), shape_of((N_Z * unit, BLOCK), f32)],
        [pltpu.VMEM((N_MP * unit, BLOCK), f32), pltpu.VMEM((1, (n_blocks - COUNT_FLAT) * BLOCK), f32)],
        name="pack", megabytes=4, us=1,
    )
    p1, p2, p3, own = run(
        pair_kernel,
        [where, kept, mp_swap(give, 1)],
        "shh",
        [shape_of((unit, BLOCK), bf16)] * 3 + [shape_of((unit, BLOCK), f32)],
        name="pack_sums",
    )
    own, p1, p2, p3 = run(
        local_kernel,
        [where, own, mp_swap(p1, 2), mp_swap(p2, 4), mp_swap(p3, 6), b_f, b_a, a_d, a_o],
        "s" + "h" * 8,
        [shape_of((part, BLOCK), f32)] + [shape_of((part, BLOCK), bf16)] * 3,
        [pltpu.VMEM((N_DP * part, BLOCK), f32)],
        name="local_sums",
    )
    own = run(
        last_sum_kernel,
        [own, dp_swap(p1, 1), dp_swap(p2, 2), dp_swap(p3, 3)],
        "hhhh",
        [shape_of((part, BLOCK), bf16)],
        name="last_sums",
    )[0]
    lines = jnp.concatenate([own] + [mp_swap(own, 2 * step) for step in range(1, N_Z)])
    summed = [lines] + [dp_swap(lines, step) for step in range(1, N_DP)]
    summed = summed + [mp_swap(one, 1) for one in summed]

    table = np.zeros((n_blocks,), np.int32)

    def note(block, m, r):
        table[block] = ((r // part) * N_MP + m) * 64 + r % part

    def split_pairs(count, r):
        return r // 2 + (r % 2) * (count // 2)

    def blocks_of(names):
        def listing(count, m):
            each = count // len(names)
            for position, blocks in enumerate(names):
                for k, block in enumerate(blocks(m)):
                    if block is not None:
                        yield position * each + split_pairs(each, k), block

        return listing

    def lower_columns(p):
        return lambda m: [starts[("A", p)] + int(k) for k in by_dp]

    def upper_rows(p):
        return lambda m: [starts[("B", p)] + int(k) for k in all_blocks]

    def lower_rows(p, per):
        return lambda m: [starts[("A", p)] + m * per + k for k in range(per)]

    def upper_columns(p):
        if p < 3:
            return lambda m: [starts[("B", p)] + m * 4 + k for k in range(4)]
        return lambda m: [
            starts[("B", p)] + (m // 2) * 22 + (m % 2) * 10 + k
            if (k < 11 if m % 2 == 0 else k >= 1)
            else None
            for k in range(12)
        ]

    begin = 0
    for listing, count in (
        (blocks_of([lower_columns(4), lower_columns(5)]), a_f.shape[0]),
        (blocks_of([lower_columns(p) for p in range(3)]), a_a.shape[0]),
        (blocks_of([upper_rows(6)]), b_d.shape[0]),
        (blocks_of([upper_rows(3)]), b_o.shape[0]),
        (lambda count, m: [(r, COUNT_FLAT + r) for r in range(count)], n_blocks - COUNT_FLAT),
    ):
        for r, block in listing(count, None):
            note(block, (begin + r) // unit, (begin + r) % unit)
        begin += count
    begin = unit
    for listing, count in (
        (blocks_of([upper_columns(4), upper_columns(5)]), b_f.shape[0]),
        (blocks_of([upper_columns(p) for p in range(3)]), b_a.shape[0]),
        (blocks_of([lower_rows(6, 11)]), a_d.shape[0]),
        (blocks_of([lower_rows(3, 4)]), a_o.shape[0]),
    ):
        for m in range(N_MP):
            for r, block in listing(count, m):
                note(block, m, begin + r)
        begin += count
    me = di * N_MP + mi
    hits = (owners * capacity + ranks)[None, :] == me * capacity + jnp.arange(capacity)[:, None]
    mine = jnp.sum(jnp.where(hits, jnp.arange(n_blocks)[None, :] + 1, 0), axis=1) - 1
    code = jnp.sum(jnp.where(hits, jnp.asarray(table)[None, :], 0), axis=1)
    device, inner = code // 64, code % 64
    d_from, m_from = device // N_MP, device % N_MP
    list_at = (((m_from % 2) ^ core) * N_DP + (d_from ^ di)) * N_Z + ((m_from // 2) ^ zi)
    index = list_at * part + inner
    new_master, new_first, new_second = run(
        update_kernel,
        [index[:, None], mine[:, None]] + summed + [master, first_moment, second_moment],
        "vv" + "h" * 11,
        [shape_of(master.shape, f32)] * 3,
        name="update", megabytes=4, us=2,
    )
    return (layer_out, input_grad, new_master, new_first, new_second)


def solution(mesh):
    fast = mesh.shape["dp"] == 4 and mesh.shape["mp"] == 8
    return jax.shard_map(
        fast_body if fast else body,
        mesh=mesh,
        in_specs=(
            P("dp", None),
            P("dp", None),
            P(),
            P(None, "mp", None),
            P(None, "mp", None),
            P("mp", None),
            P("dp", None),
            P(),
            P(("dp", "mp"), None),
            P(("dp", "mp"), None),
            P(("dp", "mp"), None),
        ),
        out_specs=(
            P("dp", None),
            P("dp", None),
            P(("dp", "mp"), None),
            P(("dp", "mp"), None),
            P(("dp", "mp"), None),
        ),
        check_vma=False,
    )
```

```python
import functools

import jax
import jax.numpy as jnp
import numpy as np
from jax import lax
from jax.experimental import pallas as pl
from jax.experimental.pallas import tpu as pltpu
from jax.sharding import PartitionSpec as P

D = 2048
FF = 5632
HEADS = 16
HEAD_DIM = 128
RANK = 16
BLOCK = 1024
STEP = 5


dora_scale = 2.0
rope_base = 10000.0
norm_eps = 1e-05
column_eps = 1e-06
beta_one = 0.5
beta_two = 0.5
adam_eps = 1e-08
weight_decay = 0.01
rate_lower = 0.02
rate_upper = 0.1
rate_magnitude = 1.0
highest = lax.Precision.HIGHEST


def proj_dims():
    return [(D, D), (D, D), (D, D), (D, D), (D, FF), (D, FF), (FF, D)]


def unpack(flat):
    offset = 0
    lowers = []
    for inner, outer in proj_dims():
        lowers.append(flat[offset : offset + inner * RANK].reshape(inner, RANK))
        offset += inner * RANK
    uppers = []
    for inner, outer in proj_dims():
        uppers.append(flat[offset : offset + outer * RANK].reshape(outer, RANK))
        offset += outer * RANK
    magnitudes = []
    for inner, outer in proj_dims():
        magnitudes.append(flat[offset : offset + outer])
        offset += outer
    return (lowers, uppers, magnitudes)


def slot_positions(owners, capacity):
    order = jnp.arange(owners.shape[0], dtype=jnp.int32)
    same = (owners[:, None] == owners[None, :]) & (order[None, :] < order[:, None])
    ranks = jnp.sum(same.astype(jnp.int32), axis=1)
    return owners * capacity + ranks


def block_rates(block_ids):
    count_lower = RANK * (6 * D + FF) // BLOCK
    count_upper = RANK * (5 * D + 2 * FF) // BLOCK
    rates = jnp.where(block_ids < count_lower + count_upper, rate_upper, rate_magnitude)
    rates = jnp.where(block_ids < count_lower, rate_lower, rates)
    return jnp.where(block_ids < 0, 0.0, rates).astype(jnp.float32)


def adam_update(weight, grad, first, second, rates):
    first_new = beta_one * first + (1.0 - beta_one) * grad
    second_new = beta_two * second + (1.0 - beta_two) * grad * grad
    first_hat = first_new / (1.0 - beta_one**STEP)
    second_hat = second_new / (1.0 - beta_two**STEP)
    weight_new = weight - rates[:, None] * (
        first_hat / (jnp.sqrt(second_hat) + adam_eps) + weight_decay * weight
    )
    return (weight_new, first_new, second_new)


def rms_norm(values, gain):
    return values * lax.rsqrt(jnp.mean(values * values, axis=-1, keepdims=True) + norm_eps) * gain


def rms_back(values, grad, gain):
    inverse = lax.rsqrt(jnp.mean(values * values, axis=-1, keepdims=True) + norm_eps)
    scaled = grad * gain
    return inverse * (
        scaled - values * inverse * inverse * jnp.mean(scaled * values, axis=-1, keepdims=True)
    )


def segment_positions(row):
    order = jnp.arange(row.shape[0], dtype=jnp.int32)
    change = jnp.concatenate([jnp.ones((1,), dtype=bool), row[1:] != row[:-1]])
    starts = lax.cummax(jnp.where(change, order, 0), axis=0)
    return order - starts


def rotary_tables(positions):
    half = HEAD_DIM // 2
    freqs = rope_base ** (-(jnp.arange(half).astype(jnp.float32) * 2.0 / HEAD_DIM))
    angles = positions.astype(jnp.float32)[:, None] * freqs[None, :]
    return (jnp.cos(angles)[:, None, :], jnp.sin(angles)[:, None, :])


def rotate(values, cosine, sine):
    half = values.shape[-1] // 2
    first_half = values[..., :half]
    second_half = values[..., half:]
    return jnp.concatenate(
        [first_half * cosine - second_half * sine, second_half * cosine + first_half * sine],
        axis=-1,
    )


def unrotate(values, cosine, sine):
    half = values.shape[-1] // 2
    first_half = values[..., :half]
    second_half = values[..., half:]
    return jnp.concatenate(
        [first_half * cosine + second_half * sine, second_half * cosine - first_half * sine],
        axis=-1,
    )


def body(
    tokens,
    cotangent,
    norm_gains,
    w_attn,
    w_in,
    w_down,
    segments,
    owners,
    master,
    first_moment,
    second_moment,
):
    group_rows = tokens.shape[0]
    model_size = lax.axis_size("mp")
    model_index = lax.axis_index("mp")
    share = group_rows // model_size
    share_start = model_index * share
    capacity = master.shape[0]
    everyone = lax.axis_size(("dp", "mp"))
    score_scale = HEAD_DIM ** (-0.5)
    widths = [outer for inner, outer in proj_dims()]
    slot_index = slot_positions(owners, capacity)
    copies = lax.all_gather(master.astype(jnp.bfloat16), ("dp", "mp"), axis=0, tiled=True)
    lowers, uppers, magnitudes = unpack(jnp.take(copies, slot_index, axis=0).reshape(-1))
    frozen = [w_attn[0], w_attn[1], w_attn[2], w_attn[3], w_in[0], w_in[1], w_down]
    lower_local = []
    combined = []
    square_parts = []
    for index in range(7):
        rows_here = frozen[index].shape[0]
        piece = lax.dynamic_slice_in_dim(lowers[index], model_index * rows_here, rows_here, 0)
        lower_local.append(piece)
        joined = frozen[index].astype(jnp.float32) + dora_scale * jnp.dot(
            piece.astype(jnp.float32), uppers[index].astype(jnp.float32).T, precision=highest
        )
        combined.append(joined)
        square_parts.append(jnp.sum(joined * joined, axis=0))

    def rows_of(values):
        return lax.dynamic_slice_in_dim(values, share_start, share, 0)

    def split_parts(values, indices, axis):
        pieces = []
        offset = 0
        for index in indices:
            pieces.append(lax.slice_in_dim(values, offset, offset + widths[index], axis=axis))
            offset += widths[index]
        return pieces

    norms = [None] * 7
    mixed_share = [None] * 7
    low_share = [None] * 7
    mixed_full = [None] * 7
    grads = [None] * 7

    def set_scales(indices):
        summed = lax.psum(jnp.concatenate([square_parts[index] for index in indices]), "mp")
        squares = split_parts(summed, indices, 0)
        for index, value in zip(indices, squares):
            norms[index] = jnp.sqrt(value + column_eps)

    def scale(index):
        return magnitudes[index].astype(jnp.float32) / norms[index]

    def local_partials(inputs_local, indices):
        mixed_list = []
        low_list = []
        for index in indices:
            low_part = jnp.dot(inputs_local, lower_local[index], preferred_element_type=jnp.float32)
            mixed = jnp.dot(
                inputs_local, frozen[index], preferred_element_type=jnp.float32
            ) + dora_scale * jnp.dot(
                low_part, uppers[index].astype(jnp.float32).T, precision=highest
            )
            mixed_list.append(mixed)
            low_list.append(low_part)
        return (
            inputs_local,
            jnp.concatenate(mixed_list, axis=1),
            jnp.concatenate(low_list, axis=1),
        )

    def group_partials(inputs_b, indices):
        rows_here = frozen[indices[0]].shape[0]
        inputs_local = lax.dynamic_slice_in_dim(inputs_b, model_index * rows_here, rows_here, 1)
        return local_partials(inputs_local, indices)

    def finish(indices, local_mixed, local_low):
        summed_mixed, summed_low = lax.psum((local_mixed, local_low), "mp")
        pieces = split_parts(summed_mixed, indices, 1)
        for position, index in enumerate(indices):
            mixed_full[index] = pieces[position]
            mixed_share[index] = rows_of(pieces[position])
            low_share[index] = rows_of(summed_low[:, position * RANK : (position + 1) * RANK])
        return pieces

    def gather_inputs(local):
        return lax.all_gather(local, "mp", axis=1, tiled=True)

    xf = tokens.astype(jnp.float32)
    row = segments[0]
    cosine, sine = rotary_tables(segment_positions(row))
    order = jnp.arange(group_rows)
    allowed = (row[:, None] == row[None, :]) & (order[None, :] <= order[:, None])
    features = rms_norm(xf, norm_gains[0]).astype(jnp.bfloat16)
    first_local, first_mixed, first_low = group_partials(features, (0, 1, 2))
    set_scales((0, 1, 2))
    summed_mixed, summed_low = lax.psum((first_mixed, first_low), "mp")
    pieces = split_parts(summed_mixed, (0, 1, 2), 1)
    heads_in = []
    for index in range(3):
        mixed_full[index] = pieces[index]
        mixed_share[index] = rows_of(pieces[index])
        low_share[index] = rows_of(summed_low[:, index * RANK : (index + 1) * RANK])
        projected = (pieces[index] * scale(index)).reshape(group_rows, HEADS, HEAD_DIM)
        if index < 2:
            projected = rotate(projected, cosine, sine)
        heads_in.append(projected.astype(jnp.bfloat16))
    query_b, key_b, value_b = heads_in

    def attention_scores(query_h, key_h):
        scores = (
            jnp.einsum("thd,shd->hts", query_h, key_h, preferred_element_type=jnp.float32)
            * score_scale
        )
        return jnp.where(allowed[None], scores, -1e30)

    scores = attention_scores(query_b, key_b)
    top = jnp.max(scores, axis=-1, keepdims=True)
    expd = jnp.exp(scores - top)
    total = jnp.sum(expd, axis=-1, keepdims=True)
    probs = (expd / total).astype(jnp.bfloat16)
    attended_h = jnp.einsum("hts,shd->thd", probs, value_b, preferred_element_type=jnp.float32)
    attended_h, log_total = (attended_h, top + jnp.log(total))
    attended = attended_h.reshape(group_rows, D).astype(jnp.bfloat16)
    out_local, out_mixed, out_low = group_partials(attended, (3,))
    set_scales((3,))
    x_two = xf + finish((3,), out_mixed, out_low)[0] * scale(3)
    second_features = rms_norm(x_two, norm_gains[1]).astype(jnp.bfloat16)
    ffn_local, ffn_mixed, ffn_low = group_partials(second_features, (4, 5))
    set_scales((4, 5))
    gate_pre, up_pre = finish((4, 5), ffn_mixed, ffn_low)
    gate = gate_pre * scale(4)
    upward = up_pre * scale(5)
    sigmoid_gate = jax.nn.sigmoid(gate)
    act = (gate * sigmoid_gate * upward).astype(jnp.bfloat16)
    down_local, down_mixed, down_low = group_partials(act, (6,))
    set_scales((6,))
    down_pre = finish((6,), down_mixed, down_low)[0]
    layer_out = (x_two + down_pre * scale(6)).astype(jnp.bfloat16)

    def whole_dot(index, grad):
        return jnp.sum(grad * mixed_full[index], axis=0)

    def project_back(index, grad, inputs_local, group_dot):
        norm = norms[index]
        magnitude = magnitudes[index].astype(jnp.float32)
        grad_b = (grad * (magnitude / norm)).astype(jnp.bfloat16)
        share_dot = jnp.sum(rows_of(grad) * mixed_share[index], axis=0)
        grad_full = combined[index] * (-group_dot * magnitude / (norm * norm * norm))[None, :]
        upper_f = uppers[index].astype(jnp.float32)
        lower_f = lower_local[index].astype(jnp.float32)
        through = dora_scale * jnp.dot(grad_b, uppers[index], preferred_element_type=jnp.float32)
        grad_lower = jnp.dot(
            inputs_local.astype(jnp.float32).T, through, precision=highest
        ) + dora_scale * jnp.dot(grad_full, upper_f, precision=highest)
        grad_upper = dora_scale * jnp.dot(
            rows_of(grad_b).astype(jnp.float32).T, low_share[index], precision=highest
        ) + dora_scale * jnp.dot(grad_full.T, lower_f, precision=highest)
        grads[index] = (grad_lower, grad_upper, share_dot / norm)
        return jnp.dot(grad_b, frozen[index].T, preferred_element_type=jnp.float32) + jnp.dot(
            through, lower_f.T, precision=highest
        )

    grad_out = cotangent.astype(jnp.float32)
    grad_act = gather_inputs(project_back(6, grad_out, down_local, whole_dot(6, grad_out)))
    grad_gate = grad_act * upward * sigmoid_gate * (1.0 + gate * (1.0 - sigmoid_gate))
    grad_up = grad_act * gate * sigmoid_gate
    ffn_back = project_back(4, grad_gate, ffn_local, whole_dot(4, grad_gate)) + project_back(
        5, grad_up, ffn_local, whole_dot(5, grad_up)
    )
    grad_two = grad_out + rms_back(x_two, gather_inputs(ffn_back), norm_gains[1])
    grad_att = gather_inputs(project_back(3, grad_two, out_local, whole_dot(3, grad_two)))
    grad_att = grad_att.astype(jnp.bfloat16).reshape(group_rows, HEADS, HEAD_DIM)
    weights = jnp.exp(attention_scores(query_b, key_b) - log_total)
    weights_b = weights.astype(jnp.bfloat16)
    grad_weights = jnp.einsum("thd,shd->hts", grad_att, value_b, preferred_element_type=jnp.float32)
    grad_value = jnp.einsum("hts,thd->shd", weights_b, grad_att, preferred_element_type=jnp.float32)
    centred = jnp.sum(weights * grad_weights, axis=-1, keepdims=True)
    grad_scores = (weights * (grad_weights - centred)).astype(jnp.bfloat16)
    grad_query = (
        jnp.einsum("hts,shd->thd", grad_scores, key_b, preferred_element_type=jnp.float32)
        * score_scale
    )
    grad_key = (
        jnp.einsum("hts,thd->shd", grad_scores, query_b, preferred_element_type=jnp.float32)
        * score_scale
    )
    grad_query, grad_key, grad_value = (
        unrotate(grad_query, cosine, sine),
        unrotate(grad_key, cosine, sine),
        grad_value,
    )
    incoming = [
        grad_query.reshape(group_rows, D),
        grad_key.reshape(group_rows, D),
        grad_value.reshape(group_rows, D),
    ]
    group_dots = [whole_dot(index, incoming[index]) for index in range(3)]
    first_back = project_back(0, incoming[0], first_local, group_dots[0])
    first_back = first_back + project_back(1, incoming[1], first_local, group_dots[1])
    first_back = first_back + project_back(2, incoming[2], first_local, group_dots[2])
    input_grad = grad_two + rms_back(xf, gather_inputs(first_back), norm_gains[0])
    pieces = []
    for index in range(7):
        rows_total = proj_dims()[index][0]
        grad_lower = grads[index][0]
        placed = lax.dynamic_update_slice_in_dim(
            jnp.zeros((rows_total, RANK), jnp.float32),
            grad_lower,
            model_index * grad_lower.shape[0],
            0,
        )
        pieces.append(placed.reshape(-1))
    for index in range(7):
        pieces.append(grads[index][1].reshape(-1))
    for index in range(7):
        pieces.append(grads[index][2])
    blocks = jnp.concatenate(pieces).reshape(-1, BLOCK)
    buffer = jnp.zeros((capacity * everyone, BLOCK), jnp.float32).at[slot_index].set(blocks)
    owned = lax.psum_scatter(buffer, ("dp", "mp"), scatter_dimension=0, tiled=True)
    slot_block = (
        jnp.full((capacity * everyone,), -1, jnp.int32)
        .at[slot_index]
        .set(jnp.arange(blocks.shape[0], dtype=jnp.int32))
    )
    local_blocks = lax.dynamic_slice_in_dim(
        slot_block, lax.axis_index(("dp", "mp")) * capacity, capacity, 0
    )
    new_master, new_first, new_second = adam_update(
        master, owned, first_moment, second_moment, block_rates(local_blocks)
    )
    return (layer_out, input_grad, new_master, new_first, new_second)


f32 = jnp.float32
bf16 = jnp.bfloat16
VM = pl.BlockSpec(memory_space=pltpu.VMEM)
SM = pl.BlockSpec(memory_space=pltpu.SMEM)
ANY = pl.BlockSpec(memory_space=pl.ANY)
HBM = pl.BlockSpec(memory_space=pltpu.HBM)
TILE = 128
CHUNK = 256
N_DP = 4
N_MP = 8
N_Z = 4
WIDE = 768
FILL = 64


def mm(left, right):
    return lax.dot_general(left, right, (((1,), (0,)), ((), ())), preferred_element_type=f32)


def mm_t(left, right):
    return lax.dot_general(left, right, (((1,), (1,)), ((), ())), preferred_element_type=f32)


def mm_f(left, right):
    return lax.dot_general(left, right, (((0,), (0,)), ((), ())), preferred_element_type=f32)


def halves(value):
    high = value.astype(bf16)
    return high, (value - high.astype(f32)).astype(bf16)


def mm2(left, right):
    high, low = halves(left)
    return mm(high, right) + mm(low, right)


def mm2_t(left, right):
    high, low = halves(left)
    return mm_t(high, right) + mm_t(low, right)


def mm2_f(left, right):
    high, low = halves(left)
    return mm_f(high, right) + mm_f(low, right)


def swap64(value):
    return pltpu.roll(value, 64, 1)


def low_lanes(rows):
    return lax.broadcasted_iota(jnp.int32, (rows, TILE), 1) < 64


def merge(first, second):
    low = low_lanes(first.shape[0])
    return (
        jnp.where(low, first, swap64(second)),
        jnp.where(low, swap64(first), second),
    )


def tile(value, index):
    return value[:, index * TILE : (index + 1) * TILE]


def to_dp_order(value):
    out = [None] * 16
    for core in range(2):
        for pair in range(2):
            for part in range(2):
                first = 8 * pair + 2 * core + part
                low, high = merge(tile(value, first), tile(value, first + 4))
                out[8 * part + 2 * core + pair] = low
                out[8 * part + 4 + 2 * core + pair] = high
    return jnp.concatenate(out, axis=1)


def to_mp_order(value):
    out = [None] * 16
    for core in range(2):
        for pair in range(2):
            for part in range(2):
                first = 8 * part + 2 * core + pair
                low, high = merge(tile(value, first), tile(value, first + 4))
                out[8 * pair + 2 * core + part] = low
                out[8 * pair + 2 * core + part + 4] = high
    return jnp.concatenate(out, axis=1)


def shape_of(shape, dtype):
    return jax.ShapeDtypeStruct(shape, dtype)


def run(kernel, ins, specs, outs, scratch=(), name=None, after=(), megabytes=4, us=1.0):
    n_in, n_after = len(ins), len(after)

    def body(*refs):
        kernel(*refs[:n_in], *refs[n_in + n_after :])

    kinds = {"s": SM, "v": VM, "h": VM, "r": ANY}
    return pl.pallas_call(
        body,
        out_shape=list(outs),
        in_specs=[kinds[kind] for kind in specs] + [ANY] * n_after,
        out_specs=[VM] * len(outs),
        scratch_shapes=list(scratch),
        compiler_params=pltpu.CompilerParams(vmem_limit_bytes=megabytes * 2**20),
        cost_estimate=pl.CostEstimate(flops=int(us * 10**9), bytes_accessed=int(us * 10**6), transcendentals=0),
        name=name,
    )(*ins, *after)


def at(index, unit):
    return pl.ds(pl.multiple_of(index * unit, unit), unit)


def first_norm_kernel(tokens, gains, out):
    value = tokens[...].astype(f32)
    inverse = lax.rsqrt(jnp.mean(value * value, axis=-1, keepdims=True) + norm_eps)
    out[...] = to_dp_order(value * inverse * gains[0:1, :]).astype(bf16)


def line_kernel(step, where, p0, p1, p2, p3, out, forward):
    width = out.shape[2]
    for index, piece in enumerate((p0, p1, p2, p3)):
        rows = at(jnp.bitwise_xor(where[2], index), 64)
        for result, core in ((out, where[3]), (forward, 1 - where[3])):
            lanes = pl.ds(pl.multiple_of(core * step, TILE), width)
            result[:, rows, :] = piece[:, :, lanes]


def stack_kernel(first, second, out):
    out[0] = first[...]
    out[1] = second[...]


def join_all_kernel(p0, p1, p2, p3, p4, p5, first, second):
    for out, pieces in ((first, (p0, p1, p2)), (second, (p3, p4, p5))):
        begin = 0
        for piece in pieces:
            out[begin : begin + piece.shape[0]] = piece[...]
            begin += piece.shape[0]


def thirds(first, second):
    parts = []
    for value in (first, second):
        for _ in range(3):
            part = value.astype(bf16).astype(f32)
            parts.append(part)
            value = value - part
    parts += [jnp.zeros_like(first)] * 2
    return jnp.concatenate(parts, axis=0).astype(bf16)


def from_thirds(rows):
    value = rows.astype(f32)
    return [value[k : k + 1] + value[k + 1 : k + 2] + value[k + 2 : k + 3] for k in (0, 3)]


def eight(a, ax, y2, b, by, x2):
    return [
        lambda p: a[p],
        lambda p: ax[p],
        lambda p: y2[0, p],
        lambda p: y2[1, p],
        lambda p: b[p],
        lambda p: by[p],
        lambda p: x2[0, p],
        lambda p: x2[1, p],
    ]


def order_matrix():
    rows = lax.broadcasted_iota(jnp.int32, (BLOCK, BLOCK), 0)
    cols = lax.broadcasted_iota(jnp.int32, (BLOCK, BLOCK), 1)
    target = jnp.bitwise_and(rows, RANK - 1) * (BLOCK // RANK) + jnp.right_shift(rows, 4)
    return jnp.where(cols == target, 1.0, 0.0).astype(bf16)


def pick(indices, pieces):
    total = None
    first = 0
    for piece in pieces:
        rows = piece.shape[0]
        lanes = lax.broadcasted_iota(jnp.int32, (indices.shape[0], rows), 1) + first
        part = mm(jnp.where(lanes == indices, 1.0, 0.0).astype(bf16), piece[...])
        total = part if total is None else total + part
        first += rows
    return total


def adapters_kernel(even_at, odd_at, flat_at, *rest):
    pieces, (out, out_m, tiles) = rest[:-3], rest[-3:]
    order = order_matrix()
    even = mm(pick(even_at[...], pieces).astype(bf16), order)
    odd = mm(pick(odd_at[...], pieces).astype(bf16), order)
    for part in range(8):
        low, high = merge(tile(even, part), tile(odd, part))
        tiles[:, part, :] = low
        tiles[:, 8 + part, :] = high
    for index in range(out.shape[1] // TILE):
        out[:, index * TILE : (index + 1) * TILE] = tiles[index].astype(bf16)
    flat = pick(flat_at[...], pieces)
    for index in range(out_m.shape[1] // BLOCK):
        out_m[0:1, index * BLOCK : (index + 1) * BLOCK] = flat[index : index + 1, :]


def column_norm(weights, lowers, uppers):
    joined = weights.astype(f32) + dora_scale * mm_f(lowers, uppers)
    return jnp.sum(joined * joined, axis=0, keepdims=True)


def split_rows(where, part, send, keep, share):
    core = where[3]
    for line in range(N_Z):
        send[line * share : (line + 1) * share] = part[at(2 * line + 1 - core, share)].astype(bf16)
    for line in range(N_Z):
        keep[line * share : (line + 1) * share] = part[at(2 * line + core, share)]


def attention_kernel(spans, where, x, b0, b1, b2, b3, b4, b5, w_out, flat, mags, cos, sin, seg_row, seg_col, squares,
                     send, keep, mixed, qkv, probs, att, low_qkv, low_out, stats, part):
    blocks = eight(b0, b1, b2, b3, b4, b5)
    width = CHUNK
    rows = x.shape[0]
    la = [spans[("A", p)][0] for p in range(3)]
    lb = [spans[("B", p)][0] for p in range(3)]
    allowed = seg_col[...] == seg_row[...]
    t_index = lax.broadcasted_iota(jnp.int32, (rows, rows), 0)
    s_index = lax.broadcasted_iota(jnp.int32, (rows, rows), 1)
    allowed = jnp.logical_and(allowed, s_index <= t_index)
    for p in range(3):
        upper = flat[:, lb[p] : lb[p] + width]
        low = mm_t(x[...], flat[:, la[p] : la[p] + D])
        total = dora_scale * mm2(low, upper)
        square = jnp.zeros((1, width), f32)
        for index, block in enumerate(blocks):
            chunk = where[4 + index]
            weights = block(p)
            total += mm(x[:, at(chunk, CHUNK)], weights)
            lowers = flat[:, pl.ds(pl.multiple_of(la[p] + chunk * CHUNK, TILE), CHUNK)]
            square += column_norm(weights, lowers, upper)
        norm = jnp.sqrt(square + column_eps)
        magnitude = mags[:, pl.ds(pl.multiple_of(p * D + where[1] * width, TILE), width)]
        scale = magnitude / norm
        lanes = slice(p * width, (p + 1) * width)
        mixed[:, lanes] = total
        low_qkv[:, p * RANK : (p + 1) * RANK] = low
        stats[0:1, lanes] = scale
        stats[1:2, lanes] = norm
        stats[2:3, lanes] = magnitude
        value = total * scale
        for head in range(width // HEAD_DIM):
            one = value[:, head * HEAD_DIM : (head + 1) * HEAD_DIM]
            if p < 2:
                one = one * cos[...] + swap64(one) * sin[...]
            begin = p * width + head * HEAD_DIM
            qkv[:, begin : begin + HEAD_DIM] = one.astype(bf16)
    for head in range(width // HEAD_DIM):
        lanes = slice(head * HEAD_DIM, (head + 1) * HEAD_DIM)
        query = qkv[:, lanes]
        keys = qkv[:, width + head * HEAD_DIM : width + (head + 1) * HEAD_DIM]
        value = qkv[:, 2 * width + head * HEAD_DIM : 2 * width + (head + 1) * HEAD_DIM]
        scores = mm_t(query, keys) * HEAD_DIM ** (-0.5)
        scores = jnp.where(allowed, scores, -1e30)
        expd = jnp.exp(scores - jnp.max(scores, axis=-1, keepdims=True))
        weights = expd / jnp.sum(expd, axis=-1, keepdims=True)
        probs[head] = weights
        att[:, lanes] = mm(weights.astype(bf16), value).astype(bf16)
    a_out, b_out = spans[("A", 3)][0], spans[("B", 3)][0]
    low = mm_t(att[...], flat[:, a_out : a_out + width])
    low_out[...] = low
    part[...] = mm(att[...], w_out[...]) + dora_scale * mm2(low, flat[:, b_out : b_out + D])
    split_rows(where, part, send, keep, keep.shape[0] // N_Z)
    send[keep.shape[0] :] = thirds(squares[0:1], squares[1:2])


def pair_kernel(where, keep, received, p1, p2, p3, own):
    share = own.shape[0]

    def line(index):
        rows = at(index, share)
        return keep[rows] + received[rows].astype(f32)

    own[...] = line(where[2])
    for step, piece in ((1, p1), (2, p2), (3, p3)):
        piece[...] = line(jnp.bitwise_xor(where[2], step)).astype(bf16)


def pair_more_kernel(where, keep, received, squares, p1, p2, p3, own, more):
    share = own.shape[0]

    def line(index):
        rows = at(index, share)
        return keep[rows] + received[rows].astype(f32)

    own[...] = line(where[2])
    first, second = from_thirds(received[keep.shape[0] :])
    first, second = first + squares[0:1], second + squares[1:2]
    more[0:1], more[1:2] = first, second
    rows = thirds(first, second)
    for step, piece in ((1, p1), (2, p2), (3, p3)):
        piece[0:share] = line(jnp.bitwise_xor(where[2], step)).astype(bf16)
        piece[share:] = rows


def total_of(own, r1, r2, r3):
    return own[...] + r1[...].astype(f32) + r2[...].astype(f32) + r3[...].astype(f32)


def second_norm_kernel(own, more, r1, r2, r3, tokens, gains, mags, x_two, mixed, out, scale_o, norm_o, scale_d, norm_d):
    share = own.shape[0]
    total = own[...]
    squares = [more[0:1], more[1:2]]
    for piece in (r1, r2, r3):
        total = total + piece[0:share].astype(f32)
        for row, value in enumerate(from_thirds(piece[share:])):
            squares[row] = squares[row] + value
    for square, begin, scale, norm in (
        (squares[0], 3 * D, scale_o, norm_o),
        (squares[1], 4 * D + 2 * FF, scale_d, norm_d),
    ):
        value = jnp.sqrt(square + column_eps)
        norm[...] = value
        scale[...] = mags[:, begin : begin + D] / value
    mixed[...] = total
    value = tokens[...].astype(f32) + total * scale_o[...]
    x_two[...] = value
    inverse = lax.rsqrt(jnp.mean(value * value, axis=-1, keepdims=True) + norm_eps)
    out[...] = to_dp_order(value * inverse * gains[1:2, :]).astype(bf16)


def join_rows(where, pieces, out):
    share = out.shape[0] // N_MP
    for index, piece in enumerate(pieces):
        line = jnp.bitwise_xor(where[2], index % N_Z)
        core = where[3] if index < N_Z else 1 - where[3]
        out[at(2 * line + core, share)] = piece[0:share].astype(out.dtype)


def join_kernel(where, p0, p1, p2, p3, p4, p5, p6, p7, input_grad, layer_out):
    share = layer_out.shape[0] // N_MP
    pieces = (p0, p1, p2, p3, p4, p5, p6, p7)
    join_rows(where, pieces, input_grad)
    join_rows(where, [piece.at[share : 2 * share] for piece in pieces], layer_out)


def wide_squares(spans, where, blocks, chunks, flat):
    squares = []
    for p in range(2):
        a, b = spans[("A", 4 + p)][0], spans[("B", 4 + p)][0]
        square = jnp.zeros((1, WIDE), f32)
        for index, block in zip(chunks, blocks):
            begin = pl.multiple_of(a + where[4 + index] * CHUNK, TILE)
            square += column_norm(block(p), flat[:, pl.ds(begin, CHUNK)], flat[:, b : b + WIDE])
        squares.append(square)
    return jnp.concatenate(squares, axis=1)


def wide_first_kernel(spans, where, a, ax, b, by, flat, squares):
    blocks = eight(a, ax, None, b, by, None)
    squares[...] = wide_squares(spans, where, [blocks[k] for k in (0, 1, 4, 5)], (0, 1, 4, 5), flat)


def wide_norm_kernel(spans, where, y2, x2, flat, mags, squares, stats):
    blocks = eight(None, None, y2, None, None, x2)
    total = squares[...] + wide_squares(spans, where, [blocks[k] for k in (2, 3, 6, 7)], (2, 3, 6, 7), flat)
    for p in range(2):
        lanes = slice(p * WIDE, (p + 1) * WIDE)
        norm = jnp.sqrt(total[:, lanes] + column_eps)
        first = 4 * D + p * FF + where[2] * (2 * FF // N_MP) + where[3] * (WIDE - TILE)
        magnitude = mags[:, pl.ds(pl.multiple_of(first, TILE), WIDE)]
        stats[0:1, lanes] = magnitude / norm
        stats[1:2, lanes] = norm
        stats[2:3, lanes] = magnitude


def row_norm_kernel(spans, w_out, w_down, flat, squares):
    for row, (p, weights) in enumerate(((3, w_out[...]), (6, w_down[...]))):
        a, size = spans[("A", p)]
        b = spans[("B", p)][0]
        squares[row : row + 1, :] = column_norm(weights, flat[:, a : a + size], flat[:, b : b + D])


def down_back_kernel(spans, where, cotangent, scale, w_down, flat, d_act, grad_b, through, padded):
    a, size = spans[("A", 6)]
    b = spans[("B", 6)][0]
    grad = (cotangent[...].astype(f32) * scale[...]).astype(bf16)
    grad_b[...] = grad
    low = dora_scale * mm_t(grad, flat[:, b : b + D])
    through[...] = low
    padded[...] = jnp.zeros_like(padded)
    padded[:, 0:size] = mm_t(grad, w_down[...]) + mm2(low, flat[:, a : a + size])
    value = padded[...]
    d_act[...] = jnp.where(where[3] == 0, value, pltpu.roll(value, FILL, 1))


def middle_kernel(spans, where, p0, p1, p2, p3, p4, p5, p6, p7, b0, b1, b2, b3, b4, b5, d_act, flat, stats,
                  send, keep, x, act, grads, throughs, lows, dots, part, mixed):
    blocks = eight(b0, b1, b2, b3, b4, b5)
    join_rows(where, (p0, p1, p2, p3, p4, p5, p6, p7), x)
    for p in range(2):
        a, b = spans[("A", 4 + p)][0], spans[("B", 4 + p)][0]
        low = mm_t(x[...], flat[:, a : a + D])
        lows[:, p * RANK : (p + 1) * RANK] = low
        total = dora_scale * mm2(low, flat[:, b : b + WIDE])
        for index, block in enumerate(blocks):
            total += mm(x[:, at(where[4 + index], CHUNK)], block(p))
        mixed[:, p * WIDE : (p + 1) * WIDE] = total
    lanes = lax.broadcasted_iota(jnp.int32, d_act.shape, 1) - where[3] * FILL
    used = jnp.logical_and(lanes >= 0, lanes < WIDE - FILL)
    gate = mixed[:, :WIDE] * stats[0:1, :WIDE]
    upward = mixed[:, WIDE:] * stats[0:1, WIDE:]
    sigmoid_gate = jax.nn.sigmoid(gate)
    silu = gate * sigmoid_gate
    act[...] = jnp.where(used, silu * upward, 0.0).astype(bf16)
    back = jnp.where(used, d_act[...], 0.0)
    grad = back * upward * sigmoid_gate * (1.0 + gate * (1.0 - sigmoid_gate))
    dots[0:1, :WIDE] = jnp.sum(grad * mixed[:, :WIDE], axis=0, keepdims=True)
    grads[:, :WIDE] = (grad * stats[0:1, :WIDE]).astype(bf16)
    grad = back * silu
    dots[0:1, WIDE:] = jnp.sum(grad * mixed[:, WIDE:], axis=0, keepdims=True)
    grads[:, WIDE:] = (grad * stats[0:1, WIDE:]).astype(bf16)
    through = []
    for p in range(2):
        b = spans[("B", 4 + p)][0]
        low = dora_scale * mm_t(grads[:, p * WIDE : (p + 1) * WIDE], flat[:, b : b + WIDE])
        throughs[:, p * RANK : (p + 1) * RANK] = low
        through.append(halves(low))
    for index, block in enumerate(blocks):
        chunk = where[4 + index]
        total = None
        for p in range(2):
            a = spans[("A", 4 + p)][0]
            lowers = flat[:, pl.ds(pl.multiple_of(a + chunk * CHUNK, TILE), CHUNK)]
            one = mm_t(grads[:, p * WIDE : (p + 1) * WIDE], block(p))
            one += mm(through[p][0], lowers) + mm(through[p][1], lowers)
            total = one if total is None else total + one
        part[:, at(chunk, CHUNK)] = total
    split_rows(where, part, send, keep, send.shape[0] // N_Z)


def down_kernel(spans, where, act, w_down, flat, cotangent, send, keep, low_out, dots, part, local):
    a, size = spans[("A", 6)]
    b = spans[("B", 6)][0]
    value = act[...].astype(f32)
    value = jnp.where(where[3] == 0, value, pltpu.roll(value, WIDE - FILL, 1))
    local[...] = value.astype(bf16)
    inputs = local[:, 0:size]
    low = mm_t(inputs, flat[:, a : a + size])
    low_out[...] = low
    part[...] = mm(inputs, w_down[...]) + dora_scale * mm2(low, flat[:, b : b + D])
    split_rows(where, part, send, keep, send.shape[0] // N_Z)
    dots[...] = jnp.sum(cotangent[...].astype(f32) * part[...], axis=0, keepdims=True)


def norm_back(value, grad, gain):
    inverse = lax.rsqrt(jnp.mean(value * value, axis=-1, keepdims=True) + norm_eps)
    scaled = grad * gain
    inner = jnp.mean(scaled * value, axis=-1, keepdims=True)
    return inverse * (scaled - value * inverse * inverse * inner)


def second_back_kernel(own, r1, r2, r3, x_two, mixed, cotangent, gains, scale, dots_d, grad_two, grad_b, dots):
    total = to_mp_order(total_of(own, r1, r2, r3))
    grad = cotangent[...].astype(f32) + norm_back(x_two[...], total, gains[1:2, :])
    grad_two[...] = grad
    grad_b[0 : grad.shape[0]] = (grad * scale[...]).astype(bf16)
    own = jnp.sum(grad * mixed[...], axis=0, keepdims=True)
    dots[...] = own
    grad_b[grad.shape[0] :] = thirds(own, dots_d[...])


def last_rows_kernel(own, r1, r2, r3, tokens, grad_two, gains, own_d, d1, d2, d3, x_two, scale, out):
    share = own.shape[0]
    total = to_mp_order(total_of(own, r1, r2, r3))
    value = tokens[...].astype(f32)
    out[0:share] = (grad_two[...] + norm_back(value, total, gains[0:1, :])).astype(bf16)
    out[share:] = (x_two[...] + total_of(own_d, d1, d2, d3) * scale[...]).astype(bf16)


def attention_back_kernel(spans, where, p0, p1, p2, p3, p4, p5, p6, p7, b0, b1, b2, b3, b4, b5, w_out, flat,
                          cos, sin, mixed, qkv, probs, stats,
                          send, keep, grad_out, grads, throughs, through_out, dots, dots_o, dots_d, part, incoming):
    blocks = eight(b0, b1, b2, b3, b4, b5)
    width = CHUNK
    join_rows(where, (p0, p1, p2, p3, p4, p5, p6, p7), grad_out)
    sums = [jnp.zeros((1, D), f32)] * 2
    for piece in (p0, p1, p2, p3, p4, p5, p6, p7):
        for index, value in enumerate(from_thirds(piece[grad_out.shape[0] // N_MP :])):
            sums[index] = sums[index] + value
    dots_o[...], dots_d[...] = sums
    a, b = spans[("A", 3)][0], spans[("B", 3)][0]
    low = dora_scale * mm_t(grad_out[...], flat[:, b : b + D])
    through_out[...] = low
    grad_att = (mm_t(grad_out[...], w_out[...]) + mm2(low, flat[:, a : a + width])).astype(bf16)
    for head in range(width // HEAD_DIM):
        lanes = [slice(p * width + head * HEAD_DIM, p * width + (head + 1) * HEAD_DIM) for p in range(3)]
        query, keys, value = [qkv[:, one] for one in lanes]
        grad = grad_att[:, head * HEAD_DIM : (head + 1) * HEAD_DIM]
        weights = probs[head]
        grad_weights = mm_t(grad, value)
        incoming[:, lanes[2]] = mm_f(weights.astype(bf16), grad)
        centred = jnp.sum(weights * grad_weights, axis=-1, keepdims=True)
        grad_scores = (weights * (grad_weights - centred)).astype(bf16)
        grad_query = mm(grad_scores, keys) * HEAD_DIM ** (-0.5)
        grad_key = mm_f(grad_scores, query) * HEAD_DIM ** (-0.5)
        incoming[:, lanes[0]] = grad_query * cos[...] - swap64(grad_query) * sin[...]
        incoming[:, lanes[1]] = grad_key * cos[...] - swap64(grad_key) * sin[...]
    dots[...] = jnp.sum(incoming[...] * mixed[...], axis=0, keepdims=True)
    grads[...] = (incoming[...] * stats[0:1, :]).astype(bf16)
    through = []
    for p in range(3):
        b = spans[("B", p)][0]
        low = dora_scale * mm_t(grads[:, p * width : (p + 1) * width], flat[:, b : b + width])
        throughs[:, p * RANK : (p + 1) * RANK] = low
        through.append(halves(low))
    for index, block in enumerate(blocks):
        chunk = where[4 + index]
        total = None
        for p in range(3):
            a = spans[("A", p)][0]
            lowers = flat[:, pl.ds(pl.multiple_of(a + chunk * CHUNK, TILE), CHUNK)]
            one = mm_t(grads[:, p * width : (p + 1) * width], block(p))
            one += mm(through[p][0], lowers) + mm(through[p][1], lowers)
            total = one if total is None else total + one
        part[:, at(chunk, CHUNK)] = total
    split_rows(where, part, send, keep, send.shape[0] // N_Z)


def to_blocks(value, tiles, out, begin):
    pairs = value.shape[1] // TILE
    for index in range(pairs):
        tiles[index] = tile(value, index)
    for part in range(8):
        even, odd = merge(tiles[0:pairs, part, :], tiles[0:pairs, 8 + part, :])
        lanes = slice(part * TILE, (part + 1) * TILE)
        out[begin : begin + pairs, lanes] = even
        out[begin + pairs : begin + 2 * pairs, lanes] = odd


def column_grads_kernel(spans, projections, width, where, x, b0, b1, b2, b3, b4, b5, flat, stats, grads, throughs,
                        lows, dots, out_a, out_b, out_m, tiles, whole):
    blocks = eight(b0, b1, b2, b3, b4, b5)
    for position, p in enumerate(projections):
        a, b = spans[("A", p)][0], spans[("B", p)][0]
        lanes = slice(position * width, (position + 1) * width)
        ranks = slice(position * RANK, (position + 1) * RANK)
        upper = flat[:, b : b + width]
        norm = stats[1:2, lanes]
        inverse = 1.0 / norm
        e = dots[0:1, lanes]
        out_m[0:1, lanes] = e * inverse
        ratio = -e * stats[2:3, lanes] * inverse * inverse * inverse
        scaled = halves(dora_scale * upper.astype(f32) * ratio)
        through = halves(throughs[:, ranks])
        square = dora_scale * (mm_t(scaled[0], upper) + mm_t(scaled[1], upper))
        lower = flat[:, a : a + D]
        whole[...] = mm2(square, lower) + mm_f(through[0], x[...]) + mm_f(through[1], x[...])
        crossed = dora_scale * mm2(mm_t(lower, lower), upper)
        for index, block in enumerate(blocks):
            chunk = where[4 + index]
            weights = block(position)
            whole[:, at(chunk, CHUNK)] += mm_t(scaled[0], weights) + mm_t(scaled[1], weights)
            crossed += mm(flat[:, pl.ds(pl.multiple_of(a + chunk * CHUNK, TILE), CHUNK)], weights)
        to_blocks(whole[...], tiles, out_a, position * D * RANK // BLOCK)
        upper_grad = dora_scale * (mm2_f(lows[:, ranks], grads[:, lanes]) + crossed * ratio)
        to_blocks(upper_grad, tiles, out_b, position * width * RANK // BLOCK)


def row_grads_kernel(spans, p, where, x, weights_ref, flat, scale_row, norm_row, mag_row, grads, through_in, low, dots,
                     out_a, out_b, tiles, local):
    a, size = spans[("A", p)]
    b = spans[("B", p)][0]
    weights = weights_ref[...]
    inputs = x[...]
    if p == 6:
        value = inputs.astype(f32)
        value = jnp.where(where[3] == 0, value, pltpu.roll(value, WIDE - FILL, 1))
        local[...] = value.astype(bf16)
        inputs = local[:, 0:size]
    lower = flat[:, a : a + size]
    upper = flat[:, b : b + D]
    inverse = 1.0 / norm_row[...]
    ratio = -dots[...] * mag_row[...] * inverse * inverse * inverse
    scaled = halves(dora_scale * upper.astype(f32) * ratio)
    square = dora_scale * (mm_t(scaled[0], upper) + mm_t(scaled[1], upper))
    grad = mm2(square, lower) + mm2_f(through_in[...], inputs)
    grad += mm_t(scaled[0], weights) + mm_t(scaled[1], weights)
    if size % TILE:
        grad = jnp.concatenate([grad, jnp.zeros((RANK, TILE - size % TILE), f32)], axis=1)
    to_blocks(grad, tiles, out_a, 0)
    crossed = mm(lower, weights) + dora_scale * mm2(mm_t(lower, lower), upper)
    to_blocks(dora_scale * (mm2_f(low[...], grads[...]) + crossed * ratio), tiles, out_b, 0)


def pack_kernel(where, a_f, a_a, b_d, b_o, m_f, m_a, dots_o, norm_o, dots_d, norm_d, give, keep, rows, flat):
    begin = 0
    for array in (a_f, a_a, b_d, b_o):
        rows[begin : begin + array.shape[0]] = array[...]
        begin += array.shape[0]
    flat[...] = jnp.zeros_like(flat)
    for p in range(3):
        lanes = pl.ds(pl.multiple_of(p * D + where[1] * CHUNK, TILE), CHUNK)
        flat[:, lanes] = m_a[:, p * CHUNK : (p + 1) * CHUNK]
    flat[:, 3 * D : 4 * D] = dots_o[...] / norm_o[...]
    for p in range(2):
        first = 4 * D + p * FF + where[2] * (2 * FF // N_MP) + where[3] * (WIDE - TILE)
        flat[:, pl.ds(pl.multiple_of(first, TILE), WIDE)] = m_f[:, p * WIDE : (p + 1) * WIDE]
    flat[:, 4 * D + 2 * FF :] = dots_d[...] / norm_d[...]
    rows[begin:] = jnp.zeros((rows.shape[0] - begin, BLOCK), f32)
    for index in range(flat.shape[1] // BLOCK):
        rows[begin + index : begin + index + 1] = flat[:, index * BLOCK : (index + 1) * BLOCK]
    unit = rows.shape[0] // N_MP
    for line in range(N_Z):
        give[line * unit : (line + 1) * unit] = rows[at(2 * line + 1 - where[3], unit)].astype(bf16)
        keep[line * unit : (line + 1) * unit] = rows[at(2 * line + where[3], unit)]


def local_kernel(where, own, r1, r2, r3, b_f, b_a, a_d, a_o, mine, p1, p2, p3, rows):
    begin = own.shape[0]
    rows[0:begin] = total_of(own, r1, r2, r3)
    for array in (b_f, b_a, a_d, a_o):
        rows[begin : begin + array.shape[0]] = array[...]
        begin += array.shape[0]
    rows[begin:] = jnp.zeros((rows.shape[0] - begin, BLOCK), f32)
    part = mine.shape[0]
    mine[...] = rows[at(where[0], part)]
    for step, piece in ((1, p1), (2, p2), (3, p3)):
        piece[...] = rows[at(jnp.bitwise_xor(where[0], step), part)].astype(bf16)


def last_sum_kernel(own, r1, r2, r3, out):
    out[...] = total_of(own, r1, r2, r3).astype(bf16)


def update_kernel(index, mine, s0, s1, s2, s3, s4, s5, s6, s7, master, first, second, new_master, new_first, new_second):
    picked = pick(index[...], (s0, s1, s2, s3, s4, s5, s6, s7)).astype(bf16)
    grad = jnp.where(mine[...] >= COUNT_FLAT, picked.astype(f32), mm_t(picked, order_matrix()))
    grad = jnp.where(mine[...] >= 0, grad, 0.0)
    rates = jnp.where(mine[...] < COUNT_FLAT, rate_upper, rate_magnitude)
    rates = jnp.where(mine[...] < COUNT_LOWER, rate_lower, rates)
    rates = jnp.where(mine[...] < 0, 0.0, rates)
    weight = master[...]
    first_new = beta_one * first[...] + (1.0 - beta_one) * grad
    second_new = beta_two * second[...] + (1.0 - beta_two) * grad * grad
    first_hat = first_new / (1.0 - beta_one**STEP)
    second_hat = second_new / (1.0 - beta_two**STEP)
    new_master[...] = weight - rates * (
        first_hat / (jnp.sqrt(second_hat) + adam_eps) + weight_decay * weight
    )
    new_first[...] = first_new
    new_second[...] = second_new


COUNT_LOWER = RANK * (6 * D + FF) // BLOCK
COUNT_FLAT = COUNT_LOWER + RANK * (5 * D + 2 * FF) // BLOCK


def block_starts():
    starts = {}
    total = 0
    for kind, side in (("A", 0), ("B", 1)):
        for index, sizes in enumerate(proj_dims()):
            starts[(kind, index)] = total
            total += sizes[side] * RANK // BLOCK
    return starts


def fast_body(
    tokens,
    cotangent,
    norm_gains,
    w_attn,
    w_in,
    w_down,
    segments,
    owners,
    master,
    first_moment,
    second_moment,
):
    rows = tokens.shape[0]
    mi = lax.axis_index("mp")
    di = lax.axis_index("dp")
    core = mi % 2
    zi = mi // 2
    share = rows // N_MP
    capacity = master.shape[0]
    n_blocks = owners.shape[0]
    width = D // N_MP
    starts = block_starts()

    def mp_swap(values, step):
        return lax.ppermute(values, "mp", [(i, i ^ step) for i in range(N_MP)])

    def dp_swap(values, step):
        return lax.ppermute(values, "dp", [(i, i ^ step) for i in range(N_DP)])

    order = [(0, 0), (1, 0), (2, 0), (3, 0), (0, 1), (2, 1), (1, 1), (3, 1)]
    chunks = [(di ^ t) * 2 + (core ^ h) for t, h in order]
    where = jnp.stack([di, mi, zi, core] + chunks).astype(jnp.int32)

    def stack(first, second, after=()):
        shape = (2,) + first.shape
        return run(
            stack_kernel, [first, second], "hh", [shape_of(shape, bf16)], name="stack", after=after, us=0.6
        )[0]

    def plane_first(a, b):
        return a, dp_swap(a, 1), b, dp_swap(b, 2)

    def plane_second(a, ax, b, by, after=()):
        return [a, ax, dp_swap(stack(a, ax, after), 2), b, by, dp_swap(stack(b, by, after), 1)]

    def plane(a, b):
        return plane_second(*plane_first(a, b))

    sent = master.astype(bf16)
    line = [sent] + [mp_swap(sent, 2 * step) for step in range(1, N_Z)]
    first_b = plane_first(jnp.concatenate(line[:2]), jnp.concatenate(line[2:]))
    owners, segments, w_late, tokens, line_end = lax.optimization_barrier(
        (owners, segments, w_attn, tokens, first_b[2])
    )
    first_b = first_b[:2] + (line_end,) + first_b[3:]
    sheet = plane_second(*first_b)
    sheet = [one.reshape(-1, BLOCK) for one in sheet]
    features = run(
        first_norm_kernel,
        [tokens, norm_gains],
        "hh",
        [shape_of((rows, D), bf16)],
        name="first_norm",
        megabytes=6,
        us=1.2,
        after=[first_b[2]],
    )[0]
    def cut(weights, count, chip):
        pieces = []
        for index in range(N_Z):
            piece = lax.dynamic_slice(weights, (0, di * 64, (zi ^ index) * chip), (count, 64, chip))
            pieces.append(mp_swap(piece, 2 * index) if index else piece)
        return pieces

    def columns_of(pieces, size, step, name, after=()):
        count = pieces[0].shape[0]
        a, forward = run(
            functools.partial(line_kernel, step),
            [where] + pieces,
            "shhhh",
            [shape_of((count, CHUNK, size), bf16)] * 2,
            name=name,
            after=after,
        )
        return plane_first(a, mp_swap(forward, 1))

    first_a = columns_of(cut(w_attn, 3, 2 * width), width, width, "line_a", [features])
    blocks_a = plane_second(*first_a)
    sheet = run(
        join_all_kernel,
        sheet,
        "h" * 6,
        [shape_of((8 * capacity, BLOCK), bf16)] * 2,
        name="adapter_rows",
        after=[first_a[0]],
        us=0.1,
    )
    stacked = list(sheet) + [mp_swap(one, 1) for one in sheet]
    w_in_late, own_a = lax.optimization_barrier((w_in, first_a[0]))
    pieces_f = cut(w_in_late, 2, 2 * FF // N_MP)
    w_out = w_late[3]

    ranks = slot_positions(owners, 0)
    owner_d, owner_m = owners // N_MP, owners % N_MP
    piece_at = (owner_d ^ di) * N_Z + ((owner_m // 2) ^ zi)
    listed = np.array([0, 1, 8, 9, 2, 3, 12, 13, 4, 5, 10, 11, 6, 7, 14, 15], np.int32)
    piece_at = jnp.sum(jnp.where(piece_at[:, None] == np.arange(16), listed, 0), axis=1)
    slot = (((owner_m % 2) ^ core) * 16 + piece_at) * capacity + ranks
    wanted = []
    spans = {}

    def want(name, blocks, size):
        spans[name] = (sum(w.shape[0] for w in wanted) * 64, size)
        wanted.append(blocks)

    by_dp = np.array(
        [(2 * z + c) * 4 + d for d in range(N_DP) for c in range(2) for z in range(N_Z)], np.int32
    )
    all_blocks = np.arange(D * RANK // BLOCK, dtype=np.int32)
    for index in (0, 1, 2, 4, 5):
        want(("A", index), starts[("A", index)] + by_dp, D)
        if index < 3:
            want(("B", index), starts[("B", index)] + mi * 4 + np.arange(4), width)
        else:
            first_block = starts[("B", index)] + zi * 22 + core * 10
            want(("B", index), first_block + np.arange(12), WIDE)
    want(("A", 3), starts[("A", 3)] + mi * 4 + np.arange(4), width)
    want(("B", 3), starts[("B", 3)] + all_blocks, D)
    want(("A", 6), starts[("A", 6)] + mi * 11 + np.minimum(np.arange(12), 10), FF // N_MP)
    want(("B", 6), starts[("B", 6)] + all_blocks, D)
    chosen = jnp.take(slot, jnp.concatenate([jnp.asarray(w, jnp.int32) for w in wanted]))
    n_pairs = chosen.shape[0] // 2
    pairs = chosen.reshape(n_pairs, 2)
    flat, mags = run(
        adapters_kernel,
        [pairs[:, :1], pairs[:, 1:], slot[COUNT_FLAT:, None]] + stacked,
        "vvv" + "h" * len(stacked),
        [shape_of((RANK, n_pairs * TILE), bf16), shape_of((1, (n_blocks - COUNT_FLAT) * BLOCK), f32)],
        [pltpu.VMEM((n_pairs, RANK, TILE), f32)],
        name="adapters", megabytes=13, us=0.3,
    )

    def bind(kernel, *args):
        return functools.partial(kernel, spans, *args)

    def column_grads(projections, size, x, blocks, flat, stats, grads, throughs, lows, dots, after):
        count = len(projections)
        return run(
            bind(column_grads_kernel, projections, size),
            [where, x] + blocks + [flat, stats, grads, throughs, lows, dots],
            "s" + "h" * 13,
            [
                shape_of((count * D * RANK // BLOCK, BLOCK), f32),
                shape_of((count * size * RANK // BLOCK, BLOCK), f32),
                shape_of((1, count * size), f32),
            ],
            [pltpu.VMEM((D // TILE, RANK, TILE), f32), pltpu.VMEM((RANK, D), f32)],
            name="column_grads", megabytes=9, us=1,
            after=after,
        )

    def row_grads(p, x, weights, flat, scale, norm, mag, grads, through, low, dots, after):
        size = spans[("A", p)][1]
        return run(
            bind(row_grads_kernel, p),
            [where, x, weights, flat, scale, norm, mag, grads, through, low, dots],
            "s" + "h" * 10,
            [
                shape_of((-(-size // TILE) * 2, BLOCK), f32),
                shape_of((D * RANK // BLOCK, BLOCK), f32),
            ],
            [pltpu.VMEM((D // TILE, RANK, TILE), f32), pltpu.VMEM((rows, WIDE), bf16)],
            name="row_grads", megabytes=6, us=0.1,
            after=after,
        )

    row = segments[0]
    cosine, sine = rotary_tables(segment_positions(row))
    cosine, sine = cosine[:, 0], sine[:, 0]
    cos_full = jnp.concatenate([cosine, cosine], axis=-1)
    sin_full = jnp.concatenate([-sine, sine], axis=-1)
    tokens_here = lax.dynamic_slice_in_dim(tokens, mi * share, share, 0)
    cotangent_here = lax.dynamic_slice_in_dim(cotangent, mi * share, share, 0)
    half_rows = [shape_of((rows // 2, D), bf16), shape_of((rows // 2, D), f32)]

    def finish_rows(send, keep, after):
        received = mp_swap(send, 1)
        p1, p2, p3, own = run(
            pair_kernel,
            [where, keep, received],
            "shh",
            [shape_of((share, D), bf16)] * 3 + [shape_of((share, D), f32)],
            name="pair_sums", megabytes=4, us=1.2,
            after=after,
        )
        return [own, mp_swap(p1, 2), mp_swap(p2, 4), mp_swap(p3, 6)]

    def gather_rows(value):
        mine = [value] + [mp_swap(value, 2 * step) for step in range(1, N_Z)]
        return mine + [mp_swap(one, 1) for one in mine]

    squares = run(
        bind(row_norm_kernel),
        [w_out, w_down, flat],
        "hhh",
        [shape_of((2, D), f32)],
        name="row_norms",
        us=0.1,
    )[0]
    n_heads = width // HEAD_DIM
    send, keep, mixed_a, qkv, probs, att, low_a, low_o, stats_a = run(
        bind(attention_kernel),
        [where, features] + blocks_a + [w_out, flat, mags, cos_full, sin_full, segments, row[:, None], squares],
        "s" + "h" * 15,
        [shape_of((rows // 2 + 8, D), bf16), half_rows[1]]
        + [
            shape_of((rows, 3 * width), f32),
            shape_of((rows, 3 * width), bf16),
            shape_of((n_heads, rows, rows), f32),
            shape_of((rows, width), bf16),
            shape_of((rows, 3 * RANK), f32),
            shape_of((rows, RANK), f32),
            shape_of((8, 3 * width), f32),
        ],
        [pltpu.VMEM((rows, D), f32)],
        name="attention",
        megabytes=13,
        us=10,
    )

    p1, p2, p3, own_o, more_o = run(
        pair_more_kernel,
        [where, keep, mp_swap(send, 1), squares],
        "shhh",
        [shape_of((share + 8, D), bf16)] * 3 + [shape_of((share, D), f32), shape_of((2, D), f32)],
        name="pair_sums",
        us=1.2,
    )
    sums_o = [mp_swap(p1, 2), mp_swap(p2, 4), mp_swap(p3, 6)]
    first_f = columns_of(pieces_f, WIDE, WIDE - TILE, "line_f")
    blocks_f = plane_second(*first_f, after=sums_o)
    row_of = shape_of((1, D), f32)
    x_two, mixed_o, features_two, scale_o, norm_o, scale_d, norm_d = run(
        second_norm_kernel,
        [own_o, more_o] + sums_o + [tokens_here, norm_gains, mags],
        "h" * 8,
        [shape_of((share, D), f32)] * 2 + [shape_of((share, D), bf16)] + [row_of] * 4,
        name="second_norm",
        us=0.5,
    )
    mag_o = mags[:, 3 * D : 4 * D]
    mag_d = mags[:, 4 * D + 2 * FF :]
    pieces = gather_rows(features_two)
    squares_f = run(
        bind(wide_first_kernel),
        [where] + [blocks_f[k] for k in (0, 1, 3, 4)] + [flat],
        "s" + "h" * 5,
        [shape_of((1, 2 * WIDE), f32)],
        name="wide_squares", megabytes=8, us=3,
        after=[pieces[1]],
    )[0]
    d_act, grad_d, through_d = run(
        bind(down_back_kernel),
        [where, cotangent, scale_d, w_down, flat],
        "shhhh",
        [shape_of((rows, WIDE), f32), shape_of((rows, D), bf16), shape_of((rows, RANK), f32)],
        [pltpu.VMEM((rows, WIDE), f32)],
        name="down_back", megabytes=7, us=3.5,
        after=[squares_f],
    )
    stats_f = run(
        bind(wide_norm_kernel),
        [where] + [blocks_f[k] for k in (2, 5)] + [flat, mags, squares_f],
        "s" + "h" * 5,
        [shape_of((8, 2 * WIDE), f32)],
        name="wide_norms", megabytes=8, us=3,
        after=[through_d],
    )[0]
    send, keep, x_f, act, grads_f, through_f, low_f, dots_f = run(
        bind(middle_kernel),
        [where] + pieces + blocks_f + [d_act, flat, stats_f],
        "s" + "h" * 17,
        half_rows
        + [
            shape_of((rows, D), bf16),
            shape_of((rows, WIDE), bf16),
            shape_of((rows, 2 * WIDE), bf16),
            shape_of((rows, 2 * RANK), f32),
            shape_of((rows, 2 * RANK), f32),
            shape_of((1, 2 * WIDE), f32),
        ],
        [pltpu.VMEM((rows, D), f32), pltpu.VMEM((rows, 2 * WIDE), f32)],
        name="feed_forward", megabytes=22, us=14,
    )
    send_d, keep_d, low_d, dots_d = run(
        bind(down_kernel),
        [where, act, w_down, flat, cotangent],
        "shhhh",
        half_rows + [shape_of((rows, RANK), f32), shape_of((1, D), f32)],
        [pltpu.VMEM((rows, D), f32), pltpu.VMEM((rows, WIDE), bf16)],
        name="down", megabytes=9, us=3.5,
    )
    sums = finish_rows(send, keep, [low_d])
    a_f, b_f, m_f = column_grads(
        (4, 5), WIDE, x_f, blocks_f, flat, stats_f, grads_f, through_f, low_f, dots_f, [sums[1]]
    )
    grad_two, grad_o_piece, dots_o = run(
        second_back_kernel,
        sums + [x_two, mixed_o, cotangent_here, norm_gains, scale_o, dots_d],
        "h" * 10,
        [shape_of((share, D), f32), shape_of((share + 8, D), bf16), row_of],
        name="second_norm_back", megabytes=3, us=0.5,
        after=[m_f],
    )
    pieces_o = gather_rows(grad_o_piece)
    sums_d = finish_rows(send_d, keep_d, [pieces_o[0], pieces_o[7]])
    send, keep, grad_o, grads_a, through_a, through_o, dots_a, dots_all_o, dots_all_d = run(
        bind(attention_back_kernel),
        [where] + pieces_o + blocks_a + [w_out, flat, cos_full, sin_full, mixed_a, qkv, probs, stats_a],
        "s" + "h" * 22,
        half_rows
        + [
            shape_of((rows, D), bf16),
            shape_of((rows, 3 * width), bf16),
            shape_of((rows, 3 * RANK), f32),
            shape_of((rows, RANK), f32),
            shape_of((1, 3 * width), f32),
            row_of,
            row_of,
        ],
        [pltpu.VMEM((rows, D), f32), pltpu.VMEM((rows, 3 * width), f32)],
        name="attention_back",
        megabytes=10,
        us=0.1,
        after=[sums_d[0]],
    )
    a_o, b_o = row_grads(
        3, att, w_out, flat, scale_o, norm_o, mag_o, grad_o, through_o, low_o, dots_all_o, []
    )
    a_a, b_a, m_a = column_grads(
        (0, 1, 2), width, features, blocks_a, flat, stats_a, grads_a, through_a, low_a, dots_a, [a_o]
    )
    a_d, b_d = row_grads(
        6, act, w_down, flat, scale_d, norm_d, mag_d, grad_d, through_d, low_d, dots_all_d, [m_a]
    )
    unit, part = 32, 24
    give, kept = run(
        pack_kernel,
        [where, a_f, a_a, b_d, b_o, m_f, m_a, dots_o, norm_o, dots_d, norm_d],
        "s" + "h" * 10,
        [shape_of((N_Z * unit, BLOCK), bf16), shape_of((N_Z * unit, BLOCK), f32)],
        [pltpu.VMEM((N_MP * unit, BLOCK), f32), pltpu.VMEM((1, (n_blocks - COUNT_FLAT) * BLOCK), f32)],
        name="pack",
    )
    p1, p2, p3, own = run(
        pair_kernel,
        [where, kept, mp_swap(give, 1)],
        "shh",
        [shape_of((unit, BLOCK), bf16)] * 3 + [shape_of((unit, BLOCK), f32)],
        name="pack_sums",
        us=0.1,
    )
    sums = finish_rows(send, keep, [give])
    own, p1, p2, p3 = run(
        local_kernel,
        [where, own, mp_swap(p1, 2), mp_swap(p2, 4), mp_swap(p3, 6), b_f, b_a, a_d, a_o],
        "s" + "h" * 8,
        [shape_of((part, BLOCK), f32)] + [shape_of((part, BLOCK), bf16)] * 3,
        [pltpu.VMEM((N_DP * part, BLOCK), f32)],
        name="local_sums",
        us=0.1,
    )
    own = run(
        last_sum_kernel,
        [own, dp_swap(p1, 1), dp_swap(p2, 2), dp_swap(p3, 3)],
        "hhhh",
        [shape_of((part, BLOCK), bf16)],
        name="last_sums",
        us=0.1,
    )[0]
    last_piece = run(
        last_rows_kernel,
        sums + [tokens_here, grad_two, norm_gains] + sums_d + [x_two, scale_d],
        "h" * 13,
        [shape_of((2 * share, D), bf16)],
        name="last_rows",
        us=0.5,
    )[0]
    lines = jnp.concatenate([own] + [mp_swap(own, 2 * step) for step in range(1, N_Z)])
    summed = [lines] + [dp_swap(lines, step) for step in range(1, N_DP)]
    summed = summed + [mp_swap(one, 1) for one in summed]

    second = mp_swap(last_piece, 4)
    pieces = [last_piece, mp_swap(last_piece, 2), second, mp_swap(second, 2)]
    pieces = pieces + [mp_swap(one, 1) for one in pieces]
    input_grad, layer_out = run(
        join_kernel,
        [where] + pieces,
        "s" + "h" * 8,
        [shape_of((rows, D), f32), shape_of((rows, D), bf16)],
        name="join_rows",
        megabytes=8,
        us=4,
    )

    table = np.zeros((n_blocks,), np.int32)

    def note(block, m, r):
        table[block] = ((r // part) * N_MP + m) * 64 + r % part

    def split_pairs(count, r):
        return r // 2 + (r % 2) * (count // 2)

    def blocks_of(names):
        def listing(count, m):
            each = count // len(names)
            for position, blocks in enumerate(names):
                for k, block in enumerate(blocks(m)):
                    if block is not None:
                        yield position * each + split_pairs(each, k), block

        return listing

    def lower_columns(p):
        return lambda m: [starts[("A", p)] + int(k) for k in by_dp]

    def upper_rows(p):
        return lambda m: [starts[("B", p)] + int(k) for k in all_blocks]

    def lower_rows(p, per):
        return lambda m: [starts[("A", p)] + m * per + k for k in range(per)]

    def upper_columns(p):
        if p < 3:
            return lambda m: [starts[("B", p)] + m * 4 + k for k in range(4)]
        return lambda m: [
            starts[("B", p)] + (m // 2) * 22 + (m % 2) * 10 + k
            if (k < 11 if m % 2 == 0 else k >= 1)
            else None
            for k in range(12)
        ]

    begin = 0
    for listing, count in (
        (blocks_of([lower_columns(4), lower_columns(5)]), a_f.shape[0]),
        (blocks_of([lower_columns(p) for p in range(3)]), a_a.shape[0]),
        (blocks_of([upper_rows(6)]), b_d.shape[0]),
        (blocks_of([upper_rows(3)]), b_o.shape[0]),
        (lambda count, m: [(r, COUNT_FLAT + r) for r in range(count)], n_blocks - COUNT_FLAT),
    ):
        for r, block in listing(count, None):
            note(block, (begin + r) // unit, (begin + r) % unit)
        begin += count
    begin = unit
    for listing, count in (
        (blocks_of([upper_columns(4), upper_columns(5)]), b_f.shape[0]),
        (blocks_of([upper_columns(p) for p in range(3)]), b_a.shape[0]),
        (blocks_of([lower_rows(6, 11)]), a_d.shape[0]),
        (blocks_of([lower_rows(3, 4)]), a_o.shape[0]),
    ):
        for m in range(N_MP):
            for r, block in listing(count, m):
                note(block, m, begin + r)
        begin += count
    me = di * N_MP + mi
    hits = (owners * capacity + ranks)[None, :] == me * capacity + jnp.arange(capacity)[:, None]
    mine = jnp.sum(jnp.where(hits, jnp.arange(n_blocks)[None, :] + 1, 0), axis=1) - 1
    code = jnp.sum(jnp.where(hits, jnp.asarray(table)[None, :], 0), axis=1)
    device, inner = code // 64, code % 64
    d_from, m_from = device // N_MP, device % N_MP
    list_at = (((m_from % 2) ^ core) * N_DP + (d_from ^ di)) * N_Z + ((m_from // 2) ^ zi)
    index = list_at * part + inner
    new_master, new_first, new_second = run(
        update_kernel,
        [index[:, None], mine[:, None]] + summed + [master, first_moment, second_moment],
        "vv" + "h" * 11,
        [shape_of(master.shape, f32)] * 3,
        name="update", megabytes=4, us=2,
    )
    return (layer_out, input_grad, new_master, new_first, new_second)


def solution(mesh):
    fast = mesh.shape["dp"] == 4 and mesh.shape["mp"] == 8
    return jax.shard_map(
        fast_body if fast else body,
        mesh=mesh,
        in_specs=(
            P("dp", None),
            P("dp", None),
            P(),
            P(None, "mp", None),
            P(None, "mp", None),
            P("mp", None),
            P("dp", None),
            P(),
            P(("dp", "mp"), None),
            P(("dp", "mp"), None),
            P(("dp", "mp"), None),
        ),
        out_specs=(
            P("dp", None),
            P("dp", None),
            P(("dp", "mp"), None),
            P(("dp", "mp"), None),
            P(("dp", "mp"), None),
        ),
        check_vma=False,
    )
```

```python
import functools

import jax
import jax.numpy as jnp
import numpy as np
from jax import lax
from jax.experimental import pallas as pl
from jax.experimental.pallas import tpu as pltpu
from jax.sharding import PartitionSpec as P

D = 2048
FF = 5632
HEADS = 16
HEAD_DIM = 128
RANK = 16
BLOCK = 1024
STEP = 5


dora_scale = 2.0
rope_base = 10000.0
norm_eps = 1e-05
column_eps = 1e-06
beta_one = 0.5
beta_two = 0.5
adam_eps = 1e-08
weight_decay = 0.01
rate_lower = 0.02
rate_upper = 0.1
rate_magnitude = 1.0
highest = lax.Precision.HIGHEST


def proj_dims():
    return [(D, D), (D, D), (D, D), (D, D), (D, FF), (D, FF), (FF, D)]


def unpack(flat):
    offset = 0
    lowers = []
    for inner, outer in proj_dims():
        lowers.append(flat[offset : offset + inner * RANK].reshape(inner, RANK))
        offset += inner * RANK
    uppers = []
    for inner, outer in proj_dims():
        uppers.append(flat[offset : offset + outer * RANK].reshape(outer, RANK))
        offset += outer * RANK
    magnitudes = []
    for inner, outer in proj_dims():
        magnitudes.append(flat[offset : offset + outer])
        offset += outer
    return (lowers, uppers, magnitudes)


def slot_positions(owners, capacity):
    order = jnp.arange(owners.shape[0], dtype=jnp.int32)
    same = (owners[:, None] == owners[None, :]) & (order[None, :] < order[:, None])
    ranks = jnp.sum(same.astype(jnp.int32), axis=1)
    return owners * capacity + ranks


def block_rates(block_ids):
    count_lower = RANK * (6 * D + FF) // BLOCK
    count_upper = RANK * (5 * D + 2 * FF) // BLOCK
    rates = jnp.where(block_ids < count_lower + count_upper, rate_upper, rate_magnitude)
    rates = jnp.where(block_ids < count_lower, rate_lower, rates)
    return jnp.where(block_ids < 0, 0.0, rates).astype(jnp.float32)


def adam_update(weight, grad, first, second, rates):
    first_new = beta_one * first + (1.0 - beta_one) * grad
    second_new = beta_two * second + (1.0 - beta_two) * grad * grad
    first_hat = first_new / (1.0 - beta_one**STEP)
    second_hat = second_new / (1.0 - beta_two**STEP)
    weight_new = weight - rates[:, None] * (
        first_hat / (jnp.sqrt(second_hat) + adam_eps) + weight_decay * weight
    )
    return (weight_new, first_new, second_new)


def rms_norm(values, gain):
    return values * lax.rsqrt(jnp.mean(values * values, axis=-1, keepdims=True) + norm_eps) * gain


def rms_back(values, grad, gain):
    inverse = lax.rsqrt(jnp.mean(values * values, axis=-1, keepdims=True) + norm_eps)
    scaled = grad * gain
    return inverse * (
        scaled - values * inverse * inverse * jnp.mean(scaled * values, axis=-1, keepdims=True)
    )


def segment_positions(row):
    order = jnp.arange(row.shape[0], dtype=jnp.int32)
    change = jnp.concatenate([jnp.ones((1,), dtype=bool), row[1:] != row[:-1]])
    starts = lax.cummax(jnp.where(change, order, 0), axis=0)
    return order - starts


def rotary_tables(positions):
    half = HEAD_DIM // 2
    freqs = rope_base ** (-(jnp.arange(half).astype(jnp.float32) * 2.0 / HEAD_DIM))
    angles = positions.astype(jnp.float32)[:, None] * freqs[None, :]
    return (jnp.cos(angles)[:, None, :], jnp.sin(angles)[:, None, :])


def rotate(values, cosine, sine):
    half = values.shape[-1] // 2
    first_half = values[..., :half]
    second_half = values[..., half:]
    return jnp.concatenate(
        [first_half * cosine - second_half * sine, second_half * cosine + first_half * sine],
        axis=-1,
    )


def unrotate(values, cosine, sine):
    half = values.shape[-1] // 2
    first_half = values[..., :half]
    second_half = values[..., half:]
    return jnp.concatenate(
        [first_half * cosine + second_half * sine, second_half * cosine - first_half * sine],
        axis=-1,
    )


def body(
    tokens,
    cotangent,
    norm_gains,
    w_attn,
    w_in,
    w_down,
    segments,
    owners,
    master,
    first_moment,
    second_moment,
):
    group_rows = tokens.shape[0]
    model_size = lax.axis_size("mp")
    model_index = lax.axis_index("mp")
    share = group_rows // model_size
    share_start = model_index * share
    capacity = master.shape[0]
    everyone = lax.axis_size(("dp", "mp"))
    score_scale = HEAD_DIM ** (-0.5)
    widths = [outer for inner, outer in proj_dims()]
    slot_index = slot_positions(owners, capacity)
    copies = lax.all_gather(master.astype(jnp.bfloat16), ("dp", "mp"), axis=0, tiled=True)
    lowers, uppers, magnitudes = unpack(jnp.take(copies, slot_index, axis=0).reshape(-1))
    frozen = [w_attn[0], w_attn[1], w_attn[2], w_attn[3], w_in[0], w_in[1], w_down]
    lower_local = []
    combined = []
    square_parts = []
    for index in range(7):
        rows_here = frozen[index].shape[0]
        piece = lax.dynamic_slice_in_dim(lowers[index], model_index * rows_here, rows_here, 0)
        lower_local.append(piece)
        joined = frozen[index].astype(jnp.float32) + dora_scale * jnp.dot(
            piece.astype(jnp.float32), uppers[index].astype(jnp.float32).T, precision=highest
        )
        combined.append(joined)
        square_parts.append(jnp.sum(joined * joined, axis=0))

    def rows_of(values):
        return lax.dynamic_slice_in_dim(values, share_start, share, 0)

    def split_parts(values, indices, axis):
        pieces = []
        offset = 0
        for index in indices:
            pieces.append(lax.slice_in_dim(values, offset, offset + widths[index], axis=axis))
            offset += widths[index]
        return pieces

    norms = [None] * 7
    mixed_share = [None] * 7
    low_share = [None] * 7
    mixed_full = [None] * 7
    grads = [None] * 7

    def set_scales(indices):
        summed = lax.psum(jnp.concatenate([square_parts[index] for index in indices]), "mp")
        squares = split_parts(summed, indices, 0)
        for index, value in zip(indices, squares):
            norms[index] = jnp.sqrt(value + column_eps)

    def scale(index):
        return magnitudes[index].astype(jnp.float32) / norms[index]

    def local_partials(inputs_local, indices):
        mixed_list = []
        low_list = []
        for index in indices:
            low_part = jnp.dot(inputs_local, lower_local[index], preferred_element_type=jnp.float32)
            mixed = jnp.dot(
                inputs_local, frozen[index], preferred_element_type=jnp.float32
            ) + dora_scale * jnp.dot(
                low_part, uppers[index].astype(jnp.float32).T, precision=highest
            )
            mixed_list.append(mixed)
            low_list.append(low_part)
        return (
            inputs_local,
            jnp.concatenate(mixed_list, axis=1),
            jnp.concatenate(low_list, axis=1),
        )

    def group_partials(inputs_b, indices):
        rows_here = frozen[indices[0]].shape[0]
        inputs_local = lax.dynamic_slice_in_dim(inputs_b, model_index * rows_here, rows_here, 1)
        return local_partials(inputs_local, indices)

    def finish(indices, local_mixed, local_low):
        summed_mixed, summed_low = lax.psum((local_mixed, local_low), "mp")
        pieces = split_parts(summed_mixed, indices, 1)
        for position, index in enumerate(indices):
            mixed_full[index] = pieces[position]
            mixed_share[index] = rows_of(pieces[position])
            low_share[index] = rows_of(summed_low[:, position * RANK : (position + 1) * RANK])
        return pieces

    def gather_inputs(local):
        return lax.all_gather(local, "mp", axis=1, tiled=True)

    xf = tokens.astype(jnp.float32)
    row = segments[0]
    cosine, sine = rotary_tables(segment_positions(row))
    order = jnp.arange(group_rows)
    allowed = (row[:, None] == row[None, :]) & (order[None, :] <= order[:, None])
    features = rms_norm(xf, norm_gains[0]).astype(jnp.bfloat16)
    first_local, first_mixed, first_low = group_partials(features, (0, 1, 2))
    set_scales((0, 1, 2))
    summed_mixed, summed_low = lax.psum((first_mixed, first_low), "mp")
    pieces = split_parts(summed_mixed, (0, 1, 2), 1)
    heads_in = []
    for index in range(3):
        mixed_full[index] = pieces[index]
        mixed_share[index] = rows_of(pieces[index])
        low_share[index] = rows_of(summed_low[:, index * RANK : (index + 1) * RANK])
        projected = (pieces[index] * scale(index)).reshape(group_rows, HEADS, HEAD_DIM)
        if index < 2:
            projected = rotate(projected, cosine, sine)
        heads_in.append(projected.astype(jnp.bfloat16))
    query_b, key_b, value_b = heads_in

    def attention_scores(query_h, key_h):
        scores = (
            jnp.einsum("thd,shd->hts", query_h, key_h, preferred_element_type=jnp.float32)
            * score_scale
        )
        return jnp.where(allowed[None], scores, -1e30)

    scores = attention_scores(query_b, key_b)
    top = jnp.max(scores, axis=-1, keepdims=True)
    expd = jnp.exp(scores - top)
    total = jnp.sum(expd, axis=-1, keepdims=True)
    probs = (expd / total).astype(jnp.bfloat16)
    attended_h = jnp.einsum("hts,shd->thd", probs, value_b, preferred_element_type=jnp.float32)
    attended_h, log_total = (attended_h, top + jnp.log(total))
    attended = attended_h.reshape(group_rows, D).astype(jnp.bfloat16)
    out_local, out_mixed, out_low = group_partials(attended, (3,))
    set_scales((3,))
    x_two = xf + finish((3,), out_mixed, out_low)[0] * scale(3)
    second_features = rms_norm(x_two, norm_gains[1]).astype(jnp.bfloat16)
    ffn_local, ffn_mixed, ffn_low = group_partials(second_features, (4, 5))
    set_scales((4, 5))
    gate_pre, up_pre = finish((4, 5), ffn_mixed, ffn_low)
    gate = gate_pre * scale(4)
    upward = up_pre * scale(5)
    sigmoid_gate = jax.nn.sigmoid(gate)
    act = (gate * sigmoid_gate * upward).astype(jnp.bfloat16)
    down_local, down_mixed, down_low = group_partials(act, (6,))
    set_scales((6,))
    down_pre = finish((6,), down_mixed, down_low)[0]
    layer_out = (x_two + down_pre * scale(6)).astype(jnp.bfloat16)

    def whole_dot(index, grad):
        return jnp.sum(grad * mixed_full[index], axis=0)

    def project_back(index, grad, inputs_local, group_dot):
        norm = norms[index]
        magnitude = magnitudes[index].astype(jnp.float32)
        grad_b = (grad * (magnitude / norm)).astype(jnp.bfloat16)
        share_dot = jnp.sum(rows_of(grad) * mixed_share[index], axis=0)
        grad_full = combined[index] * (-group_dot * magnitude / (norm * norm * norm))[None, :]
        upper_f = uppers[index].astype(jnp.float32)
        lower_f = lower_local[index].astype(jnp.float32)
        through = dora_scale * jnp.dot(grad_b, uppers[index], preferred_element_type=jnp.float32)
        grad_lower = jnp.dot(
            inputs_local.astype(jnp.float32).T, through, precision=highest
        ) + dora_scale * jnp.dot(grad_full, upper_f, precision=highest)
        grad_upper = dora_scale * jnp.dot(
            rows_of(grad_b).astype(jnp.float32).T, low_share[index], precision=highest
        ) + dora_scale * jnp.dot(grad_full.T, lower_f, precision=highest)
        grads[index] = (grad_lower, grad_upper, share_dot / norm)
        return jnp.dot(grad_b, frozen[index].T, preferred_element_type=jnp.float32) + jnp.dot(
            through, lower_f.T, precision=highest
        )

    grad_out = cotangent.astype(jnp.float32)
    grad_act = gather_inputs(project_back(6, grad_out, down_local, whole_dot(6, grad_out)))
    grad_gate = grad_act * upward * sigmoid_gate * (1.0 + gate * (1.0 - sigmoid_gate))
    grad_up = grad_act * gate * sigmoid_gate
    ffn_back = project_back(4, grad_gate, ffn_local, whole_dot(4, grad_gate)) + project_back(
        5, grad_up, ffn_local, whole_dot(5, grad_up)
    )
    grad_two = grad_out + rms_back(x_two, gather_inputs(ffn_back), norm_gains[1])
    grad_att = gather_inputs(project_back(3, grad_two, out_local, whole_dot(3, grad_two)))
    grad_att = grad_att.astype(jnp.bfloat16).reshape(group_rows, HEADS, HEAD_DIM)
    weights = jnp.exp(attention_scores(query_b, key_b) - log_total)
    weights_b = weights.astype(jnp.bfloat16)
    grad_weights = jnp.einsum("thd,shd->hts", grad_att, value_b, preferred_element_type=jnp.float32)
    grad_value = jnp.einsum("hts,thd->shd", weights_b, grad_att, preferred_element_type=jnp.float32)
    centred = jnp.sum(weights * grad_weights, axis=-1, keepdims=True)
    grad_scores = (weights * (grad_weights - centred)).astype(jnp.bfloat16)
    grad_query = (
        jnp.einsum("hts,shd->thd", grad_scores, key_b, preferred_element_type=jnp.float32)
        * score_scale
    )
    grad_key = (
        jnp.einsum("hts,thd->shd", grad_scores, query_b, preferred_element_type=jnp.float32)
        * score_scale
    )
    grad_query, grad_key, grad_value = (
        unrotate(grad_query, cosine, sine),
        unrotate(grad_key, cosine, sine),
        grad_value,
    )
    incoming = [
        grad_query.reshape(group_rows, D),
        grad_key.reshape(group_rows, D),
        grad_value.reshape(group_rows, D),
    ]
    group_dots = [whole_dot(index, incoming[index]) for index in range(3)]
    first_back = project_back(0, incoming[0], first_local, group_dots[0])
    first_back = first_back + project_back(1, incoming[1], first_local, group_dots[1])
    first_back = first_back + project_back(2, incoming[2], first_local, group_dots[2])
    input_grad = grad_two + rms_back(xf, gather_inputs(first_back), norm_gains[0])
    pieces = []
    for index in range(7):
        rows_total = proj_dims()[index][0]
        grad_lower = grads[index][0]
        placed = lax.dynamic_update_slice_in_dim(
            jnp.zeros((rows_total, RANK), jnp.float32),
            grad_lower,
            model_index * grad_lower.shape[0],
            0,
        )
        pieces.append(placed.reshape(-1))
    for index in range(7):
        pieces.append(grads[index][1].reshape(-1))
    for index in range(7):
        pieces.append(grads[index][2])
    blocks = jnp.concatenate(pieces).reshape(-1, BLOCK)
    buffer = jnp.zeros((capacity * everyone, BLOCK), jnp.float32).at[slot_index].set(blocks)
    owned = lax.psum_scatter(buffer, ("dp", "mp"), scatter_dimension=0, tiled=True)
    slot_block = (
        jnp.full((capacity * everyone,), -1, jnp.int32)
        .at[slot_index]
        .set(jnp.arange(blocks.shape[0], dtype=jnp.int32))
    )
    local_blocks = lax.dynamic_slice_in_dim(
        slot_block, lax.axis_index(("dp", "mp")) * capacity, capacity, 0
    )
    new_master, new_first, new_second = adam_update(
        master, owned, first_moment, second_moment, block_rates(local_blocks)
    )
    return (layer_out, input_grad, new_master, new_first, new_second)


f32 = jnp.float32
bf16 = jnp.bfloat16
VM = pl.BlockSpec(memory_space=pltpu.VMEM)
SM = pl.BlockSpec(memory_space=pltpu.SMEM)
ANY = pl.BlockSpec(memory_space=pl.ANY)
HBM = pl.BlockSpec(memory_space=pltpu.HBM)
TILE = 128
CHUNK = 256
N_DP = 4
N_MP = 8
N_Z = 4
WIDE = 768
FILL = 64


def mm(left, right):
    return lax.dot_general(left, right, (((1,), (0,)), ((), ())), preferred_element_type=f32)


def mm_t(left, right):
    return lax.dot_general(left, right, (((1,), (1,)), ((), ())), preferred_element_type=f32)


def mm_f(left, right):
    return lax.dot_general(left, right, (((0,), (0,)), ((), ())), preferred_element_type=f32)


def halves(value):
    high = value.astype(bf16)
    return high, (value - high.astype(f32)).astype(bf16)


def mm2(left, right):
    high, low = halves(left)
    return mm(high, right) + mm(low, right)


def mm2_t(left, right):
    high, low = halves(left)
    return mm_t(high, right) + mm_t(low, right)


def mm2_f(left, right):
    high, low = halves(left)
    return mm_f(high, right) + mm_f(low, right)


def twice(parts):
    return jnp.concatenate([part for one in parts for part in (one, one)], axis=0)


def only(part, position, count):
    zero = jnp.zeros_like(part)
    return twice([part if index == position else zero for index in range(count)])


def high_low(value):
    high = value.astype(bf16).astype(f32)
    lanes = lax.broadcasted_iota(jnp.int32, value.shape, 1)
    return jnp.where(jnp.bitwise_and(lanes, RANK) == 0, high, value - high).astype(bf16)


def swap64(value):
    return pltpu.roll(value, 64, 1)


def low_lanes(rows):
    return lax.broadcasted_iota(jnp.int32, (rows, TILE), 1) < 64


def merge(first, second):
    low = low_lanes(first.shape[0])
    return (
        jnp.where(low, first, swap64(second)),
        jnp.where(low, swap64(first), second),
    )


def tile(value, index):
    return value[:, index * TILE : (index + 1) * TILE]


def to_dp_order(value):
    out = [None] * 16
    for core in range(2):
        for pair in range(2):
            for part in range(2):
                first = 8 * pair + 2 * core + part
                low, high = merge(tile(value, first), tile(value, first + 4))
                out[8 * part + 2 * core + pair] = low
                out[8 * part + 4 + 2 * core + pair] = high
    return jnp.concatenate(out, axis=1)


def to_mp_order(value):
    out = [None] * 16
    for core in range(2):
        for pair in range(2):
            for part in range(2):
                first = 8 * part + 2 * core + pair
                low, high = merge(tile(value, first), tile(value, first + 4))
                out[8 * pair + 2 * core + part] = low
                out[8 * pair + 2 * core + part + 4] = high
    return jnp.concatenate(out, axis=1)


def shape_of(shape, dtype):
    return jax.ShapeDtypeStruct(shape, dtype)


def run(kernel, ins, specs, outs, scratch=(), name=None, after=(), megabytes=4, us=1.0):
    n_in, n_after = len(ins), len(after)

    def body(*refs):
        kernel(*refs[:n_in], *refs[n_in + n_after :])

    kinds = {"s": SM, "v": VM, "h": VM, "r": ANY}
    return pl.pallas_call(
        body,
        out_shape=list(outs),
        in_specs=[kinds[kind] for kind in specs] + [ANY] * n_after,
        out_specs=[VM] * len(outs),
        scratch_shapes=list(scratch),
        compiler_params=pltpu.CompilerParams(vmem_limit_bytes=megabytes * 2**20),
        cost_estimate=pl.CostEstimate(flops=int(us * 10**9), bytes_accessed=int(us * 10**6), transcendentals=0),
        name=name,
    )(*ins, *after)


def at(index, unit):
    return pl.ds(pl.multiple_of(index * unit, unit), unit)


def first_norm_kernel(tokens, gains, out):
    value = tokens[...].astype(f32)
    inverse = lax.rsqrt(jnp.mean(value * value, axis=-1, keepdims=True) + norm_eps)
    out[...] = to_dp_order(value * inverse * gains[0:1, :]).astype(bf16)


def line_kernel(step, where, p0, p1, p2, p3, out, forward):
    width = out.shape[2]
    for index, piece in enumerate((p0, p1, p2, p3)):
        rows = at(jnp.bitwise_xor(where[2], index), 64)
        for result, core in ((out, where[3]), (forward, 1 - where[3])):
            lanes = pl.ds(pl.multiple_of(core * step, TILE), width)
            result[:, rows, :] = piece[:, :, lanes]


def stack_kernel(first, second, out):
    out[0] = first[...]
    out[1] = second[...]


def join_all_kernel(p0, p1, p2, p3, p4, p5, first, second):
    for out, pieces in ((first, (p0, p1, p2)), (second, (p3, p4, p5))):
        begin = 0
        for piece in pieces:
            out[begin : begin + piece.shape[0]] = piece[...]
            begin += piece.shape[0]


def thirds(first, second):
    parts = []
    for value in (first, second):
        for _ in range(3):
            part = value.astype(bf16).astype(f32)
            parts.append(part)
            value = value - part
    parts += [jnp.zeros_like(first)] * 2
    return jnp.concatenate(parts, axis=0).astype(bf16)


def from_thirds(rows):
    value = rows.astype(f32)
    return [value[k : k + 1] + value[k + 1 : k + 2] + value[k + 2 : k + 3] for k in (0, 3)]


def eight(a, ax, y2, b, by, x2):
    return [
        lambda p: a[p],
        lambda p: ax[p],
        lambda p: y2[0, p],
        lambda p: y2[1, p],
        lambda p: b[p],
        lambda p: by[p],
        lambda p: x2[0, p],
        lambda p: x2[1, p],
    ]


def order_matrix():
    rows = lax.broadcasted_iota(jnp.int32, (BLOCK, BLOCK), 0)
    cols = lax.broadcasted_iota(jnp.int32, (BLOCK, BLOCK), 1)
    target = jnp.bitwise_and(rows, RANK - 1) * (BLOCK // RANK) + jnp.right_shift(rows, 4)
    return jnp.where(cols == target, 1.0, 0.0).astype(bf16)


def pick(indices, pieces):
    total = None
    first = 0
    for piece in pieces:
        rows = piece.shape[0]
        lanes = lax.broadcasted_iota(jnp.int32, (indices.shape[0], rows), 1) + first
        part = mm(jnp.where(lanes == indices, 1.0, 0.0).astype(bf16), piece[...])
        total = part if total is None else total + part
        first += rows
    return total


def adapters_kernel(even_at, odd_at, flat_at, *rest):
    pieces, (out, out_m, tiles) = rest[:-3], rest[-3:]
    order = order_matrix()
    even = mm(pick(even_at[...], pieces).astype(bf16), order)
    odd = mm(pick(odd_at[...], pieces).astype(bf16), order)
    for part in range(8):
        low, high = merge(tile(even, part), tile(odd, part))
        tiles[:, part, :] = low
        tiles[:, 8 + part, :] = high
    for index in range(out.shape[1] // TILE):
        out[:, index * TILE : (index + 1) * TILE] = tiles[index].astype(bf16)
    flat = pick(flat_at[...], pieces)
    for index in range(out_m.shape[1] // BLOCK):
        out_m[0:1, index * BLOCK : (index + 1) * BLOCK] = flat[index : index + 1, :]


def column_norm(weights, lowers, uppers):
    joined = weights.astype(f32) + dora_scale * mm_f(lowers, uppers)
    return jnp.sum(joined * joined, axis=0, keepdims=True)


def split_rows(where, part, send, keep, share):
    core = where[3]
    for line in range(N_Z):
        send[line * share : (line + 1) * share] = part[at(2 * line + 1 - core, share)].astype(bf16)
    for line in range(N_Z):
        keep[line * share : (line + 1) * share] = part[at(2 * line + core, share)]


def attention_kernel(spans, where, x, b0, b1, b2, b3, b4, b5, w_out, flat, mags, cos, sin, seg_row, seg_col, squares,
                     send, keep, mixed, qkv, probs, att, low_qkv, low_out, stats, part):
    blocks = eight(b0, b1, b2, b3, b4, b5)
    width = CHUNK
    rows = x.shape[0]
    la = [spans[("A", p)][0] for p in range(3)]
    lb = [spans[("B", p)][0] for p in range(3)]
    allowed = seg_col[...] == seg_row[...]
    t_index = lax.broadcasted_iota(jnp.int32, (rows, rows), 0)
    s_index = lax.broadcasted_iota(jnp.int32, (rows, rows), 1)
    allowed = jnp.logical_and(allowed, s_index <= t_index)
    lows = mm_t(x[...], twice([flat[:, la[p] : la[p] + D] for p in range(3)]))
    low_qkv[...] = lows
    lows = high_low(lows)
    for p in range(3):
        upper = flat[:, lb[p] : lb[p] + width]
        total = dora_scale * mm(lows, only(upper, p, 3))
        square = jnp.zeros((1, width), f32)
        for index, block in enumerate(blocks):
            chunk = where[4 + index]
            weights = block(p)
            total += mm(x[:, at(chunk, CHUNK)], weights)
            lowers = flat[:, pl.ds(pl.multiple_of(la[p] + chunk * CHUNK, TILE), CHUNK)]
            square += column_norm(weights, lowers, upper)
        norm = jnp.sqrt(square + column_eps)
        magnitude = mags[:, pl.ds(pl.multiple_of(p * D + where[1] * width, TILE), width)]
        scale = magnitude / norm
        lanes = slice(p * width, (p + 1) * width)
        mixed[:, lanes] = total
        stats[0:1, lanes] = scale
        stats[1:2, lanes] = norm
        stats[2:3, lanes] = magnitude
        value = total * scale
        for head in range(width // HEAD_DIM):
            one = value[:, head * HEAD_DIM : (head + 1) * HEAD_DIM]
            if p < 2:
                one = one * cos[...] + swap64(one) * sin[...]
            begin = p * width + head * HEAD_DIM
            qkv[:, begin : begin + HEAD_DIM] = one.astype(bf16)
    for head in range(width // HEAD_DIM):
        lanes = slice(head * HEAD_DIM, (head + 1) * HEAD_DIM)
        query = qkv[:, lanes]
        keys = qkv[:, width + head * HEAD_DIM : width + (head + 1) * HEAD_DIM]
        value = qkv[:, 2 * width + head * HEAD_DIM : 2 * width + (head + 1) * HEAD_DIM]
        scores = mm_t(query, keys) * HEAD_DIM ** (-0.5)
        scores = jnp.where(allowed, scores, -1e30)
        expd = jnp.exp(scores - jnp.max(scores, axis=-1, keepdims=True))
        weights = expd / jnp.sum(expd, axis=-1, keepdims=True)
        probs[head] = weights
        att[:, lanes] = mm(weights.astype(bf16), value).astype(bf16)
    a_out, b_out = spans[("A", 3)][0], spans[("B", 3)][0]
    low = mm_t(att[...], flat[:, a_out : a_out + width])
    low_out[...] = low
    part[...] = mm(att[...], w_out[...]) + dora_scale * mm2(low, flat[:, b_out : b_out + D])
    split_rows(where, part, send, keep, keep.shape[0] // N_Z)
    send[keep.shape[0] :] = thirds(squares[0:1], squares[1:2])


def pair_kernel(where, keep, received, p1, p2, p3, own):
    share = own.shape[0]

    def line(index):
        rows = at(index, share)
        return keep[rows] + received[rows].astype(f32)

    own[...] = line(where[2])
    for step, piece in ((1, p1), (2, p2), (3, p3)):
        piece[...] = line(jnp.bitwise_xor(where[2], step)).astype(bf16)


def pair_more_kernel(where, keep, received, squares, p1, p2, p3, own, more):
    share = own.shape[0]

    def line(index):
        rows = at(index, share)
        return keep[rows] + received[rows].astype(f32)

    own[...] = line(where[2])
    first, second = from_thirds(received[keep.shape[0] :])
    first, second = first + squares[0:1], second + squares[1:2]
    more[0:1], more[1:2] = first, second
    rows = thirds(first, second)
    for step, piece in ((1, p1), (2, p2), (3, p3)):
        piece[0:share] = line(jnp.bitwise_xor(where[2], step)).astype(bf16)
        piece[share:] = rows


def total_of(own, r1, r2, r3):
    rows = own.shape[0]
    return own[...] + r1[0:rows].astype(f32) + r2[0:rows].astype(f32) + r3[0:rows].astype(f32)


def pair_grads_kernel(where, keep, received, kept, got, p1, p2, p3, own, own_grads):
    share, unit = own.shape[0], own_grads.shape[0]
    half = unit // 2

    def line(index):
        rows = at(index, share)
        return keep[rows] + received[rows].astype(f32)

    def grads(index):
        rows = at(index, unit)
        return kept[rows] + got[rows].astype(f32)

    own[...] = line(where[2])
    own_grads[...] = grads(where[2])
    for step, piece in ((1, p1), (2, p2), (3, p3)):
        index = jnp.bitwise_xor(where[2], step)
        piece[0:share] = line(index).astype(bf16)
        value = grads(index).astype(bf16)
        piece[share:, 0:BLOCK] = value[0:half]
        piece[share:, BLOCK:] = value[half:]


def second_norm_kernel(own, more, r1, r2, r3, tokens, gains, mags, x_two, mixed, out, scale_o, norm_o, scale_d, norm_d):
    share = own.shape[0]
    total = own[...]
    squares = [more[0:1], more[1:2]]
    for piece in (r1, r2, r3):
        total = total + piece[0:share].astype(f32)
        for row, value in enumerate(from_thirds(piece[share:])):
            squares[row] = squares[row] + value
    for square, begin, scale, norm in (
        (squares[0], 3 * D, scale_o, norm_o),
        (squares[1], 4 * D + 2 * FF, scale_d, norm_d),
    ):
        value = jnp.sqrt(square + column_eps)
        norm[...] = value
        scale[...] = mags[:, begin : begin + D] / value
    mixed[...] = total
    value = tokens[...].astype(f32) + total * scale_o[...]
    x_two[...] = value
    inverse = lax.rsqrt(jnp.mean(value * value, axis=-1, keepdims=True) + norm_eps)
    out[...] = to_dp_order(value * inverse * gains[1:2, :]).astype(bf16)


def join_rows(where, pieces, out):
    share = out.shape[0] // N_MP
    for index, piece in enumerate(pieces):
        line = jnp.bitwise_xor(where[2], index % N_Z)
        core = where[3] if index < N_Z else 1 - where[3]
        out[at(2 * line + core, share)] = piece[0:share].astype(out.dtype)


def join_kernel(where, p0, p1, p2, p3, p4, p5, p6, p7, input_grad, layer_out):
    share = layer_out.shape[0] // N_MP
    pieces = (p0, p1, p2, p3, p4, p5, p6, p7)
    join_rows(where, pieces, input_grad)
    join_rows(where, [piece.at[share : 2 * share] for piece in pieces], layer_out)


def wide_squares(spans, where, blocks, chunks, flat):
    squares = []
    for p in range(2):
        a, b = spans[("A", 4 + p)][0], spans[("B", 4 + p)][0]
        square = jnp.zeros((1, WIDE), f32)
        for index, block in zip(chunks, blocks):
            begin = pl.multiple_of(a + where[4 + index] * CHUNK, TILE)
            square += column_norm(block(p), flat[:, pl.ds(begin, CHUNK)], flat[:, b : b + WIDE])
        squares.append(square)
    return jnp.concatenate(squares, axis=1)


def wide_first_kernel(spans, where, a, ax, b, by, flat, squares):
    blocks = eight(a, ax, None, b, by, None)
    squares[...] = wide_squares(spans, where, [blocks[k] for k in (0, 1, 4, 5)], (0, 1, 4, 5), flat)


def wide_norm_kernel(spans, where, y2, x2, flat, mags, squares, stats):
    blocks = eight(None, None, y2, None, None, x2)
    total = squares[...] + wide_squares(spans, where, [blocks[k] for k in (2, 3, 6, 7)], (2, 3, 6, 7), flat)
    for p in range(2):
        lanes = slice(p * WIDE, (p + 1) * WIDE)
        norm = jnp.sqrt(total[:, lanes] + column_eps)
        first = 4 * D + p * FF + where[2] * (2 * FF // N_MP) + where[3] * (WIDE - TILE)
        magnitude = mags[:, pl.ds(pl.multiple_of(first, TILE), WIDE)]
        stats[0:1, lanes] = magnitude / norm
        stats[1:2, lanes] = norm
        stats[2:3, lanes] = magnitude


def row_norm_kernel(spans, w_out, w_down, flat, squares):
    for row, (p, weights) in enumerate(((3, w_out[...]), (6, w_down[...]))):
        a, size = spans[("A", p)]
        b = spans[("B", p)][0]
        squares[row : row + 1, :] = column_norm(weights, flat[:, a : a + size], flat[:, b : b + D])


def down_back_kernel(spans, where, cotangent, scale, w_down, flat, d_act, grad_b, through, padded):
    a, size = spans[("A", 6)]
    b = spans[("B", 6)][0]
    grad = (cotangent[...].astype(f32) * scale[...]).astype(bf16)
    grad_b[...] = grad
    low = dora_scale * mm_t(grad, flat[:, b : b + D])
    through[...] = low
    padded[...] = jnp.zeros_like(padded)
    padded[:, 0:size] = mm_t(grad, w_down[...]) + mm2(low, flat[:, a : a + size])
    value = padded[...]
    d_act[...] = jnp.where(where[3] == 0, value, pltpu.roll(value, FILL, 1))


def middle_kernel(spans, where, p0, p1, p2, p3, p4, p5, p6, p7, b0, b1, b2, b3, b4, b5, d_act, flat, stats,
                  send, keep, x, act, grads, throughs, lows, dots, part, mixed):
    blocks = eight(b0, b1, b2, b3, b4, b5)
    join_rows(where, (p0, p1, p2, p3, p4, p5, p6, p7), x)
    la = [spans[("A", 4 + p)][0] for p in range(2)]
    lb = [spans[("B", 4 + p)][0] for p in range(2)]
    uppers = [flat[:, b : b + WIDE] for b in lb]
    low = mm_t(x[...], twice([flat[:, a : a + D] for a in la]))
    lows[...] = low
    low = high_low(low)
    for p in range(2):
        total = dora_scale * mm(low, only(uppers[p], p, 2))
        for index, block in enumerate(blocks):
            total += mm(x[:, at(where[4 + index], CHUNK)], block(p))
        mixed[:, p * WIDE : (p + 1) * WIDE] = total
    lanes = lax.broadcasted_iota(jnp.int32, d_act.shape, 1) - where[3] * FILL
    used = jnp.logical_and(lanes >= 0, lanes < WIDE - FILL)
    gate = mixed[:, :WIDE] * stats[0:1, :WIDE]
    upward = mixed[:, WIDE:] * stats[0:1, WIDE:]
    sigmoid_gate = jax.nn.sigmoid(gate)
    silu = gate * sigmoid_gate
    act[...] = jnp.where(used, silu * upward, 0.0).astype(bf16)
    back = jnp.where(used, d_act[...], 0.0)
    grad = back * upward * sigmoid_gate * (1.0 + gate * (1.0 - sigmoid_gate))
    dots[0:1, :WIDE] = jnp.sum(grad * mixed[:, :WIDE], axis=0, keepdims=True)
    grads[:, :WIDE] = (grad * stats[0:1, :WIDE]).astype(bf16)
    grad = back * silu
    dots[0:1, WIDE:] = jnp.sum(grad * mixed[:, WIDE:], axis=0, keepdims=True)
    grads[:, WIDE:] = (grad * stats[0:1, WIDE:]).astype(bf16)
    through = dora_scale * (
        mm_t(grads[:, :WIDE], only(uppers[0], 0, 2)) + mm_t(grads[:, WIDE:], only(uppers[1], 1, 2))
    )
    throughs[...] = through
    through = high_low(through)
    for index, block in enumerate(blocks):
        chunk = where[4 + index]
        lowers = [flat[:, pl.ds(pl.multiple_of(a + chunk * CHUNK, TILE), CHUNK)] for a in la]
        total = mm(through, twice(lowers))
        for p in range(2):
            total += mm_t(grads[:, p * WIDE : (p + 1) * WIDE], block(p))
        part[:, at(chunk, CHUNK)] = total
    split_rows(where, part, send, keep, send.shape[0] // N_Z)


def down_kernel(spans, where, act, w_down, flat, cotangent, send, keep, low_out, dots, part, local):
    a, size = spans[("A", 6)]
    b = spans[("B", 6)][0]
    value = act[...].astype(f32)
    value = jnp.where(where[3] == 0, value, pltpu.roll(value, WIDE - FILL, 1))
    local[...] = value.astype(bf16)
    inputs = local[:, 0:size]
    low = mm_t(inputs, flat[:, a : a + size])
    low_out[...] = low
    part[...] = mm(inputs, w_down[...]) + dora_scale * mm2(low, flat[:, b : b + D])
    split_rows(where, part, send, keep, send.shape[0] // N_Z)
    dots[...] = jnp.sum(cotangent[...].astype(f32) * part[...], axis=0, keepdims=True)


def norm_back(value, grad, gain):
    inverse = lax.rsqrt(jnp.mean(value * value, axis=-1, keepdims=True) + norm_eps)
    scaled = grad * gain
    inner = jnp.mean(scaled * value, axis=-1, keepdims=True)
    return inverse * (scaled - value * inverse * inverse * inner)


def second_back_kernel(own, r1, r2, r3, x_two, mixed, cotangent, gains, scale, dots_d, grad_two, grad_b, dots):
    total = to_mp_order(total_of(own, r1, r2, r3))
    grad = cotangent[...].astype(f32) + norm_back(x_two[...], total, gains[1:2, :])
    grad_two[...] = grad
    grad_b[0 : grad.shape[0]] = (grad * scale[...]).astype(bf16)
    own = jnp.sum(grad * mixed[...], axis=0, keepdims=True)
    dots[...] = own
    grad_b[grad.shape[0] :] = thirds(own, dots_d[...])


def last_rows_kernel(own, r1, r2, r3, tokens, grad_two, gains, own_d, d1, d2, d3, x_two, scale, out):
    share = own.shape[0]
    total = to_mp_order(total_of(own, r1, r2, r3))
    value = tokens[...].astype(f32)
    out[0:share] = (grad_two[...] + norm_back(value, total, gains[0:1, :])).astype(bf16)
    out[share:] = (x_two[...] + total_of(own_d, d1, d2, d3) * scale[...]).astype(bf16)


def attention_back_kernel(spans, where, p0, p1, p2, p3, p4, p5, p6, p7, b0, b1, b2, b3, b4, b5, w_out, flat,
                          cos, sin, mixed, qkv, probs, stats,
                          send, keep, grad_out, grads, throughs, through_out, dots, dots_o, dots_d, part, incoming):
    blocks = eight(b0, b1, b2, b3, b4, b5)
    width = CHUNK
    join_rows(where, (p0, p1, p2, p3, p4, p5, p6, p7), grad_out)
    sums = [jnp.zeros((1, D), f32)] * 2
    for piece in (p0, p1, p2, p3, p4, p5, p6, p7):
        for index, value in enumerate(from_thirds(piece[grad_out.shape[0] // N_MP :])):
            sums[index] = sums[index] + value
    dots_o[...], dots_d[...] = sums
    a, b = spans[("A", 3)][0], spans[("B", 3)][0]
    low = dora_scale * mm_t(grad_out[...], flat[:, b : b + D])
    through_out[...] = low
    grad_att = (mm_t(grad_out[...], w_out[...]) + mm2(low, flat[:, a : a + width])).astype(bf16)
    for head in range(width // HEAD_DIM):
        lanes = [slice(p * width + head * HEAD_DIM, p * width + (head + 1) * HEAD_DIM) for p in range(3)]
        query, keys, value = [qkv[:, one] for one in lanes]
        grad = grad_att[:, head * HEAD_DIM : (head + 1) * HEAD_DIM]
        weights = probs[head]
        grad_weights = mm_t(grad, value)
        incoming[:, lanes[2]] = mm_f(weights.astype(bf16), grad)
        centred = jnp.sum(weights * grad_weights, axis=-1, keepdims=True)
        grad_scores = (weights * (grad_weights - centred)).astype(bf16)
        grad_query = mm(grad_scores, keys) * HEAD_DIM ** (-0.5)
        grad_key = mm_f(grad_scores, query) * HEAD_DIM ** (-0.5)
        incoming[:, lanes[0]] = grad_query * cos[...] - swap64(grad_query) * sin[...]
        incoming[:, lanes[1]] = grad_key * cos[...] - swap64(grad_key) * sin[...]
    dots[...] = jnp.sum(incoming[...] * mixed[...], axis=0, keepdims=True)
    grads[...] = (incoming[...] * stats[0:1, :]).astype(bf16)
    la = [spans[("A", p)][0] for p in range(3)]
    uppers = [flat[:, spans[("B", p)][0] : spans[("B", p)][0] + width] for p in range(3)]
    through = mm_t(grads[:, :width], only(uppers[0], 0, 3))
    for p in (1, 2):
        through += mm_t(grads[:, p * width : (p + 1) * width], only(uppers[p], p, 3))
    through = dora_scale * through
    throughs[...] = through
    through = high_low(through)
    for index, block in enumerate(blocks):
        chunk = where[4 + index]
        lowers = [flat[:, pl.ds(pl.multiple_of(a + chunk * CHUNK, TILE), CHUNK)] for a in la]
        total = mm(through, twice(lowers))
        for p in range(3):
            total += mm_t(grads[:, p * width : (p + 1) * width], block(p))
        part[:, at(chunk, CHUNK)] = total
    split_rows(where, part, send, keep, send.shape[0] // N_Z)


def to_blocks(value, tiles, out, begin):
    pairs = value.shape[1] // TILE
    for index in range(pairs):
        tiles[index] = tile(value, index)
    for part in range(8):
        even, odd = merge(tiles[0:pairs, part, :], tiles[0:pairs, 8 + part, :])
        lanes = slice(part * TILE, (part + 1) * TILE)
        out[begin : begin + pairs, lanes] = even
        out[begin + pairs : begin + 2 * pairs, lanes] = odd


def column_grads_kernel(spans, projections, width, where, x, b0, b1, b2, b3, b4, b5, flat, stats, grads, throughs,
                        lows, dots, out_a, out_b, out_m, tiles, whole):
    blocks = eight(b0, b1, b2, b3, b4, b5)
    for position, p in enumerate(projections):
        a, b = spans[("A", p)][0], spans[("B", p)][0]
        lanes = slice(position * width, (position + 1) * width)
        ranks = slice(2 * position * RANK, (2 * position + 1) * RANK)
        upper = flat[:, b : b + width]
        norm = stats[1:2, lanes]
        inverse = 1.0 / norm
        e = dots[0:1, lanes]
        out_m[0:1, lanes] = e * inverse
        ratio = -e * stats[2:3, lanes] * inverse * inverse * inverse
        scaled = halves(dora_scale * upper.astype(f32) * ratio)
        through = halves(throughs[:, ranks])
        square = dora_scale * (mm_t(scaled[0], upper) + mm_t(scaled[1], upper))
        lower = flat[:, a : a + D]
        whole[...] = mm2(square, lower) + mm_f(through[0], x[...]) + mm_f(through[1], x[...])
        crossed = dora_scale * mm2(mm_t(lower, lower), upper)
        for index, block in enumerate(blocks):
            chunk = where[4 + index]
            weights = block(position)
            whole[:, at(chunk, CHUNK)] += mm_t(scaled[0], weights) + mm_t(scaled[1], weights)
            crossed += mm(flat[:, pl.ds(pl.multiple_of(a + chunk * CHUNK, TILE), CHUNK)], weights)
        to_blocks(whole[...], tiles, out_a, position * D * RANK // BLOCK)
        upper_grad = dora_scale * (mm2_f(lows[:, ranks], grads[:, lanes]) + crossed * ratio)
        to_blocks(upper_grad, tiles, out_b, position * width * RANK // BLOCK)


def row_grads_kernel(spans, p, where, x, weights_ref, flat, scale_row, norm_row, mag_row, grads, through_in, low, dots,
                     out_a, out_b, tiles, local):
    a, size = spans[("A", p)]
    b = spans[("B", p)][0]
    weights = weights_ref[...]
    inputs = x[...]
    if p == 6:
        value = inputs.astype(f32)
        value = jnp.where(where[3] == 0, value, pltpu.roll(value, WIDE - FILL, 1))
        local[...] = value.astype(bf16)
        inputs = local[:, 0:size]
    lower = flat[:, a : a + size]
    upper = flat[:, b : b + D]
    inverse = 1.0 / norm_row[...]
    ratio = -dots[...] * mag_row[...] * inverse * inverse * inverse
    scaled = halves(dora_scale * upper.astype(f32) * ratio)
    square = dora_scale * (mm_t(scaled[0], upper) + mm_t(scaled[1], upper))
    grad = mm2(square, lower) + mm2_f(through_in[...], inputs)
    grad += mm_t(scaled[0], weights) + mm_t(scaled[1], weights)
    if size % TILE:
        grad = jnp.concatenate([grad, jnp.zeros((RANK, TILE - size % TILE), f32)], axis=1)
    to_blocks(grad, tiles, out_a, 0)
    crossed = mm(lower, weights) + dora_scale * mm2(mm_t(lower, lower), upper)
    to_blocks(dora_scale * (mm2_f(low[...], grads[...]) + crossed * ratio), tiles, out_b, 0)


def pack_kernel(where, a_f, a_a, b_d, b_o, m_f, m_a, dots_o, norm_o, dots_d, norm_d, give, keep, rows, flat):
    begin = 0
    for array in (a_f, a_a, b_d, b_o):
        rows[begin : begin + array.shape[0]] = array[...]
        begin += array.shape[0]
    flat[...] = jnp.zeros_like(flat)
    for p in range(3):
        lanes = pl.ds(pl.multiple_of(p * D + where[1] * CHUNK, TILE), CHUNK)
        flat[:, lanes] = m_a[:, p * CHUNK : (p + 1) * CHUNK]
    flat[:, 3 * D : 4 * D] = dots_o[...] / norm_o[...]
    for p in range(2):
        first = 4 * D + p * FF + where[2] * (2 * FF // N_MP) + where[3] * (WIDE - TILE)
        flat[:, pl.ds(pl.multiple_of(first, TILE), WIDE)] = m_f[:, p * WIDE : (p + 1) * WIDE]
    flat[:, 4 * D + 2 * FF :] = dots_d[...] / norm_d[...]
    rows[begin:] = jnp.zeros((rows.shape[0] - begin, BLOCK), f32)
    for index in range(flat.shape[1] // BLOCK):
        rows[begin + index : begin + index + 1] = flat[:, index * BLOCK : (index + 1) * BLOCK]
    unit = rows.shape[0] // N_MP
    for line in range(N_Z):
        give[line * unit : (line + 1) * unit] = rows[at(2 * line + 1 - where[3], unit)].astype(bf16)
        keep[line * unit : (line + 1) * unit] = rows[at(2 * line + where[3], unit)]


def local_kernel(where, own, r1, r2, r3, b_f, b_a, a_d, a_o, mine, p1, p2, p3, rows):
    begin = own.shape[0]
    half = begin // 2
    for index in range(2):
        lanes = slice(index * BLOCK, (index + 1) * BLOCK)
        total = own[index * half : (index + 1) * half]
        for piece in (r1, r2, r3):
            total = total + piece[piece.shape[0] - half :, lanes].astype(f32)
        rows[index * half : (index + 1) * half] = total
    for array in (b_f, b_a, a_d, a_o):
        rows[begin : begin + array.shape[0]] = array[...]
        begin += array.shape[0]
    rows[begin:] = jnp.zeros((rows.shape[0] - begin, BLOCK), f32)
    part = mine.shape[0]
    mine[...] = rows[at(where[0], part)]
    for step, piece in ((1, p1), (2, p2), (3, p3)):
        piece[...] = rows[at(jnp.bitwise_xor(where[0], step), part)].astype(bf16)


def last_sum_kernel(own, r1, r2, r3, out):
    out[...] = total_of(own, r1, r2, r3).astype(bf16)


def update_kernel(index, mine, s0, s1, s2, s3, s4, s5, s6, s7, master, first, second, new_master, new_first, new_second):
    picked = pick(index[...], (s0, s1, s2, s3, s4, s5, s6, s7)).astype(bf16)
    grad = jnp.where(mine[...] >= COUNT_FLAT, picked.astype(f32), mm_t(picked, order_matrix()))
    grad = jnp.where(mine[...] >= 0, grad, 0.0)
    rates = jnp.where(mine[...] < COUNT_FLAT, rate_upper, rate_magnitude)
    rates = jnp.where(mine[...] < COUNT_LOWER, rate_lower, rates)
    rates = jnp.where(mine[...] < 0, 0.0, rates)
    weight = master[...]
    first_new = beta_one * first[...] + (1.0 - beta_one) * grad
    second_new = beta_two * second[...] + (1.0 - beta_two) * grad * grad
    first_hat = first_new / (1.0 - beta_one**STEP)
    second_hat = second_new / (1.0 - beta_two**STEP)
    new_master[...] = weight - rates * (
        first_hat / (jnp.sqrt(second_hat) + adam_eps) + weight_decay * weight
    )
    new_first[...] = first_new
    new_second[...] = second_new


COUNT_LOWER = RANK * (6 * D + FF) // BLOCK
COUNT_FLAT = COUNT_LOWER + RANK * (5 * D + 2 * FF) // BLOCK


def block_starts():
    starts = {}
    total = 0
    for kind, side in (("A", 0), ("B", 1)):
        for index, sizes in enumerate(proj_dims()):
            starts[(kind, index)] = total
            total += sizes[side] * RANK // BLOCK
    return starts


def fast_body(
    tokens,
    cotangent,
    norm_gains,
    w_attn,
    w_in,
    w_down,
    segments,
    owners,
    master,
    first_moment,
    second_moment,
):
    rows = tokens.shape[0]
    mi = lax.axis_index("mp")
    di = lax.axis_index("dp")
    core = mi % 2
    zi = mi // 2
    share = rows // N_MP
    capacity = master.shape[0]
    n_blocks = owners.shape[0]
    width = D // N_MP
    starts = block_starts()

    def mp_swap(values, step):
        return lax.ppermute(values, "mp", [(i, i ^ step) for i in range(N_MP)])

    def dp_swap(values, step):
        return lax.ppermute(values, "dp", [(i, i ^ step) for i in range(N_DP)])

    order = [(0, 0), (1, 0), (2, 0), (3, 0), (0, 1), (2, 1), (1, 1), (3, 1)]
    chunks = [(di ^ t) * 2 + (core ^ h) for t, h in order]
    where = jnp.stack([di, mi, zi, core] + chunks).astype(jnp.int32)

    def stack(first, second, after=()):
        shape = (2,) + first.shape
        return run(
            stack_kernel, [first, second], "hh", [shape_of(shape, bf16)], name="stack", after=after, us=0.6
        )[0]

    def plane_first(a, b):
        return a, dp_swap(a, 1), b, dp_swap(b, 2)

    def plane_second(a, ax, b, by, after=()):
        return [a, ax, dp_swap(stack(a, ax, after), 2), b, by, dp_swap(stack(b, by, after), 1)]

    def plane(a, b):
        return plane_second(*plane_first(a, b))

    sent = master.astype(bf16)
    line = [sent] + [mp_swap(sent, 2 * step) for step in range(1, N_Z)]
    first_b = plane_first(jnp.concatenate(line[:2]), jnp.concatenate(line[2:]))
    owners, segments, w_late, tokens, line_end = lax.optimization_barrier(
        (owners, segments, w_attn, tokens, first_b[2])
    )
    first_b = first_b[:2] + (line_end,) + first_b[3:]
    sheet = plane_second(*first_b)
    sheet = [one.reshape(-1, BLOCK) for one in sheet]
    features = run(
        first_norm_kernel,
        [tokens, norm_gains],
        "hh",
        [shape_of((rows, D), bf16)],
        name="first_norm",
        megabytes=6,
        us=1.2,
        after=[first_b[2]],
    )[0]
    def cut(weights, count, chip):
        pieces = []
        for index in range(N_Z):
            piece = lax.dynamic_slice(weights, (0, di * 64, (zi ^ index) * chip), (count, 64, chip))
            pieces.append(mp_swap(piece, 2 * index) if index else piece)
        return pieces

    def columns_of(pieces, size, step, name, after=()):
        count = pieces[0].shape[0]
        a, forward = run(
            functools.partial(line_kernel, step),
            [where] + pieces,
            "shhhh",
            [shape_of((count, CHUNK, size), bf16)] * 2,
            name=name,
            after=after,
        )
        return plane_first(a, mp_swap(forward, 1))

    first_a = columns_of(cut(w_attn, 3, 2 * width), width, width, "line_a", [features])
    blocks_a = plane_second(*first_a)
    sheet = run(
        join_all_kernel,
        sheet,
        "h" * 6,
        [shape_of((8 * capacity, BLOCK), bf16)] * 2,
        name="adapter_rows",
        after=[first_a[0]],
        us=0.1,
    )
    stacked = list(sheet) + [mp_swap(one, 1) for one in sheet]
    w_in_late, own_a = lax.optimization_barrier((w_in, first_a[0]))
    pieces_f = cut(w_in_late, 2, 2 * FF // N_MP)
    w_out = w_late[3]

    ranks = slot_positions(owners, 0)
    owner_d, owner_m = owners // N_MP, owners % N_MP
    piece_at = (owner_d ^ di) * N_Z + ((owner_m // 2) ^ zi)
    listed = np.array([0, 1, 8, 9, 2, 3, 12, 13, 4, 5, 10, 11, 6, 7, 14, 15], np.int32)
    piece_at = jnp.sum(jnp.where(piece_at[:, None] == np.arange(16), listed, 0), axis=1)
    slot = (((owner_m % 2) ^ core) * 16 + piece_at) * capacity + ranks
    wanted = []
    spans = {}

    def want(name, blocks, size):
        spans[name] = (sum(w.shape[0] for w in wanted) * 64, size)
        wanted.append(blocks)

    by_dp = np.array(
        [(2 * z + c) * 4 + d for d in range(N_DP) for c in range(2) for z in range(N_Z)], np.int32
    )
    all_blocks = np.arange(D * RANK // BLOCK, dtype=np.int32)
    for index in (0, 1, 2, 4, 5):
        want(("A", index), starts[("A", index)] + by_dp, D)
        if index < 3:
            want(("B", index), starts[("B", index)] + mi * 4 + np.arange(4), width)
        else:
            first_block = starts[("B", index)] + zi * 22 + core * 10
            want(("B", index), first_block + np.arange(12), WIDE)
    want(("A", 3), starts[("A", 3)] + mi * 4 + np.arange(4), width)
    want(("B", 3), starts[("B", 3)] + all_blocks, D)
    want(("A", 6), starts[("A", 6)] + mi * 11 + np.minimum(np.arange(12), 10), FF // N_MP)
    want(("B", 6), starts[("B", 6)] + all_blocks, D)
    chosen = jnp.take(slot, jnp.concatenate([jnp.asarray(w, jnp.int32) for w in wanted]))
    n_pairs = chosen.shape[0] // 2
    pairs = chosen.reshape(n_pairs, 2)
    flat, mags = run(
        adapters_kernel,
        [pairs[:, :1], pairs[:, 1:], slot[COUNT_FLAT:, None]] + stacked,
        "vvv" + "h" * len(stacked),
        [shape_of((RANK, n_pairs * TILE), bf16), shape_of((1, (n_blocks - COUNT_FLAT) * BLOCK), f32)],
        [pltpu.VMEM((n_pairs, RANK, TILE), f32)],
        name="adapters", megabytes=13, us=0.3,
    )

    def bind(kernel, *args):
        return functools.partial(kernel, spans, *args)

    def column_grads(projections, size, x, blocks, flat, stats, grads, throughs, lows, dots, after):
        count = len(projections)
        return run(
            bind(column_grads_kernel, projections, size),
            [where, x] + blocks + [flat, stats, grads, throughs, lows, dots],
            "s" + "h" * 13,
            [
                shape_of((count * D * RANK // BLOCK, BLOCK), f32),
                shape_of((count * size * RANK // BLOCK, BLOCK), f32),
                shape_of((1, count * size), f32),
            ],
            [pltpu.VMEM((D // TILE, RANK, TILE), f32), pltpu.VMEM((RANK, D), f32)],
            name="column_grads", megabytes=9, us=1,
            after=after,
        )

    def row_grads(p, x, weights, flat, scale, norm, mag, grads, through, low, dots, after):
        size = spans[("A", p)][1]
        return run(
            bind(row_grads_kernel, p),
            [where, x, weights, flat, scale, norm, mag, grads, through, low, dots],
            "s" + "h" * 10,
            [
                shape_of((-(-size // TILE) * 2, BLOCK), f32),
                shape_of((D * RANK // BLOCK, BLOCK), f32),
            ],
            [pltpu.VMEM((D // TILE, RANK, TILE), f32), pltpu.VMEM((rows, WIDE), bf16)],
            name="row_grads", megabytes=6, us=0.1,
            after=after,
        )

    row = segments[0]
    cosine, sine = rotary_tables(segment_positions(row))
    cosine, sine = cosine[:, 0], sine[:, 0]
    cos_full = jnp.concatenate([cosine, cosine], axis=-1)
    sin_full = jnp.concatenate([-sine, sine], axis=-1)
    tokens_here = lax.dynamic_slice_in_dim(tokens, mi * share, share, 0)
    cotangent_here = lax.dynamic_slice_in_dim(cotangent, mi * share, share, 0)
    half_rows = [shape_of((rows // 2, D), bf16), shape_of((rows // 2, D), f32)]

    def finish_rows(send, keep, after):
        received = mp_swap(send, 1)
        p1, p2, p3, own = run(
            pair_kernel,
            [where, keep, received],
            "shh",
            [shape_of((share, D), bf16)] * 3 + [shape_of((share, D), f32)],
            name="pair_sums", megabytes=4, us=1.2,
            after=after,
        )
        return [own, mp_swap(p1, 2), mp_swap(p2, 4), mp_swap(p3, 6)]

    def gather_rows(value):
        mine = [value] + [mp_swap(value, 2 * step) for step in range(1, N_Z)]
        return mine + [mp_swap(one, 1) for one in mine]

    squares = run(
        bind(row_norm_kernel),
        [w_out, w_down, flat],
        "hhh",
        [shape_of((2, D), f32)],
        name="row_norms",
        us=0.1,
    )[0]
    n_heads = width // HEAD_DIM
    send, keep, mixed_a, qkv, probs, att, low_a, low_o, stats_a = run(
        bind(attention_kernel),
        [where, features] + blocks_a + [w_out, flat, mags, cos_full, sin_full, segments, row[:, None], squares],
        "s" + "h" * 15,
        [shape_of((rows // 2 + 8, D), bf16), half_rows[1]]
        + [
            shape_of((rows, 3 * width), f32),
            shape_of((rows, 3 * width), bf16),
            shape_of((n_heads, rows, rows), f32),
            shape_of((rows, width), bf16),
            shape_of((rows, 6 * RANK), f32),
            shape_of((rows, RANK), f32),
            shape_of((8, 3 * width), f32),
        ],
        [pltpu.VMEM((rows, D), f32)],
        name="attention",
        megabytes=13,
        us=10,
    )

    p1, p2, p3, own_o, more_o = run(
        pair_more_kernel,
        [where, keep, mp_swap(send, 1), squares],
        "shhh",
        [shape_of((share + 8, D), bf16)] * 3 + [shape_of((share, D), f32), shape_of((2, D), f32)],
        name="pair_sums",
        us=1.2,
    )
    sums_o = [mp_swap(p1, 2), mp_swap(p2, 4), mp_swap(p3, 6)]
    first_f = columns_of(pieces_f, WIDE, WIDE - TILE, "line_f")
    blocks_f = plane_second(*first_f, after=sums_o[1:2])
    row_of = shape_of((1, D), f32)
    x_two, mixed_o, features_two, scale_o, norm_o, scale_d, norm_d = run(
        second_norm_kernel,
        [own_o, more_o] + sums_o + [tokens_here, norm_gains, mags],
        "h" * 8,
        [shape_of((share, D), f32)] * 2 + [shape_of((share, D), bf16)] + [row_of] * 4,
        name="second_norm",
        us=0.5,
    )
    mag_o = mags[:, 3 * D : 4 * D]
    mag_d = mags[:, 4 * D + 2 * FF :]
    pieces = gather_rows(features_two)
    squares_f = run(
        bind(wide_first_kernel),
        [where] + [blocks_f[k] for k in (0, 1, 3, 4)] + [flat],
        "s" + "h" * 5,
        [shape_of((1, 2 * WIDE), f32)],
        name="wide_squares", megabytes=8, us=3,
        after=[pieces[1]],
    )[0]
    d_act, grad_d, through_d = run(
        bind(down_back_kernel),
        [where, cotangent, scale_d, w_down, flat],
        "shhhh",
        [shape_of((rows, WIDE), f32), shape_of((rows, D), bf16), shape_of((rows, RANK), f32)],
        [pltpu.VMEM((rows, WIDE), f32)],
        name="down_back", megabytes=7, us=3.5,
        after=[squares_f],
    )
    stats_f = run(
        bind(wide_norm_kernel),
        [where] + [blocks_f[k] for k in (2, 5)] + [flat, mags, squares_f],
        "s" + "h" * 5,
        [shape_of((8, 2 * WIDE), f32)],
        name="wide_norms", megabytes=8, us=3,
        after=[through_d],
    )[0]
    send, keep, x_f, act, grads_f, through_f, low_f, dots_f = run(
        bind(middle_kernel),
        [where] + pieces + blocks_f + [d_act, flat, stats_f],
        "s" + "h" * 17,
        half_rows
        + [
            shape_of((rows, D), bf16),
            shape_of((rows, WIDE), bf16),
            shape_of((rows, 2 * WIDE), bf16),
            shape_of((rows, 4 * RANK), f32),
            shape_of((rows, 4 * RANK), f32),
            shape_of((1, 2 * WIDE), f32),
        ],
        [pltpu.VMEM((rows, D), f32), pltpu.VMEM((rows, 2 * WIDE), f32)],
        name="feed_forward", megabytes=22, us=14,
    )
    send_d, keep_d, low_d, dots_d = run(
        bind(down_kernel),
        [where, act, w_down, flat, cotangent],
        "shhhh",
        half_rows + [shape_of((rows, RANK), f32), shape_of((1, D), f32)],
        [pltpu.VMEM((rows, D), f32), pltpu.VMEM((rows, WIDE), bf16)],
        name="down", megabytes=9, us=3.5,
    )
    sums = finish_rows(send, keep, [low_d])
    a_f, b_f, m_f = column_grads(
        (4, 5), WIDE, x_f, blocks_f, flat, stats_f, grads_f, through_f, low_f, dots_f, [sums[1]]
    )
    grad_two, grad_o_piece, dots_o = run(
        second_back_kernel,
        sums + [x_two, mixed_o, cotangent_here, norm_gains, scale_o, dots_d],
        "h" * 10,
        [shape_of((share, D), f32), shape_of((share + 8, D), bf16), row_of],
        name="second_norm_back", megabytes=3, us=0.5,
        after=[m_f],
    )
    pieces_o = gather_rows(grad_o_piece)
    sums_d = finish_rows(send_d, keep_d, [pieces_o[0], pieces_o[7]])
    send, keep, grad_o, grads_a, through_a, through_o, dots_a, dots_all_o, dots_all_d = run(
        bind(attention_back_kernel),
        [where] + pieces_o + blocks_a + [w_out, flat, cos_full, sin_full, mixed_a, qkv, probs, stats_a],
        "s" + "h" * 22,
        half_rows
        + [
            shape_of((rows, D), bf16),
            shape_of((rows, 3 * width), bf16),
            shape_of((rows, 6 * RANK), f32),
            shape_of((rows, RANK), f32),
            shape_of((1, 3 * width), f32),
            row_of,
            row_of,
        ],
        [pltpu.VMEM((rows, D), f32), pltpu.VMEM((rows, 3 * width), f32)],
        name="attention_back",
        megabytes=10,
        us=0.1,
        after=[sums_d[0]],
    )
    a_o, b_o = row_grads(
        3, att, w_out, flat, scale_o, norm_o, mag_o, grad_o, through_o, low_o, dots_all_o, []
    )
    a_a, b_a, m_a = column_grads(
        (0, 1, 2), width, features, blocks_a, flat, stats_a, grads_a, through_a, low_a, dots_a, [a_o]
    )
    a_d, b_d = row_grads(
        6, act, w_down, flat, scale_d, norm_d, mag_d, grad_d, through_d, low_d, dots_all_d, [m_a]
    )
    unit, part = 32, 24
    give, kept = run(
        pack_kernel,
        [where, a_f, a_a, b_d, b_o, m_f, m_a, dots_o, norm_o, dots_d, norm_d],
        "s" + "h" * 10,
        [shape_of((N_Z * unit, BLOCK), bf16), shape_of((N_Z * unit, BLOCK), f32)],
        [pltpu.VMEM((N_MP * unit, BLOCK), f32), pltpu.VMEM((1, (n_blocks - COUNT_FLAT) * BLOCK), f32)],
        name="pack",
    )
    p1, p2, p3, own = run(
        pair_kernel,
        [where, kept, mp_swap(give, 1)],
        "shh",
        [shape_of((unit, BLOCK), bf16)] * 3 + [shape_of((unit, BLOCK), f32)],
        name="pack_sums",
        us=0.1,
    )
    p1, p2, p3, own, own_grads = run(
        pair_grads_kernel,
        [where, keep, mp_swap(send, 1), kept, mp_swap(give, 1)],
        "shhhh",
        [shape_of((share + unit // 2, D), bf16)] * 3 + [shape_of((share, D), f32), shape_of((unit, BLOCK), f32)],
        name="pair_grads",
        us=1.2,
    )
    sums = [own, mp_swap(p1, 2), mp_swap(p2, 4), mp_swap(p3, 6)]
    local_own, p1, p2, p3 = run(
        local_kernel,
        [where, own_grads] + sums[1:] + [b_f, b_a, a_d, a_o],
        "s" + "h" * 8,
        [shape_of((part, BLOCK), f32)] + [shape_of((part, BLOCK), bf16)] * 3,
        [pltpu.VMEM((N_DP * part, BLOCK), f32)],
        name="local_sums",
        us=0.1,
    )
    own = run(
        last_sum_kernel,
        [local_own, dp_swap(p1, 1), dp_swap(p2, 2), dp_swap(p3, 3)],
        "hhhh",
        [shape_of((part, BLOCK), bf16)],
        name="last_sums",
        us=0.1,
    )[0]
    last_piece = run(
        last_rows_kernel,
        sums + [tokens_here, grad_two, norm_gains] + sums_d + [x_two, scale_d],
        "h" * 13,
        [shape_of((2 * share, D), bf16)],
        name="last_rows",
        us=0.5,
    )[0]
    lines = jnp.concatenate([own] + [mp_swap(own, 2 * step) for step in range(1, N_Z)])
    summed = [lines] + [dp_swap(lines, step) for step in range(1, N_DP)]
    summed = summed + [mp_swap(one, 1) for one in summed]

    second = mp_swap(last_piece, 4)
    pieces = [last_piece, mp_swap(last_piece, 2), second, mp_swap(second, 2)]
    pieces = pieces + [mp_swap(one, 1) for one in pieces]
    input_grad, layer_out = run(
        join_kernel,
        [where] + pieces,
        "s" + "h" * 8,
        [shape_of((rows, D), f32), shape_of((rows, D), bf16)],
        name="join_rows",
        megabytes=8,
        us=4,
    )

    table = np.zeros((n_blocks,), np.int32)

    def note(block, m, r):
        table[block] = ((r // part) * N_MP + m) * 64 + r % part

    def split_pairs(count, r):
        return r // 2 + (r % 2) * (count // 2)

    def blocks_of(names):
        def listing(count, m):
            each = count // len(names)
            for position, blocks in enumerate(names):
                for k, block in enumerate(blocks(m)):
                    if block is not None:
                        yield position * each + split_pairs(each, k), block

        return listing

    def lower_columns(p):
        return lambda m: [starts[("A", p)] + int(k) for k in by_dp]

    def upper_rows(p):
        return lambda m: [starts[("B", p)] + int(k) for k in all_blocks]

    def lower_rows(p, per):
        return lambda m: [starts[("A", p)] + m * per + k for k in range(per)]

    def upper_columns(p):
        if p < 3:
            return lambda m: [starts[("B", p)] + m * 4 + k for k in range(4)]
        return lambda m: [
            starts[("B", p)] + (m // 2) * 22 + (m % 2) * 10 + k
            if (k < 11 if m % 2 == 0 else k >= 1)
            else None
            for k in range(12)
        ]

    begin = 0
    for listing, count in (
        (blocks_of([lower_columns(4), lower_columns(5)]), a_f.shape[0]),
        (blocks_of([lower_columns(p) for p in range(3)]), a_a.shape[0]),
        (blocks_of([upper_rows(6)]), b_d.shape[0]),
        (blocks_of([upper_rows(3)]), b_o.shape[0]),
        (lambda count, m: [(r, COUNT_FLAT + r) for r in range(count)], n_blocks - COUNT_FLAT),
    ):
        for r, block in listing(count, None):
            note(block, (begin + r) // unit, (begin + r) % unit)
        begin += count
    begin = unit
    for listing, count in (
        (blocks_of([upper_columns(4), upper_columns(5)]), b_f.shape[0]),
        (blocks_of([upper_columns(p) for p in range(3)]), b_a.shape[0]),
        (blocks_of([lower_rows(6, 11)]), a_d.shape[0]),
        (blocks_of([lower_rows(3, 4)]), a_o.shape[0]),
    ):
        for m in range(N_MP):
            for r, block in listing(count, m):
                note(block, m, begin + r)
        begin += count
    me = di * N_MP + mi
    hits = (owners * capacity + ranks)[None, :] == me * capacity + jnp.arange(capacity)[:, None]
    mine = jnp.sum(jnp.where(hits, jnp.arange(n_blocks)[None, :] + 1, 0), axis=1) - 1
    code = jnp.sum(jnp.where(hits, jnp.asarray(table)[None, :], 0), axis=1)
    device, inner = code // 64, code % 64
    d_from, m_from = device // N_MP, device % N_MP
    list_at = (((m_from % 2) ^ core) * N_DP + (d_from ^ di)) * N_Z + ((m_from // 2) ^ zi)
    index = list_at * part + inner
    new_master, new_first, new_second = run(
        update_kernel,
        [index[:, None], mine[:, None]] + summed + [master, first_moment, second_moment],
        "vv" + "h" * 11,
        [shape_of(master.shape, f32)] * 3,
        name="update", megabytes=4, us=2,
    )
    return (layer_out, input_grad, new_master, new_first, new_second)


def solution(mesh):
    fast = mesh.shape["dp"] == 4 and mesh.shape["mp"] == 8
    return jax.shard_map(
        fast_body if fast else body,
        mesh=mesh,
        in_specs=(
            P("dp", None),
            P("dp", None),
            P(),
            P(None, "mp", None),
            P(None, "mp", None),
            P("mp", None),
            P("dp", None),
            P(),
            P(("dp", "mp"), None),
            P(("dp", "mp"), None),
            P(("dp", "mp"), None),
        ),
        out_specs=(
            P("dp", None),
            P("dp", None),
            P(("dp", "mp"), None),
            P(("dp", "mp"), None),
            P(("dp", "mp"), None),
        ),
        check_vma=False,
    )
```

```python
import functools

import jax
import jax.numpy as jnp
import numpy as np
from jax import lax
from jax.experimental import pallas as pl
from jax.experimental.pallas import tpu as pltpu
from jax.sharding import PartitionSpec as P

D = 2048
FF = 5632
HEADS = 16
HEAD_DIM = 128
RANK = 16
BLOCK = 1024
STEP = 5


dora_scale = 2.0
rope_base = 10000.0
norm_eps = 1e-05
column_eps = 1e-06
beta_one = 0.5
beta_two = 0.5
adam_eps = 1e-08
weight_decay = 0.01
rate_lower = 0.02
rate_upper = 0.1
rate_magnitude = 1.0
highest = lax.Precision.HIGHEST


def proj_dims():
    return [(D, D), (D, D), (D, D), (D, D), (D, FF), (D, FF), (FF, D)]


def unpack(flat):
    offset = 0
    lowers = []
    for inner, outer in proj_dims():
        lowers.append(flat[offset : offset + inner * RANK].reshape(inner, RANK))
        offset += inner * RANK
    uppers = []
    for inner, outer in proj_dims():
        uppers.append(flat[offset : offset + outer * RANK].reshape(outer, RANK))
        offset += outer * RANK
    magnitudes = []
    for inner, outer in proj_dims():
        magnitudes.append(flat[offset : offset + outer])
        offset += outer
    return (lowers, uppers, magnitudes)


def slot_positions(owners, capacity):
    order = jnp.arange(owners.shape[0], dtype=jnp.int32)
    same = (owners[:, None] == owners[None, :]) & (order[None, :] < order[:, None])
    ranks = jnp.sum(same.astype(jnp.int32), axis=1)
    return owners * capacity + ranks


def block_rates(block_ids):
    count_lower = RANK * (6 * D + FF) // BLOCK
    count_upper = RANK * (5 * D + 2 * FF) // BLOCK
    rates = jnp.where(block_ids < count_lower + count_upper, rate_upper, rate_magnitude)
    rates = jnp.where(block_ids < count_lower, rate_lower, rates)
    return jnp.where(block_ids < 0, 0.0, rates).astype(jnp.float32)


def adam_update(weight, grad, first, second, rates):
    first_new = beta_one * first + (1.0 - beta_one) * grad
    second_new = beta_two * second + (1.0 - beta_two) * grad * grad
    first_hat = first_new / (1.0 - beta_one**STEP)
    second_hat = second_new / (1.0 - beta_two**STEP)
    weight_new = weight - rates[:, None] * (
        first_hat / (jnp.sqrt(second_hat) + adam_eps) + weight_decay * weight
    )
    return (weight_new, first_new, second_new)


def rms_norm(values, gain):
    return values * lax.rsqrt(jnp.mean(values * values, axis=-1, keepdims=True) + norm_eps) * gain


def rms_back(values, grad, gain):
    inverse = lax.rsqrt(jnp.mean(values * values, axis=-1, keepdims=True) + norm_eps)
    scaled = grad * gain
    return inverse * (
        scaled - values * inverse * inverse * jnp.mean(scaled * values, axis=-1, keepdims=True)
    )


def segment_positions(row):
    order = jnp.arange(row.shape[0], dtype=jnp.int32)
    change = jnp.concatenate([jnp.ones((1,), dtype=bool), row[1:] != row[:-1]])
    starts = lax.cummax(jnp.where(change, order, 0), axis=0)
    return order - starts


def rotary_tables(positions):
    half = HEAD_DIM // 2
    freqs = rope_base ** (-(jnp.arange(half).astype(jnp.float32) * 2.0 / HEAD_DIM))
    angles = positions.astype(jnp.float32)[:, None] * freqs[None, :]
    return (jnp.cos(angles)[:, None, :], jnp.sin(angles)[:, None, :])


def rotate(values, cosine, sine):
    half = values.shape[-1] // 2
    first_half = values[..., :half]
    second_half = values[..., half:]
    return jnp.concatenate(
        [first_half * cosine - second_half * sine, second_half * cosine + first_half * sine],
        axis=-1,
    )


def unrotate(values, cosine, sine):
    half = values.shape[-1] // 2
    first_half = values[..., :half]
    second_half = values[..., half:]
    return jnp.concatenate(
        [first_half * cosine + second_half * sine, second_half * cosine - first_half * sine],
        axis=-1,
    )


def body(
    tokens,
    cotangent,
    norm_gains,
    w_attn,
    w_in,
    w_down,
    segments,
    owners,
    master,
    first_moment,
    second_moment,
):
    group_rows = tokens.shape[0]
    model_size = lax.axis_size("mp")
    model_index = lax.axis_index("mp")
    share = group_rows // model_size
    share_start = model_index * share
    capacity = master.shape[0]
    everyone = lax.axis_size(("dp", "mp"))
    score_scale = HEAD_DIM ** (-0.5)
    widths = [outer for inner, outer in proj_dims()]
    slot_index = slot_positions(owners, capacity)
    copies = lax.all_gather(master.astype(jnp.bfloat16), ("dp", "mp"), axis=0, tiled=True)
    lowers, uppers, magnitudes = unpack(jnp.take(copies, slot_index, axis=0).reshape(-1))
    frozen = [w_attn[0], w_attn[1], w_attn[2], w_attn[3], w_in[0], w_in[1], w_down]
    lower_local = []
    combined = []
    square_parts = []
    for index in range(7):
        rows_here = frozen[index].shape[0]
        piece = lax.dynamic_slice_in_dim(lowers[index], model_index * rows_here, rows_here, 0)
        lower_local.append(piece)
        joined = frozen[index].astype(jnp.float32) + dora_scale * jnp.dot(
            piece.astype(jnp.float32), uppers[index].astype(jnp.float32).T, precision=highest
        )
        combined.append(joined)
        square_parts.append(jnp.sum(joined * joined, axis=0))

    def rows_of(values):
        return lax.dynamic_slice_in_dim(values, share_start, share, 0)

    def split_parts(values, indices, axis):
        pieces = []
        offset = 0
        for index in indices:
            pieces.append(lax.slice_in_dim(values, offset, offset + widths[index], axis=axis))
            offset += widths[index]
        return pieces

    norms = [None] * 7
    mixed_share = [None] * 7
    low_share = [None] * 7
    mixed_full = [None] * 7
    grads = [None] * 7

    def set_scales(indices):
        summed = lax.psum(jnp.concatenate([square_parts[index] for index in indices]), "mp")
        squares = split_parts(summed, indices, 0)
        for index, value in zip(indices, squares):
            norms[index] = jnp.sqrt(value + column_eps)

    def scale(index):
        return magnitudes[index].astype(jnp.float32) / norms[index]

    def local_partials(inputs_local, indices):
        mixed_list = []
        low_list = []
        for index in indices:
            low_part = jnp.dot(inputs_local, lower_local[index], preferred_element_type=jnp.float32)
            mixed = jnp.dot(
                inputs_local, frozen[index], preferred_element_type=jnp.float32
            ) + dora_scale * jnp.dot(
                low_part, uppers[index].astype(jnp.float32).T, precision=highest
            )
            mixed_list.append(mixed)
            low_list.append(low_part)
        return (
            inputs_local,
            jnp.concatenate(mixed_list, axis=1),
            jnp.concatenate(low_list, axis=1),
        )

    def group_partials(inputs_b, indices):
        rows_here = frozen[indices[0]].shape[0]
        inputs_local = lax.dynamic_slice_in_dim(inputs_b, model_index * rows_here, rows_here, 1)
        return local_partials(inputs_local, indices)

    def finish(indices, local_mixed, local_low):
        summed_mixed, summed_low = lax.psum((local_mixed, local_low), "mp")
        pieces = split_parts(summed_mixed, indices, 1)
        for position, index in enumerate(indices):
            mixed_full[index] = pieces[position]
            mixed_share[index] = rows_of(pieces[position])
            low_share[index] = rows_of(summed_low[:, position * RANK : (position + 1) * RANK])
        return pieces

    def gather_inputs(local):
        return lax.all_gather(local, "mp", axis=1, tiled=True)

    xf = tokens.astype(jnp.float32)
    row = segments[0]
    cosine, sine = rotary_tables(segment_positions(row))
    order = jnp.arange(group_rows)
    allowed = (row[:, None] == row[None, :]) & (order[None, :] <= order[:, None])
    features = rms_norm(xf, norm_gains[0]).astype(jnp.bfloat16)
    first_local, first_mixed, first_low = group_partials(features, (0, 1, 2))
    set_scales((0, 1, 2))
    summed_mixed, summed_low = lax.psum((first_mixed, first_low), "mp")
    pieces = split_parts(summed_mixed, (0, 1, 2), 1)
    heads_in = []
    for index in range(3):
        mixed_full[index] = pieces[index]
        mixed_share[index] = rows_of(pieces[index])
        low_share[index] = rows_of(summed_low[:, index * RANK : (index + 1) * RANK])
        projected = (pieces[index] * scale(index)).reshape(group_rows, HEADS, HEAD_DIM)
        if index < 2:
            projected = rotate(projected, cosine, sine)
        heads_in.append(projected.astype(jnp.bfloat16))
    query_b, key_b, value_b = heads_in

    def attention_scores(query_h, key_h):
        scores = (
            jnp.einsum("thd,shd->hts", query_h, key_h, preferred_element_type=jnp.float32)
            * score_scale
        )
        return jnp.where(allowed[None], scores, -1e30)

    scores = attention_scores(query_b, key_b)
    top = jnp.max(scores, axis=-1, keepdims=True)
    expd = jnp.exp(scores - top)
    total = jnp.sum(expd, axis=-1, keepdims=True)
    probs = (expd / total).astype(jnp.bfloat16)
    attended_h = jnp.einsum("hts,shd->thd", probs, value_b, preferred_element_type=jnp.float32)
    attended_h, log_total = (attended_h, top + jnp.log(total))
    attended = attended_h.reshape(group_rows, D).astype(jnp.bfloat16)
    out_local, out_mixed, out_low = group_partials(attended, (3,))
    set_scales((3,))
    x_two = xf + finish((3,), out_mixed, out_low)[0] * scale(3)
    second_features = rms_norm(x_two, norm_gains[1]).astype(jnp.bfloat16)
    ffn_local, ffn_mixed, ffn_low = group_partials(second_features, (4, 5))
    set_scales((4, 5))
    gate_pre, up_pre = finish((4, 5), ffn_mixed, ffn_low)
    gate = gate_pre * scale(4)
    upward = up_pre * scale(5)
    sigmoid_gate = jax.nn.sigmoid(gate)
    act = (gate * sigmoid_gate * upward).astype(jnp.bfloat16)
    down_local, down_mixed, down_low = group_partials(act, (6,))
    set_scales((6,))
    down_pre = finish((6,), down_mixed, down_low)[0]
    layer_out = (x_two + down_pre * scale(6)).astype(jnp.bfloat16)

    def whole_dot(index, grad):
        return jnp.sum(grad * mixed_full[index], axis=0)

    def project_back(index, grad, inputs_local, group_dot):
        norm = norms[index]
        magnitude = magnitudes[index].astype(jnp.float32)
        grad_b = (grad * (magnitude / norm)).astype(jnp.bfloat16)
        share_dot = jnp.sum(rows_of(grad) * mixed_share[index], axis=0)
        grad_full = combined[index] * (-group_dot * magnitude / (norm * norm * norm))[None, :]
        upper_f = uppers[index].astype(jnp.float32)
        lower_f = lower_local[index].astype(jnp.float32)
        through = dora_scale * jnp.dot(grad_b, uppers[index], preferred_element_type=jnp.float32)
        grad_lower = jnp.dot(
            inputs_local.astype(jnp.float32).T, through, precision=highest
        ) + dora_scale * jnp.dot(grad_full, upper_f, precision=highest)
        grad_upper = dora_scale * jnp.dot(
            rows_of(grad_b).astype(jnp.float32).T, low_share[index], precision=highest
        ) + dora_scale * jnp.dot(grad_full.T, lower_f, precision=highest)
        grads[index] = (grad_lower, grad_upper, share_dot / norm)
        return jnp.dot(grad_b, frozen[index].T, preferred_element_type=jnp.float32) + jnp.dot(
            through, lower_f.T, precision=highest
        )

    grad_out = cotangent.astype(jnp.float32)
    grad_act = gather_inputs(project_back(6, grad_out, down_local, whole_dot(6, grad_out)))
    grad_gate = grad_act * upward * sigmoid_gate * (1.0 + gate * (1.0 - sigmoid_gate))
    grad_up = grad_act * gate * sigmoid_gate
    ffn_back = project_back(4, grad_gate, ffn_local, whole_dot(4, grad_gate)) + project_back(
        5, grad_up, ffn_local, whole_dot(5, grad_up)
    )
    grad_two = grad_out + rms_back(x_two, gather_inputs(ffn_back), norm_gains[1])
    grad_att = gather_inputs(project_back(3, grad_two, out_local, whole_dot(3, grad_two)))
    grad_att = grad_att.astype(jnp.bfloat16).reshape(group_rows, HEADS, HEAD_DIM)
    weights = jnp.exp(attention_scores(query_b, key_b) - log_total)
    weights_b = weights.astype(jnp.bfloat16)
    grad_weights = jnp.einsum("thd,shd->hts", grad_att, value_b, preferred_element_type=jnp.float32)
    grad_value = jnp.einsum("hts,thd->shd", weights_b, grad_att, preferred_element_type=jnp.float32)
    centred = jnp.sum(weights * grad_weights, axis=-1, keepdims=True)
    grad_scores = (weights * (grad_weights - centred)).astype(jnp.bfloat16)
    grad_query = (
        jnp.einsum("hts,shd->thd", grad_scores, key_b, preferred_element_type=jnp.float32)
        * score_scale
    )
    grad_key = (
        jnp.einsum("hts,thd->shd", grad_scores, query_b, preferred_element_type=jnp.float32)
        * score_scale
    )
    grad_query, grad_key, grad_value = (
        unrotate(grad_query, cosine, sine),
        unrotate(grad_key, cosine, sine),
        grad_value,
    )
    incoming = [
        grad_query.reshape(group_rows, D),
        grad_key.reshape(group_rows, D),
        grad_value.reshape(group_rows, D),
    ]
    group_dots = [whole_dot(index, incoming[index]) for index in range(3)]
    first_back = project_back(0, incoming[0], first_local, group_dots[0])
    first_back = first_back + project_back(1, incoming[1], first_local, group_dots[1])
    first_back = first_back + project_back(2, incoming[2], first_local, group_dots[2])
    input_grad = grad_two + rms_back(xf, gather_inputs(first_back), norm_gains[0])
    pieces = []
    for index in range(7):
        rows_total = proj_dims()[index][0]
        grad_lower = grads[index][0]
        placed = lax.dynamic_update_slice_in_dim(
            jnp.zeros((rows_total, RANK), jnp.float32),
            grad_lower,
            model_index * grad_lower.shape[0],
            0,
        )
        pieces.append(placed.reshape(-1))
    for index in range(7):
        pieces.append(grads[index][1].reshape(-1))
    for index in range(7):
        pieces.append(grads[index][2])
    blocks = jnp.concatenate(pieces).reshape(-1, BLOCK)
    buffer = jnp.zeros((capacity * everyone, BLOCK), jnp.float32).at[slot_index].set(blocks)
    owned = lax.psum_scatter(buffer, ("dp", "mp"), scatter_dimension=0, tiled=True)
    slot_block = (
        jnp.full((capacity * everyone,), -1, jnp.int32)
        .at[slot_index]
        .set(jnp.arange(blocks.shape[0], dtype=jnp.int32))
    )
    local_blocks = lax.dynamic_slice_in_dim(
        slot_block, lax.axis_index(("dp", "mp")) * capacity, capacity, 0
    )
    new_master, new_first, new_second = adam_update(
        master, owned, first_moment, second_moment, block_rates(local_blocks)
    )
    return (layer_out, input_grad, new_master, new_first, new_second)


f32 = jnp.float32
bf16 = jnp.bfloat16
VM = pl.BlockSpec(memory_space=pltpu.VMEM)
SM = pl.BlockSpec(memory_space=pltpu.SMEM)
ANY = pl.BlockSpec(memory_space=pl.ANY)
HBM = pl.BlockSpec(memory_space=pltpu.HBM)
TILE = 128
CHUNK = 256
N_DP = 4
N_MP = 8
N_Z = 4
WIDE = 768
FILL = 64


def mm(left, right):
    return lax.dot_general(left, right, (((1,), (0,)), ((), ())), preferred_element_type=f32)


def mm_t(left, right):
    return lax.dot_general(left, right, (((1,), (1,)), ((), ())), preferred_element_type=f32)


def mm_f(left, right):
    return lax.dot_general(left, right, (((0,), (0,)), ((), ())), preferred_element_type=f32)


def halves(value):
    high = value.astype(bf16)
    return high, (value - high.astype(f32)).astype(bf16)


def mm2(left, right):
    high, low = halves(left)
    return mm(high, right) + mm(low, right)


def mm2_t(left, right):
    high, low = halves(left)
    return mm_t(high, right) + mm_t(low, right)


def mm2_f(left, right):
    high, low = halves(left)
    return mm_f(high, right) + mm_f(low, right)


def twice(parts):
    return jnp.concatenate([part for one in parts for part in (one, one)], axis=0)


def only(part, position, count):
    zero = jnp.zeros_like(part)
    return twice([part if index == position else zero for index in range(count)])


def high_low(value):
    high = value.astype(bf16).astype(f32)
    lanes = lax.broadcasted_iota(jnp.int32, value.shape, 1)
    return jnp.where(jnp.bitwise_and(lanes, RANK) == 0, high, value - high).astype(bf16)


def swap64(value):
    return pltpu.roll(value, 64, 1)


def low_lanes(rows):
    return lax.broadcasted_iota(jnp.int32, (rows, TILE), 1) < 64


def merge(first, second):
    low = low_lanes(first.shape[0])
    return (
        jnp.where(low, first, swap64(second)),
        jnp.where(low, swap64(first), second),
    )


def tile(value, index):
    return value[:, index * TILE : (index + 1) * TILE]


def to_dp_order(value):
    out = [None] * 16
    for core in range(2):
        for pair in range(2):
            for part in range(2):
                first = 8 * pair + 2 * core + part
                low, high = merge(tile(value, first), tile(value, first + 4))
                out[8 * part + 2 * core + pair] = low
                out[8 * part + 4 + 2 * core + pair] = high
    return jnp.concatenate(out, axis=1)


def to_mp_order(value):
    out = [None] * 16
    for core in range(2):
        for pair in range(2):
            for part in range(2):
                first = 8 * part + 2 * core + pair
                low, high = merge(tile(value, first), tile(value, first + 4))
                out[8 * pair + 2 * core + part] = low
                out[8 * pair + 2 * core + part + 4] = high
    return jnp.concatenate(out, axis=1)


def shape_of(shape, dtype):
    return jax.ShapeDtypeStruct(shape, dtype)


def run(kernel, ins, specs, outs, scratch=(), name=None, after=(), megabytes=4, us=1.0):
    n_in, n_after = len(ins), len(after)

    def body(*refs):
        kernel(*refs[:n_in], *refs[n_in + n_after :])

    kinds = {"s": SM, "v": VM, "h": VM, "r": ANY}
    return pl.pallas_call(
        body,
        out_shape=list(outs),
        in_specs=[kinds[kind] for kind in specs] + [ANY] * n_after,
        out_specs=[VM] * len(outs),
        scratch_shapes=list(scratch),
        compiler_params=pltpu.CompilerParams(vmem_limit_bytes=megabytes * 2**20),
        cost_estimate=pl.CostEstimate(flops=int(us * 10**9), bytes_accessed=int(us * 10**6), transcendentals=0),
        name=name,
    )(*ins, *after)


def at(index, unit):
    return pl.ds(pl.multiple_of(index * unit, unit), unit)


def first_norm_kernel(tokens, gains, out):
    value = tokens[...].astype(f32)
    inverse = lax.rsqrt(jnp.mean(value * value, axis=-1, keepdims=True) + norm_eps)
    out[...] = to_dp_order(value * inverse * gains[0:1, :]).astype(bf16)


def line_kernel(step, where, p0, p1, p2, p3, out, forward):
    width = out.shape[2]
    for index, piece in enumerate((p0, p1, p2, p3)):
        rows = at(jnp.bitwise_xor(where[2], index), 64)
        for result, core in ((out, where[3]), (forward, 1 - where[3])):
            lanes = pl.ds(pl.multiple_of(core * step, TILE), width)
            result[:, rows, :] = piece[:, :, lanes]


def stack_kernel(first, second, out):
    out[0] = first[...]
    out[1] = second[...]


def join_all_kernel(p0, p1, p2, p3, p4, p5, first, second):
    for out, pieces in ((first, (p0, p1, p2)), (second, (p3, p4, p5))):
        begin = 0
        for piece in pieces:
            out[begin : begin + piece.shape[0]] = piece[...]
            begin += piece.shape[0]


def thirds(first, second):
    parts = []
    for value in (first, second):
        for _ in range(3):
            part = value.astype(bf16).astype(f32)
            parts.append(part)
            value = value - part
    parts += [jnp.zeros_like(first)] * 2
    return jnp.concatenate(parts, axis=0).astype(bf16)


def from_thirds(rows):
    value = rows.astype(f32)
    return [value[k : k + 1] + value[k + 1 : k + 2] + value[k + 2 : k + 3] for k in (0, 3)]


def eight(a, ax, y2, b, by, x2):
    return [
        lambda p: a[p],
        lambda p: ax[p],
        lambda p: y2[0, p],
        lambda p: y2[1, p],
        lambda p: b[p],
        lambda p: by[p],
        lambda p: x2[0, p],
        lambda p: x2[1, p],
    ]


def order_matrix():
    rows = lax.broadcasted_iota(jnp.int32, (BLOCK, BLOCK), 0)
    cols = lax.broadcasted_iota(jnp.int32, (BLOCK, BLOCK), 1)
    target = jnp.bitwise_and(rows, RANK - 1) * (BLOCK // RANK) + jnp.right_shift(rows, 4)
    return jnp.where(cols == target, 1.0, 0.0).astype(bf16)


def pick(indices, pieces):
    total = None
    first = 0
    for piece in pieces:
        rows = piece.shape[0]
        lanes = lax.broadcasted_iota(jnp.int32, (indices.shape[0], rows), 1) + first
        part = mm(jnp.where(lanes == indices, 1.0, 0.0).astype(bf16), piece[...])
        total = part if total is None else total + part
        first += rows
    return total


def adapters_kernel(even_at, odd_at, flat_at, *rest):
    pieces, (out, out_m, tiles) = rest[:-3], rest[-3:]
    order = order_matrix()
    even = mm(pick(even_at[...], pieces).astype(bf16), order)
    odd = mm(pick(odd_at[...], pieces).astype(bf16), order)
    for part in range(8):
        low, high = merge(tile(even, part), tile(odd, part))
        tiles[:, part, :] = low
        tiles[:, 8 + part, :] = high
    for index in range(out.shape[1] // TILE):
        out[:, index * TILE : (index + 1) * TILE] = tiles[index].astype(bf16)
    flat = pick(flat_at[...], pieces)
    for index in range(out_m.shape[1] // BLOCK):
        out_m[0:1, index * BLOCK : (index + 1) * BLOCK] = flat[index : index + 1, :]


def column_norm(weights, lowers, uppers):
    joined = weights.astype(f32) + dora_scale * mm_f(lowers, uppers)
    return jnp.sum(joined * joined, axis=0, keepdims=True)


def split_rows(where, part, send, keep, share):
    core = where[3]
    for line in range(N_Z):
        send[line * share : (line + 1) * share] = part[at(2 * line + 1 - core, share)].astype(bf16)
    for line in range(N_Z):
        keep[line * share : (line + 1) * share] = part[at(2 * line + core, share)]


def attention_kernel(spans, where, x, b0, b1, b2, b3, b4, b5, w_out, flat, mags, cos, sin, seg_row, seg_col, squares,
                     send, keep, mixed, qkv, probs, att, low_qkv, low_out, stats, part):
    blocks = eight(b0, b1, b2, b3, b4, b5)
    width = CHUNK
    rows = x.shape[0]
    la = [spans[("A", p)][0] for p in range(3)]
    lb = [spans[("B", p)][0] for p in range(3)]
    allowed = seg_col[...] == seg_row[...]
    t_index = lax.broadcasted_iota(jnp.int32, (rows, rows), 0)
    s_index = lax.broadcasted_iota(jnp.int32, (rows, rows), 1)
    allowed = jnp.logical_and(allowed, s_index <= t_index)
    lows = mm_t(x[...], twice([flat[:, la[p] : la[p] + D] for p in range(3)]))
    low_qkv[...] = lows
    lows = high_low(lows)
    for p in range(3):
        upper = flat[:, lb[p] : lb[p] + width]
        total = dora_scale * mm(lows, only(upper, p, 3))
        square = jnp.zeros((1, width), f32)
        for index, block in enumerate(blocks):
            chunk = where[4 + index]
            weights = block(p)
            total += mm(x[:, at(chunk, CHUNK)], weights)
            lowers = flat[:, pl.ds(pl.multiple_of(la[p] + chunk * CHUNK, TILE), CHUNK)]
            square += column_norm(weights, lowers, upper)
        norm = jnp.sqrt(square + column_eps)
        magnitude = mags[:, pl.ds(pl.multiple_of(p * D + where[1] * width, TILE), width)]
        scale = magnitude / norm
        lanes = slice(p * width, (p + 1) * width)
        mixed[:, lanes] = total
        stats[0:1, lanes] = scale
        stats[1:2, lanes] = norm
        stats[2:3, lanes] = magnitude
        value = total * scale
        for head in range(width // HEAD_DIM):
            one = value[:, head * HEAD_DIM : (head + 1) * HEAD_DIM]
            if p < 2:
                one = one * cos[...] + swap64(one) * sin[...]
            begin = p * width + head * HEAD_DIM
            qkv[:, begin : begin + HEAD_DIM] = one.astype(bf16)
    for head in range(width // HEAD_DIM):
        lanes = slice(head * HEAD_DIM, (head + 1) * HEAD_DIM)
        query = qkv[:, lanes]
        keys = qkv[:, width + head * HEAD_DIM : width + (head + 1) * HEAD_DIM]
        value = qkv[:, 2 * width + head * HEAD_DIM : 2 * width + (head + 1) * HEAD_DIM]
        scores = mm_t(query, keys) * HEAD_DIM ** (-0.5)
        scores = jnp.where(allowed, scores, -1e30)
        expd = jnp.exp(scores - jnp.max(scores, axis=-1, keepdims=True))
        weights = expd / jnp.sum(expd, axis=-1, keepdims=True)
        probs[head] = weights
        att[:, lanes] = mm(weights.astype(bf16), value).astype(bf16)
    a_out, b_out = spans[("A", 3)][0], spans[("B", 3)][0]
    low = mm_t(att[...], flat[:, a_out : a_out + width])
    low_out[...] = low
    part[...] = mm(att[...], w_out[...]) + dora_scale * mm2(low, flat[:, b_out : b_out + D])
    split_rows(where, part, send, keep, keep.shape[0] // N_Z)
    send[keep.shape[0] :] = thirds(squares[0:1], squares[1:2])


def pair_kernel(where, keep, received, p1, p2, p3, own):
    share = own.shape[0]

    def line(index):
        rows = at(index, share)
        return keep[rows] + received[rows].astype(f32)

    own[...] = line(where[2])
    for step, piece in ((1, p1), (2, p2), (3, p3)):
        piece[...] = line(jnp.bitwise_xor(where[2], step)).astype(bf16)


def pair_more_kernel(where, keep, received, squares, p1, p2, p3, own, more):
    share = own.shape[0]

    def line(index):
        rows = at(index, share)
        return keep[rows] + received[rows].astype(f32)

    own[...] = line(where[2])
    first, second = from_thirds(received[keep.shape[0] :])
    first, second = first + squares[0:1], second + squares[1:2]
    more[0:1], more[1:2] = first, second
    rows = thirds(first, second)
    for step, piece in ((1, p1), (2, p2), (3, p3)):
        piece[0:share] = line(jnp.bitwise_xor(where[2], step)).astype(bf16)
        piece[share:] = rows


def total_of(own, r1, r2, r3):
    rows = own.shape[0]
    return own[...] + r1[0:rows].astype(f32) + r2[0:rows].astype(f32) + r3[0:rows].astype(f32)


def pair_grads_kernel(where, keep, received, kept, got, p1, p2, p3, own, own_grads):
    share, unit = own.shape[0], own_grads.shape[0]
    half = unit // 2

    def line(index):
        rows = at(index, share)
        return keep[rows] + received[rows].astype(f32)

    def grads(index):
        rows = at(index, unit)
        return kept[rows] + got[rows].astype(f32)

    own[...] = line(where[2])
    own_grads[...] = grads(where[2])
    for step, piece in ((1, p1), (2, p2), (3, p3)):
        index = jnp.bitwise_xor(where[2], step)
        piece[0:share] = line(index).astype(bf16)
        value = grads(index).astype(bf16)
        piece[share:, 0:BLOCK] = value[0:half]
        piece[share:, BLOCK:] = value[half:]


def second_norm_kernel(own, more, r1, r2, r3, tokens, gains, mags, x_two, mixed, out, scale_o, norm_o, scale_d, norm_d):
    share = own.shape[0]
    total = own[...]
    squares = [more[0:1], more[1:2]]
    for piece in (r1, r2, r3):
        total = total + piece[0:share].astype(f32)
        for row, value in enumerate(from_thirds(piece[share:])):
            squares[row] = squares[row] + value
    for square, begin, scale, norm in (
        (squares[0], 3 * D, scale_o, norm_o),
        (squares[1], 4 * D + 2 * FF, scale_d, norm_d),
    ):
        value = jnp.sqrt(square + column_eps)
        norm[...] = value
        scale[...] = mags[:, begin : begin + D] / value
    mixed[...] = total
    value = tokens[...].astype(f32) + total * scale_o[...]
    x_two[...] = value
    inverse = lax.rsqrt(jnp.mean(value * value, axis=-1, keepdims=True) + norm_eps)
    out[...] = to_dp_order(value * inverse * gains[1:2, :]).astype(bf16)


def join_rows(where, pieces, out):
    share = out.shape[0] // N_MP
    for index, piece in enumerate(pieces):
        line = jnp.bitwise_xor(where[2], index % N_Z)
        core = where[3] if index < N_Z else 1 - where[3]
        out[at(2 * line + core, share)] = piece[0:share].astype(out.dtype)


def join_kernel(where, p0, p1, p2, p3, p4, p5, p6, p7, input_grad, layer_out):
    share = layer_out.shape[0] // N_MP
    pieces = (p0, p1, p2, p3, p4, p5, p6, p7)
    join_rows(where, pieces, input_grad)
    join_rows(where, [piece.at[share : 2 * share] for piece in pieces], layer_out)


def wide_squares(spans, where, blocks, chunks, flat):
    squares = []
    for p in range(2):
        a, b = spans[("A", 4 + p)][0], spans[("B", 4 + p)][0]
        square = jnp.zeros((1, WIDE), f32)
        for index, block in zip(chunks, blocks):
            begin = pl.multiple_of(a + where[4 + index] * CHUNK, TILE)
            square += column_norm(block(p), flat[:, pl.ds(begin, CHUNK)], flat[:, b : b + WIDE])
        squares.append(square)
    return jnp.concatenate(squares, axis=1)


def wide_first_kernel(spans, where, a, ax, b, by, flat, squares):
    blocks = eight(a, ax, None, b, by, None)
    squares[...] = wide_squares(spans, where, [blocks[k] for k in (0, 1, 4, 5)], (0, 1, 4, 5), flat)


def wide_norm_kernel(spans, where, y2, x2, flat, mags, squares, stats):
    blocks = eight(None, None, y2, None, None, x2)
    total = squares[...] + wide_squares(spans, where, [blocks[k] for k in (2, 3, 6, 7)], (2, 3, 6, 7), flat)
    for p in range(2):
        lanes = slice(p * WIDE, (p + 1) * WIDE)
        norm = jnp.sqrt(total[:, lanes] + column_eps)
        first = 4 * D + p * FF + where[2] * (2 * FF // N_MP) + where[3] * (WIDE - TILE)
        magnitude = mags[:, pl.ds(pl.multiple_of(first, TILE), WIDE)]
        stats[0:1, lanes] = magnitude / norm
        stats[1:2, lanes] = norm
        stats[2:3, lanes] = magnitude


def row_norm_kernel(spans, w_out, w_down, flat, squares):
    for row, (p, weights) in enumerate(((3, w_out[...]), (6, w_down[...]))):
        a, size = spans[("A", p)]
        b = spans[("B", p)][0]
        squares[row : row + 1, :] = column_norm(weights, flat[:, a : a + size], flat[:, b : b + D])


def down_back_kernel(spans, where, cotangent, scale, w_down, flat, d_act, grad_b, through, padded):
    a, size = spans[("A", 6)]
    b = spans[("B", 6)][0]
    grad = (cotangent[...].astype(f32) * scale[...]).astype(bf16)
    grad_b[...] = grad
    low = dora_scale * mm_t(grad, flat[:, b : b + D])
    through[...] = low
    padded[...] = jnp.zeros_like(padded)
    padded[:, 0:size] = mm_t(grad, w_down[...]) + mm2(low, flat[:, a : a + size])
    value = padded[...]
    d_act[...] = jnp.where(where[3] == 0, value, pltpu.roll(value, FILL, 1))


def middle_kernel(spans, where, p0, p1, p2, p3, p4, p5, p6, p7, b0, b1, b2, b3, b4, b5, d_act, flat, stats,
                  send, keep, x, act, grads, throughs, lows, dots, part, mixed):
    blocks = eight(b0, b1, b2, b3, b4, b5)
    join_rows(where, (p0, p1, p2, p3, p4, p5, p6, p7), x)
    la = [spans[("A", 4 + p)][0] for p in range(2)]
    lb = [spans[("B", 4 + p)][0] for p in range(2)]
    uppers = [flat[:, b : b + WIDE] for b in lb]
    low = mm_t(x[...], twice([flat[:, a : a + D] for a in la]))
    lows[...] = low
    low = high_low(low)
    for p in range(2):
        total = dora_scale * mm(low, only(uppers[p], p, 2))
        for index, block in enumerate(blocks):
            total += mm(x[:, at(where[4 + index], CHUNK)], block(p))
        mixed[:, p * WIDE : (p + 1) * WIDE] = total
    lanes = lax.broadcasted_iota(jnp.int32, d_act.shape, 1) - where[3] * FILL
    used = jnp.logical_and(lanes >= 0, lanes < WIDE - FILL)
    gate = mixed[:, :WIDE] * stats[0:1, :WIDE]
    upward = mixed[:, WIDE:] * stats[0:1, WIDE:]
    sigmoid_gate = jax.nn.sigmoid(gate)
    silu = gate * sigmoid_gate
    act[...] = jnp.where(used, silu * upward, 0.0).astype(bf16)
    back = jnp.where(used, d_act[...], 0.0)
    grad = back * upward * sigmoid_gate * (1.0 + gate * (1.0 - sigmoid_gate))
    dots[0:1, :WIDE] = jnp.sum(grad * mixed[:, :WIDE], axis=0, keepdims=True)
    grads[:, :WIDE] = (grad * stats[0:1, :WIDE]).astype(bf16)
    grad = back * silu
    dots[0:1, WIDE:] = jnp.sum(grad * mixed[:, WIDE:], axis=0, keepdims=True)
    grads[:, WIDE:] = (grad * stats[0:1, WIDE:]).astype(bf16)
    through = dora_scale * (
        mm_t(grads[:, :WIDE], only(uppers[0], 0, 2)) + mm_t(grads[:, WIDE:], only(uppers[1], 1, 2))
    )
    throughs[...] = through
    through = high_low(through)
    for index, block in enumerate(blocks):
        chunk = where[4 + index]
        lowers = [flat[:, pl.ds(pl.multiple_of(a + chunk * CHUNK, TILE), CHUNK)] for a in la]
        total = mm(through, twice(lowers))
        for p in range(2):
            total += mm_t(grads[:, p * WIDE : (p + 1) * WIDE], block(p))
        part[:, at(chunk, CHUNK)] = total
    split_rows(where, part, send, keep, send.shape[0] // N_Z)


def down_kernel(spans, where, act, w_down, flat, cotangent, send, keep, low_out, dots, part, local):
    a, size = spans[("A", 6)]
    b = spans[("B", 6)][0]
    value = act[...].astype(f32)
    value = jnp.where(where[3] == 0, value, pltpu.roll(value, WIDE - FILL, 1))
    local[...] = value.astype(bf16)
    inputs = local[:, 0:size]
    low = mm_t(inputs, flat[:, a : a + size])
    low_out[...] = low
    part[...] = mm(inputs, w_down[...]) + dora_scale * mm2(low, flat[:, b : b + D])
    split_rows(where, part, send, keep, send.shape[0] // N_Z)
    dots[...] = jnp.sum(cotangent[...].astype(f32) * part[...], axis=0, keepdims=True)


def norm_back(value, grad, gain):
    inverse = lax.rsqrt(jnp.mean(value * value, axis=-1, keepdims=True) + norm_eps)
    scaled = grad * gain
    inner = jnp.mean(scaled * value, axis=-1, keepdims=True)
    return inverse * (scaled - value * inverse * inverse * inner)


def second_back_kernel(own, r1, r2, r3, x_two, mixed, cotangent, gains, scale, dots_d, grad_two, grad_b, dots):
    total = to_mp_order(total_of(own, r1, r2, r3))
    grad = cotangent[...].astype(f32) + norm_back(x_two[...], total, gains[1:2, :])
    grad_two[...] = grad
    grad_b[0 : grad.shape[0]] = (grad * scale[...]).astype(bf16)
    own = jnp.sum(grad * mixed[...], axis=0, keepdims=True)
    dots[...] = own
    grad_b[grad.shape[0] :] = thirds(own, dots_d[...])


def last_rows_kernel(own, r1, r2, r3, tokens, grad_two, gains, own_d, d1, d2, d3, x_two, scale, out):
    share = own.shape[0]
    total = to_mp_order(total_of(own, r1, r2, r3))
    value = tokens[...].astype(f32)
    out[0:share] = (grad_two[...] + norm_back(value, total, gains[0:1, :])).astype(bf16)
    out[share:] = (x_two[...] + total_of(own_d, d1, d2, d3) * scale[...]).astype(bf16)


def attention_back_kernel(spans, where, p0, p1, p2, p3, p4, p5, p6, p7, b0, b1, b2, b3, b4, b5, w_out, flat,
                          cos, sin, mixed, qkv, probs, stats,
                          send, keep, grad_out, grads, throughs, through_out, dots, dots_o, dots_d, part, incoming):
    blocks = eight(b0, b1, b2, b3, b4, b5)
    width = CHUNK
    join_rows(where, (p0, p1, p2, p3, p4, p5, p6, p7), grad_out)
    sums = [jnp.zeros((1, D), f32)] * 2
    for piece in (p0, p1, p2, p3, p4, p5, p6, p7):
        for index, value in enumerate(from_thirds(piece[grad_out.shape[0] // N_MP :])):
            sums[index] = sums[index] + value
    dots_o[...], dots_d[...] = sums
    a, b = spans[("A", 3)][0], spans[("B", 3)][0]
    low = dora_scale * mm_t(grad_out[...], flat[:, b : b + D])
    through_out[...] = low
    grad_att = (mm_t(grad_out[...], w_out[...]) + mm2(low, flat[:, a : a + width])).astype(bf16)
    for head in range(width // HEAD_DIM):
        lanes = [slice(p * width + head * HEAD_DIM, p * width + (head + 1) * HEAD_DIM) for p in range(3)]
        query, keys, value = [qkv[:, one] for one in lanes]
        grad = grad_att[:, head * HEAD_DIM : (head + 1) * HEAD_DIM]
        weights = probs[head]
        grad_weights = mm_t(grad, value)
        incoming[:, lanes[2]] = mm_f(weights.astype(bf16), grad)
        centred = jnp.sum(weights * grad_weights, axis=-1, keepdims=True)
        grad_scores = (weights * (grad_weights - centred)).astype(bf16)
        grad_query = mm(grad_scores, keys) * HEAD_DIM ** (-0.5)
        grad_key = mm_f(grad_scores, query) * HEAD_DIM ** (-0.5)
        incoming[:, lanes[0]] = grad_query * cos[...] - swap64(grad_query) * sin[...]
        incoming[:, lanes[1]] = grad_key * cos[...] - swap64(grad_key) * sin[...]
    dots[...] = jnp.sum(incoming[...] * mixed[...], axis=0, keepdims=True)
    grads[...] = (incoming[...] * stats[0:1, :]).astype(bf16)
    la = [spans[("A", p)][0] for p in range(3)]
    uppers = [flat[:, spans[("B", p)][0] : spans[("B", p)][0] + width] for p in range(3)]
    through = mm_t(grads[:, :width], only(uppers[0], 0, 3))
    for p in (1, 2):
        through += mm_t(grads[:, p * width : (p + 1) * width], only(uppers[p], p, 3))
    through = dora_scale * through
    throughs[...] = through
    through = high_low(through)
    for index, block in enumerate(blocks):
        chunk = where[4 + index]
        lowers = [flat[:, pl.ds(pl.multiple_of(a + chunk * CHUNK, TILE), CHUNK)] for a in la]
        total = mm(through, twice(lowers))
        for p in range(3):
            total += mm_t(grads[:, p * width : (p + 1) * width], block(p))
        part[:, at(chunk, CHUNK)] = total
    split_rows(where, part, send, keep, send.shape[0] // N_Z)


def to_blocks(value, tiles, out, begin):
    pairs = value.shape[1] // TILE
    for index in range(pairs):
        tiles[index] = tile(value, index)
    for part in range(8):
        even, odd = merge(tiles[0:pairs, part, :], tiles[0:pairs, 8 + part, :])
        lanes = slice(part * TILE, (part + 1) * TILE)
        out[begin : begin + pairs, lanes] = even
        out[begin + pairs : begin + 2 * pairs, lanes] = odd


def column_grads_kernel(spans, projections, width, where, x, b0, b1, b2, b3, b4, b5, flat, stats, grads, throughs,
                        lows, dots, out_a, out_b, out_m, tiles, whole):
    blocks = eight(b0, b1, b2, b3, b4, b5)
    for position, p in enumerate(projections):
        a, b = spans[("A", p)][0], spans[("B", p)][0]
        lanes = slice(position * width, (position + 1) * width)
        ranks = slice(2 * position * RANK, (2 * position + 1) * RANK)
        upper = flat[:, b : b + width]
        norm = stats[1:2, lanes]
        inverse = 1.0 / norm
        e = dots[0:1, lanes]
        out_m[0:1, lanes] = e * inverse
        ratio = -e * stats[2:3, lanes] * inverse * inverse * inverse
        scaled = halves(dora_scale * upper.astype(f32) * ratio)
        through = halves(throughs[:, ranks])
        square = dora_scale * (mm_t(scaled[0], upper) + mm_t(scaled[1], upper))
        lower = flat[:, a : a + D]
        whole[...] = mm2(square, lower) + mm_f(through[0], x[...]) + mm_f(through[1], x[...])
        crossed = dora_scale * mm2(mm_t(lower, lower), upper)
        for index, block in enumerate(blocks):
            chunk = where[4 + index]
            weights = block(position)
            whole[:, at(chunk, CHUNK)] += mm_t(scaled[0], weights) + mm_t(scaled[1], weights)
            crossed += mm(flat[:, pl.ds(pl.multiple_of(a + chunk * CHUNK, TILE), CHUNK)], weights)
        to_blocks(whole[...], tiles, out_a, position * D * RANK // BLOCK)
        upper_grad = dora_scale * (mm2_f(lows[:, ranks], grads[:, lanes]) + crossed * ratio)
        to_blocks(upper_grad, tiles, out_b, position * width * RANK // BLOCK)


def row_grads_kernel(spans, p, where, x, weights_ref, flat, scale_row, norm_row, mag_row, grads, through_in, low, dots,
                     out_a, out_b, tiles, local):
    a, size = spans[("A", p)]
    b = spans[("B", p)][0]
    weights = weights_ref[...]
    inputs = x[...]
    if p == 6:
        value = inputs.astype(f32)
        value = jnp.where(where[3] == 0, value, pltpu.roll(value, WIDE - FILL, 1))
        local[...] = value.astype(bf16)
        inputs = local[:, 0:size]
    lower = flat[:, a : a + size]
    upper = flat[:, b : b + D]
    inverse = 1.0 / norm_row[...]
    ratio = -dots[...] * mag_row[...] * inverse * inverse * inverse
    scaled = halves(dora_scale * upper.astype(f32) * ratio)
    square = dora_scale * (mm_t(scaled[0], upper) + mm_t(scaled[1], upper))
    grad = mm2(square, lower) + mm2_f(through_in[...], inputs)
    grad += mm_t(scaled[0], weights) + mm_t(scaled[1], weights)
    if size % TILE:
        grad = jnp.concatenate([grad, jnp.zeros((RANK, TILE - size % TILE), f32)], axis=1)
    to_blocks(grad, tiles, out_a, 0)
    crossed = mm(lower, weights) + dora_scale * mm2(mm_t(lower, lower), upper)
    to_blocks(dora_scale * (mm2_f(low[...], grads[...]) + crossed * ratio), tiles, out_b, 0)


def pack_kernel(where, a_f, a_a, b_d, b_o, m_f, m_a, dots_o, norm_o, dots_d, norm_d, give, keep, rows, flat):
    begin = 0
    for array in (a_f, a_a, b_d, b_o):
        rows[begin : begin + array.shape[0]] = array[...]
        begin += array.shape[0]
    flat[...] = jnp.zeros_like(flat)
    for p in range(3):
        lanes = pl.ds(pl.multiple_of(p * D + where[1] * CHUNK, TILE), CHUNK)
        flat[:, lanes] = m_a[:, p * CHUNK : (p + 1) * CHUNK]
    flat[:, 3 * D : 4 * D] = dots_o[...] / norm_o[...]
    for p in range(2):
        first = 4 * D + p * FF + where[2] * (2 * FF // N_MP) + where[3] * (WIDE - TILE)
        flat[:, pl.ds(pl.multiple_of(first, TILE), WIDE)] = m_f[:, p * WIDE : (p + 1) * WIDE]
    flat[:, 4 * D + 2 * FF :] = dots_d[...] / norm_d[...]
    rows[begin:] = jnp.zeros((rows.shape[0] - begin, BLOCK), f32)
    for index in range(flat.shape[1] // BLOCK):
        rows[begin + index : begin + index + 1] = flat[:, index * BLOCK : (index + 1) * BLOCK]
    unit = rows.shape[0] // N_MP
    for line in range(N_Z):
        give[line * unit : (line + 1) * unit] = rows[at(2 * line + 1 - where[3], unit)].astype(bf16)
        keep[line * unit : (line + 1) * unit] = rows[at(2 * line + where[3], unit)]


def local_kernel(where, own, r1, r2, r3, b_f, b_a, a_d, a_o, mine, p1, p2, p3, rows):
    begin = own.shape[0]
    half = begin // 2
    for index in range(2):
        lanes = slice(index * BLOCK, (index + 1) * BLOCK)
        total = own[index * half : (index + 1) * half]
        for piece in (r1, r2, r3):
            total = total + piece[piece.shape[0] - half :, lanes].astype(f32)
        rows[index * half : (index + 1) * half] = total
    for array in (b_f, b_a, a_d, a_o):
        rows[begin : begin + array.shape[0]] = array[...]
        begin += array.shape[0]
    rows[begin:] = jnp.zeros((rows.shape[0] - begin, BLOCK), f32)
    part = mine.shape[0]
    mine[...] = rows[at(where[0], part)]
    for step, piece in ((1, p1), (2, p2), (3, p3)):
        piece[...] = rows[at(jnp.bitwise_xor(where[0], step), part)].astype(bf16)


def last_sum_kernel(own, r1, r2, r3, out):
    out[...] = total_of(own, r1, r2, r3).astype(bf16)


def update_kernel(index, mine, s0, s1, s2, s3, s4, s5, s6, s7, master, first, second, new_master, new_first, new_second):
    picked = pick(index[...], (s0, s1, s2, s3, s4, s5, s6, s7)).astype(bf16)
    grad = jnp.where(mine[...] >= COUNT_FLAT, picked.astype(f32), mm_t(picked, order_matrix()))
    grad = jnp.where(mine[...] >= 0, grad, 0.0)
    rates = jnp.where(mine[...] < COUNT_FLAT, rate_upper, rate_magnitude)
    rates = jnp.where(mine[...] < COUNT_LOWER, rate_lower, rates)
    rates = jnp.where(mine[...] < 0, 0.0, rates)
    weight = master[...]
    first_new = beta_one * first[...] + (1.0 - beta_one) * grad
    second_new = beta_two * second[...] + (1.0 - beta_two) * grad * grad
    first_hat = first_new / (1.0 - beta_one**STEP)
    second_hat = second_new / (1.0 - beta_two**STEP)
    new_master[...] = weight - rates * (
        first_hat / (jnp.sqrt(second_hat) + adam_eps) + weight_decay * weight
    )
    new_first[...] = first_new
    new_second[...] = second_new


COUNT_LOWER = RANK * (6 * D + FF) // BLOCK
COUNT_FLAT = COUNT_LOWER + RANK * (5 * D + 2 * FF) // BLOCK


def block_starts():
    starts = {}
    total = 0
    for kind, side in (("A", 0), ("B", 1)):
        for index, sizes in enumerate(proj_dims()):
            starts[(kind, index)] = total
            total += sizes[side] * RANK // BLOCK
    return starts


def fast_body(
    tokens,
    cotangent,
    norm_gains,
    w_attn,
    w_in,
    w_down,
    segments,
    owners,
    master,
    first_moment,
    second_moment,
):
    rows = tokens.shape[0]
    mi = lax.axis_index("mp")
    di = lax.axis_index("dp")
    core = mi % 2
    zi = mi // 2
    share = rows // N_MP
    capacity = master.shape[0]
    n_blocks = owners.shape[0]
    width = D // N_MP
    starts = block_starts()

    def mp_swap(values, step):
        return lax.ppermute(values, "mp", [(i, i ^ step) for i in range(N_MP)])

    def dp_swap(values, step):
        return lax.ppermute(values, "dp", [(i, i ^ step) for i in range(N_DP)])

    order = [(0, 0), (1, 0), (2, 0), (3, 0), (0, 1), (2, 1), (1, 1), (3, 1)]
    chunks = [(di ^ t) * 2 + (core ^ h) for t, h in order]
    where = jnp.stack([di, mi, zi, core] + chunks).astype(jnp.int32)

    def stack(first, second, after=()):
        shape = (2,) + first.shape
        return run(
            stack_kernel, [first, second], "hh", [shape_of(shape, bf16)], name="stack", after=after, us=0.01
        )[0]

    def plane_first(a, b):
        return a, dp_swap(a, 1), b, dp_swap(b, 2)

    def plane_second(a, ax, b, by, after=()):
        return [a, ax, dp_swap(stack(a, ax, after), 2), b, by, dp_swap(stack(b, by, after), 1)]

    def plane(a, b):
        return plane_second(*plane_first(a, b))

    sent = master.astype(bf16)
    line = [sent] + [mp_swap(sent, 2 * step) for step in range(1, N_Z)]
    first_b = plane_first(jnp.concatenate(line[:2]), jnp.concatenate(line[2:]))
    owners, segments, w_late, tokens, line_end = lax.optimization_barrier(
        (owners, segments, w_attn, tokens, first_b[2])
    )
    first_b = first_b[:2] + (line_end,) + first_b[3:]
    sheet = plane_second(*first_b)
    sheet = [one.reshape(-1, BLOCK) for one in sheet]
    features = run(
        first_norm_kernel,
        [tokens, norm_gains],
        "hh",
        [shape_of((rows, D), bf16)],
        name="first_norm",
        megabytes=6,
        us=1.2,
        after=[first_b[2]],
    )[0]
    def cut(weights, count, chip):
        pieces = []
        for index in range(N_Z):
            piece = lax.dynamic_slice(weights, (0, di * 64, (zi ^ index) * chip), (count, 64, chip))
            pieces.append(mp_swap(piece, 2 * index) if index else piece)
        return pieces

    def columns_of(pieces, size, step, name, after=()):
        count = pieces[0].shape[0]
        a, forward = run(
            functools.partial(line_kernel, step),
            [where] + pieces,
            "shhhh",
            [shape_of((count, CHUNK, size), bf16)] * 2,
            name=name,
            after=after,
        )
        return plane_first(a, mp_swap(forward, 1))

    first_a = columns_of(cut(w_attn, 3, 2 * width), width, width, "line_a", [features])
    blocks_a = plane_second(*first_a)
    sheet = run(
        join_all_kernel,
        sheet,
        "h" * 6,
        [shape_of((8 * capacity, BLOCK), bf16)] * 2,
        name="adapter_rows",
        after=[first_a[0]],
        us=0.1,
    )
    stacked = list(sheet) + [mp_swap(one, 1) for one in sheet]
    w_in_late, own_a = lax.optimization_barrier((w_in, first_a[0]))
    pieces_f = cut(w_in_late, 2, 2 * FF // N_MP)
    w_out = w_late[3]

    ranks = slot_positions(owners, 0)
    owner_d, owner_m = owners // N_MP, owners % N_MP
    piece_at = (owner_d ^ di) * N_Z + ((owner_m // 2) ^ zi)
    listed = np.array([0, 1, 8, 9, 2, 3, 12, 13, 4, 5, 10, 11, 6, 7, 14, 15], np.int32)
    piece_at = jnp.sum(jnp.where(piece_at[:, None] == np.arange(16), listed, 0), axis=1)
    slot = (((owner_m % 2) ^ core) * 16 + piece_at) * capacity + ranks
    wanted = []
    spans = {}

    def want(name, blocks, size):
        spans[name] = (sum(w.shape[0] for w in wanted) * 64, size)
        wanted.append(blocks)

    by_dp = np.array(
        [(2 * z + c) * 4 + d for d in range(N_DP) for c in range(2) for z in range(N_Z)], np.int32
    )
    all_blocks = np.arange(D * RANK // BLOCK, dtype=np.int32)
    for index in (0, 1, 2, 4, 5):
        want(("A", index), starts[("A", index)] + by_dp, D)
        if index < 3:
            want(("B", index), starts[("B", index)] + mi * 4 + np.arange(4), width)
        else:
            first_block = starts[("B", index)] + zi * 22 + core * 10
            want(("B", index), first_block + np.arange(12), WIDE)
    want(("A", 3), starts[("A", 3)] + mi * 4 + np.arange(4), width)
    want(("B", 3), starts[("B", 3)] + all_blocks, D)
    want(("A", 6), starts[("A", 6)] + mi * 11 + np.minimum(np.arange(12), 10), FF // N_MP)
    want(("B", 6), starts[("B", 6)] + all_blocks, D)
    chosen = jnp.take(slot, jnp.concatenate([jnp.asarray(w, jnp.int32) for w in wanted]))
    n_pairs = chosen.shape[0] // 2
    pairs = chosen.reshape(n_pairs, 2)
    flat, mags = run(
        adapters_kernel,
        [pairs[:, :1], pairs[:, 1:], slot[COUNT_FLAT:, None]] + stacked,
        "vvv" + "h" * len(stacked),
        [shape_of((RANK, n_pairs * TILE), bf16), shape_of((1, (n_blocks - COUNT_FLAT) * BLOCK), f32)],
        [pltpu.VMEM((n_pairs, RANK, TILE), f32)],
        name="adapters", megabytes=13, us=0.3,
    )

    def bind(kernel, *args):
        return functools.partial(kernel, spans, *args)

    def column_grads(projections, size, x, blocks, flat, stats, grads, throughs, lows, dots, after):
        count = len(projections)
        return run(
            bind(column_grads_kernel, projections, size),
            [where, x] + blocks + [flat, stats, grads, throughs, lows, dots],
            "s" + "h" * 13,
            [
                shape_of((count * D * RANK // BLOCK, BLOCK), f32),
                shape_of((count * size * RANK // BLOCK, BLOCK), f32),
                shape_of((1, count * size), f32),
            ],
            [pltpu.VMEM((D // TILE, RANK, TILE), f32), pltpu.VMEM((RANK, D), f32)],
            name="column_grads", megabytes=9, us=1,
            after=after,
        )

    def row_grads(p, x, weights, flat, scale, norm, mag, grads, through, low, dots, after):
        size = spans[("A", p)][1]
        return run(
            bind(row_grads_kernel, p),
            [where, x, weights, flat, scale, norm, mag, grads, through, low, dots],
            "s" + "h" * 10,
            [
                shape_of((-(-size // TILE) * 2, BLOCK), f32),
                shape_of((D * RANK // BLOCK, BLOCK), f32),
            ],
            [pltpu.VMEM((D // TILE, RANK, TILE), f32), pltpu.VMEM((rows, WIDE), bf16)],
            name="row_grads", megabytes=6, us=0.1,
            after=after,
        )

    row = segments[0]
    cosine, sine = rotary_tables(segment_positions(row))
    cosine, sine = cosine[:, 0], sine[:, 0]
    cos_full = jnp.concatenate([cosine, cosine], axis=-1)
    sin_full = jnp.concatenate([-sine, sine], axis=-1)
    tokens_here = lax.dynamic_slice_in_dim(tokens, mi * share, share, 0)
    cotangent_here = lax.dynamic_slice_in_dim(cotangent, mi * share, share, 0)
    half_rows = [shape_of((rows // 2, D), bf16), shape_of((rows // 2, D), f32)]

    def finish_rows(send, keep, after):
        received = mp_swap(send, 1)
        p1, p2, p3, own = run(
            pair_kernel,
            [where, keep, received],
            "shh",
            [shape_of((share, D), bf16)] * 3 + [shape_of((share, D), f32)],
            name="pair_sums", megabytes=4, us=1.2,
            after=after,
        )
        return [own, mp_swap(p1, 2), mp_swap(p2, 4), mp_swap(p3, 6)]

    def gather_rows(value):
        mine = [value] + [mp_swap(value, 2 * step) for step in range(1, N_Z)]
        return mine + [mp_swap(one, 1) for one in mine]

    squares = run(
        bind(row_norm_kernel),
        [w_out, w_down, flat],
        "hhh",
        [shape_of((2, D), f32)],
        name="row_norms",
        us=0.1,
    )[0]
    n_heads = width // HEAD_DIM
    send, keep, mixed_a, qkv, probs, att, low_a, low_o, stats_a = run(
        bind(attention_kernel),
        [where, features] + blocks_a + [w_out, flat, mags, cos_full, sin_full, segments, row[:, None], squares],
        "s" + "h" * 15,
        [shape_of((rows // 2 + 8, D), bf16), half_rows[1]]
        + [
            shape_of((rows, 3 * width), f32),
            shape_of((rows, 3 * width), bf16),
            shape_of((n_heads, rows, rows), f32),
            shape_of((rows, width), bf16),
            shape_of((rows, 6 * RANK), f32),
            shape_of((rows, RANK), f32),
            shape_of((8, 3 * width), f32),
        ],
        [pltpu.VMEM((rows, D), f32)],
        name="attention",
        megabytes=13,
        us=10,
    )

    p1, p2, p3, own_o, more_o = run(
        pair_more_kernel,
        [where, keep, mp_swap(send, 1), squares],
        "shhh",
        [shape_of((share + 8, D), bf16)] * 3 + [shape_of((share, D), f32), shape_of((2, D), f32)],
        name="pair_sums",
        us=1.2,
    )
    sums_o = [mp_swap(p1, 2), mp_swap(p2, 4), mp_swap(p3, 6)]
    first_f = columns_of(pieces_f, WIDE, WIDE - TILE, "line_f")
    blocks_f = plane_second(*first_f, after=sums_o[1:2])
    row_of = shape_of((1, D), f32)
    x_two, mixed_o, features_two, scale_o, norm_o, scale_d, norm_d = run(
        second_norm_kernel,
        [own_o, more_o] + sums_o + [tokens_here, norm_gains, mags],
        "h" * 8,
        [shape_of((share, D), f32)] * 2 + [shape_of((share, D), bf16)] + [row_of] * 4,
        name="second_norm",
        us=0.5,
    )
    mag_o = mags[:, 3 * D : 4 * D]
    mag_d = mags[:, 4 * D + 2 * FF :]
    pieces = gather_rows(features_two)
    squares_f = run(
        bind(wide_first_kernel),
        [where] + [blocks_f[k] for k in (0, 1, 3, 4)] + [flat],
        "s" + "h" * 5,
        [shape_of((1, 2 * WIDE), f32)],
        name="wide_squares", megabytes=8, us=3,
        after=[pieces[1]],
    )[0]
    d_act, grad_d, through_d = run(
        bind(down_back_kernel),
        [where, cotangent, scale_d, w_down, flat],
        "shhhh",
        [shape_of((rows, WIDE), f32), shape_of((rows, D), bf16), shape_of((rows, RANK), f32)],
        [pltpu.VMEM((rows, WIDE), f32)],
        name="down_back", megabytes=7, us=3.5,
        after=[squares_f],
    )
    stats_f = run(
        bind(wide_norm_kernel),
        [where] + [blocks_f[k] for k in (2, 5)] + [flat, mags, squares_f],
        "s" + "h" * 5,
        [shape_of((8, 2 * WIDE), f32)],
        name="wide_norms", megabytes=8, us=3,
        after=[through_d],
    )[0]
    send, keep, x_f, act, grads_f, through_f, low_f, dots_f = run(
        bind(middle_kernel),
        [where] + pieces + blocks_f + [d_act, flat, stats_f],
        "s" + "h" * 17,
        half_rows
        + [
            shape_of((rows, D), bf16),
            shape_of((rows, WIDE), bf16),
            shape_of((rows, 2 * WIDE), bf16),
            shape_of((rows, 4 * RANK), f32),
            shape_of((rows, 4 * RANK), f32),
            shape_of((1, 2 * WIDE), f32),
        ],
        [pltpu.VMEM((rows, D), f32), pltpu.VMEM((rows, 2 * WIDE), f32)],
        name="feed_forward", megabytes=22, us=14,
    )
    send_d, keep_d, low_d, dots_d = run(
        bind(down_kernel),
        [where, act, w_down, flat, cotangent],
        "shhhh",
        half_rows + [shape_of((rows, RANK), f32), shape_of((1, D), f32)],
        [pltpu.VMEM((rows, D), f32), pltpu.VMEM((rows, WIDE), bf16)],
        name="down", megabytes=9, us=3.5,
    )
    sums = finish_rows(send, keep, [low_d])
    a_f, b_f, m_f = column_grads(
        (4, 5), WIDE, x_f, blocks_f, flat, stats_f, grads_f, through_f, low_f, dots_f, [sums[1]]
    )
    grad_two, grad_o_piece, dots_o = run(
        second_back_kernel,
        sums + [x_two, mixed_o, cotangent_here, norm_gains, scale_o, dots_d],
        "h" * 10,
        [shape_of((share, D), f32), shape_of((share + 8, D), bf16), row_of],
        name="second_norm_back", megabytes=3, us=0.5,
        after=[m_f],
    )
    pieces_o = gather_rows(grad_o_piece)
    sums_d = finish_rows(send_d, keep_d, [pieces_o[0], pieces_o[7]])
    send, keep, grad_o, grads_a, through_a, through_o, dots_a, dots_all_o, dots_all_d = run(
        bind(attention_back_kernel),
        [where] + pieces_o + blocks_a + [w_out, flat, cos_full, sin_full, mixed_a, qkv, probs, stats_a],
        "s" + "h" * 22,
        half_rows
        + [
            shape_of((rows, D), bf16),
            shape_of((rows, 3 * width), bf16),
            shape_of((rows, 6 * RANK), f32),
            shape_of((rows, RANK), f32),
            shape_of((1, 3 * width), f32),
            row_of,
            row_of,
        ],
        [pltpu.VMEM((rows, D), f32), pltpu.VMEM((rows, 3 * width), f32)],
        name="attention_back",
        megabytes=10,
        us=0.1,
        after=[sums_d[0]],
    )
    a_o, b_o = row_grads(
        3, att, w_out, flat, scale_o, norm_o, mag_o, grad_o, through_o, low_o, dots_all_o, []
    )
    a_a, b_a, m_a = column_grads(
        (0, 1, 2), width, features, blocks_a, flat, stats_a, grads_a, through_a, low_a, dots_a, [a_o]
    )
    a_d, b_d = row_grads(
        6, act, w_down, flat, scale_d, norm_d, mag_d, grad_d, through_d, low_d, dots_all_d, [m_a]
    )
    unit, part = 32, 24
    give, kept = run(
        pack_kernel,
        [where, a_f, a_a, b_d, b_o, m_f, m_a, dots_o, norm_o, dots_d, norm_d],
        "s" + "h" * 10,
        [shape_of((N_Z * unit, BLOCK), bf16), shape_of((N_Z * unit, BLOCK), f32)],
        [pltpu.VMEM((N_MP * unit, BLOCK), f32), pltpu.VMEM((1, (n_blocks - COUNT_FLAT) * BLOCK), f32)],
        name="pack",
    )
    p1, p2, p3, own = run(
        pair_kernel,
        [where, kept, mp_swap(give, 1)],
        "shh",
        [shape_of((unit, BLOCK), bf16)] * 3 + [shape_of((unit, BLOCK), f32)],
        name="pack_sums",
        us=0.1,
    )
    p1, p2, p3, own, own_grads = run(
        pair_grads_kernel,
        [where, keep, mp_swap(send, 1), kept, mp_swap(give, 1)],
        "shhhh",
        [shape_of((share + unit // 2, D), bf16)] * 3 + [shape_of((share, D), f32), shape_of((unit, BLOCK), f32)],
        name="pair_grads",
        us=1.2,
    )
    sums = [own, mp_swap(p1, 2), mp_swap(p2, 4), mp_swap(p3, 6)]
    local_own, p1, p2, p3 = run(
        local_kernel,
        [where, own_grads] + sums[1:] + [b_f, b_a, a_d, a_o],
        "s" + "h" * 8,
        [shape_of((part, BLOCK), f32)] + [shape_of((part, BLOCK), bf16)] * 3,
        [pltpu.VMEM((N_DP * part, BLOCK), f32)],
        name="local_sums",
        us=0.1,
    )
    own = run(
        last_sum_kernel,
        [local_own, dp_swap(p1, 1), dp_swap(p2, 2), dp_swap(p3, 3)],
        "hhhh",
        [shape_of((part, BLOCK), bf16)],
        name="last_sums",
        us=0.1,
    )[0]
    last_piece = run(
        last_rows_kernel,
        sums + [tokens_here, grad_two, norm_gains] + sums_d + [x_two, scale_d],
        "h" * 13,
        [shape_of((2 * share, D), bf16)],
        name="last_rows",
        us=20,
    )[0]
    lines = jnp.concatenate([own] + [mp_swap(own, 2 * step) for step in range(1, N_Z)])
    summed = [lines] + [dp_swap(lines, step) for step in range(1, N_DP)]
    summed = summed + [mp_swap(one, 1) for one in summed]

    second = mp_swap(last_piece, 4)
    pieces = [last_piece, mp_swap(last_piece, 2), second, mp_swap(second, 2)]
    pieces = pieces + [mp_swap(one, 1) for one in pieces]
    input_grad, layer_out = run(
        join_kernel,
        [where] + pieces,
        "s" + "h" * 8,
        [shape_of((rows, D), f32), shape_of((rows, D), bf16)],
        name="join_rows",
        megabytes=8,
        us=0.1,
    )

    table = np.zeros((n_blocks,), np.int32)

    def note(block, m, r):
        table[block] = ((r // part) * N_MP + m) * 64 + r % part

    def split_pairs(count, r):
        return r // 2 + (r % 2) * (count // 2)

    def blocks_of(names):
        def listing(count, m):
            each = count // len(names)
            for position, blocks in enumerate(names):
                for k, block in enumerate(blocks(m)):
                    if block is not None:
                        yield position * each + split_pairs(each, k), block

        return listing

    def lower_columns(p):
        return lambda m: [starts[("A", p)] + int(k) for k in by_dp]

    def upper_rows(p):
        return lambda m: [starts[("B", p)] + int(k) for k in all_blocks]

    def lower_rows(p, per):
        return lambda m: [starts[("A", p)] + m * per + k for k in range(per)]

    def upper_columns(p):
        if p < 3:
            return lambda m: [starts[("B", p)] + m * 4 + k for k in range(4)]
        return lambda m: [
            starts[("B", p)] + (m // 2) * 22 + (m % 2) * 10 + k
            if (k < 11 if m % 2 == 0 else k >= 1)
            else None
            for k in range(12)
        ]

    begin = 0
    for listing, count in (
        (blocks_of([lower_columns(4), lower_columns(5)]), a_f.shape[0]),
        (blocks_of([lower_columns(p) for p in range(3)]), a_a.shape[0]),
        (blocks_of([upper_rows(6)]), b_d.shape[0]),
        (blocks_of([upper_rows(3)]), b_o.shape[0]),
        (lambda count, m: [(r, COUNT_FLAT + r) for r in range(count)], n_blocks - COUNT_FLAT),
    ):
        for r, block in listing(count, None):
            note(block, (begin + r) // unit, (begin + r) % unit)
        begin += count
    begin = unit
    for listing, count in (
        (blocks_of([upper_columns(4), upper_columns(5)]), b_f.shape[0]),
        (blocks_of([upper_columns(p) for p in range(3)]), b_a.shape[0]),
        (blocks_of([lower_rows(6, 11)]), a_d.shape[0]),
        (blocks_of([lower_rows(3, 4)]), a_o.shape[0]),
    ):
        for m in range(N_MP):
            for r, block in listing(count, m):
                note(block, m, begin + r)
        begin += count
    me = di * N_MP + mi
    hits = (owners * capacity + ranks)[None, :] == me * capacity + jnp.arange(capacity)[:, None]
    mine = jnp.sum(jnp.where(hits, jnp.arange(n_blocks)[None, :] + 1, 0), axis=1) - 1
    code = jnp.sum(jnp.where(hits, jnp.asarray(table)[None, :], 0), axis=1)
    device, inner = code // 64, code % 64
    d_from, m_from = device // N_MP, device % N_MP
    list_at = (((m_from % 2) ^ core) * N_DP + (d_from ^ di)) * N_Z + ((m_from // 2) ^ zi)
    index = list_at * part + inner
    new_master, new_first, new_second = run(
        update_kernel,
        [index[:, None], mine[:, None]] + summed + [master, first_moment, second_moment],
        "vv" + "h" * 11,
        [shape_of(master.shape, f32)] * 3,
        name="update", megabytes=4, us=2,
    )
    return (layer_out, input_grad, new_master, new_first, new_second)


def solution(mesh):
    fast = mesh.shape["dp"] == 4 and mesh.shape["mp"] == 8
    return jax.shard_map(
        fast_body if fast else body,
        mesh=mesh,
        in_specs=(
            P("dp", None),
            P("dp", None),
            P(),
            P(None, "mp", None),
            P(None, "mp", None),
            P("mp", None),
            P("dp", None),
            P(),
            P(("dp", "mp"), None),
            P(("dp", "mp"), None),
            P(("dp", "mp"), None),
        ),
        out_specs=(
            P("dp", None),
            P("dp", None),
            P(("dp", "mp"), None),
            P(("dp", "mp"), None),
            P(("dp", "mp"), None),
        ),
        check_vma=False,
    )
```

```python
import functools

import jax
import jax.numpy as jnp
import numpy as np
from jax import lax
from jax.experimental import pallas as pl
from jax.experimental.pallas import tpu as pltpu
from jax.sharding import PartitionSpec as P

D = 2048
FF = 5632
HEADS = 16
HEAD_DIM = 128
RANK = 16
BLOCK = 1024
STEP = 5


dora_scale = 2.0
rope_base = 10000.0
norm_eps = 1e-05
column_eps = 1e-06
beta_one = 0.5
beta_two = 0.5
adam_eps = 1e-08
weight_decay = 0.01
rate_lower = 0.02
rate_upper = 0.1
rate_magnitude = 1.0
highest = lax.Precision.HIGHEST


def proj_dims():
    return [(D, D), (D, D), (D, D), (D, D), (D, FF), (D, FF), (FF, D)]


def unpack(flat):
    offset = 0
    lowers = []
    for inner, outer in proj_dims():
        lowers.append(flat[offset : offset + inner * RANK].reshape(inner, RANK))
        offset += inner * RANK
    uppers = []
    for inner, outer in proj_dims():
        uppers.append(flat[offset : offset + outer * RANK].reshape(outer, RANK))
        offset += outer * RANK
    magnitudes = []
    for inner, outer in proj_dims():
        magnitudes.append(flat[offset : offset + outer])
        offset += outer
    return (lowers, uppers, magnitudes)


def slot_positions(owners, capacity):
    order = jnp.arange(owners.shape[0], dtype=jnp.int32)
    same = (owners[:, None] == owners[None, :]) & (order[None, :] < order[:, None])
    ranks = jnp.sum(same.astype(jnp.int32), axis=1)
    return owners * capacity + ranks


def block_rates(block_ids):
    count_lower = RANK * (6 * D + FF) // BLOCK
    count_upper = RANK * (5 * D + 2 * FF) // BLOCK
    rates = jnp.where(block_ids < count_lower + count_upper, rate_upper, rate_magnitude)
    rates = jnp.where(block_ids < count_lower, rate_lower, rates)
    return jnp.where(block_ids < 0, 0.0, rates).astype(jnp.float32)


def adam_update(weight, grad, first, second, rates):
    first_new = beta_one * first + (1.0 - beta_one) * grad
    second_new = beta_two * second + (1.0 - beta_two) * grad * grad
    first_hat = first_new / (1.0 - beta_one**STEP)
    second_hat = second_new / (1.0 - beta_two**STEP)
    weight_new = weight - rates[:, None] * (
        first_hat / (jnp.sqrt(second_hat) + adam_eps) + weight_decay * weight
    )
    return (weight_new, first_new, second_new)


def rms_norm(values, gain):
    return values * lax.rsqrt(jnp.mean(values * values, axis=-1, keepdims=True) + norm_eps) * gain


def rms_back(values, grad, gain):
    inverse = lax.rsqrt(jnp.mean(values * values, axis=-1, keepdims=True) + norm_eps)
    scaled = grad * gain
    return inverse * (
        scaled - values * inverse * inverse * jnp.mean(scaled * values, axis=-1, keepdims=True)
    )


def segment_positions(row):
    order = jnp.arange(row.shape[0], dtype=jnp.int32)
    change = jnp.concatenate([jnp.ones((1,), dtype=bool), row[1:] != row[:-1]])
    starts = lax.cummax(jnp.where(change, order, 0), axis=0)
    return order - starts


def rotary_tables(positions):
    half = HEAD_DIM // 2
    freqs = rope_base ** (-(jnp.arange(half).astype(jnp.float32) * 2.0 / HEAD_DIM))
    angles = positions.astype(jnp.float32)[:, None] * freqs[None, :]
    return (jnp.cos(angles)[:, None, :], jnp.sin(angles)[:, None, :])


def rotate(values, cosine, sine):
    half = values.shape[-1] // 2
    first_half = values[..., :half]
    second_half = values[..., half:]
    return jnp.concatenate(
        [first_half * cosine - second_half * sine, second_half * cosine + first_half * sine],
        axis=-1,
    )


def unrotate(values, cosine, sine):
    half = values.shape[-1] // 2
    first_half = values[..., :half]
    second_half = values[..., half:]
    return jnp.concatenate(
        [first_half * cosine + second_half * sine, second_half * cosine - first_half * sine],
        axis=-1,
    )


def body(
    tokens,
    cotangent,
    norm_gains,
    w_attn,
    w_in,
    w_down,
    segments,
    owners,
    master,
    first_moment,
    second_moment,
):
    group_rows = tokens.shape[0]
    model_size = lax.axis_size("mp")
    model_index = lax.axis_index("mp")
    share = group_rows // model_size
    share_start = model_index * share
    capacity = master.shape[0]
    everyone = lax.axis_size(("dp", "mp"))
    score_scale = HEAD_DIM ** (-0.5)
    widths = [outer for inner, outer in proj_dims()]
    slot_index = slot_positions(owners, capacity)
    copies = lax.all_gather(master.astype(jnp.bfloat16), ("dp", "mp"), axis=0, tiled=True)
    lowers, uppers, magnitudes = unpack(jnp.take(copies, slot_index, axis=0).reshape(-1))
    frozen = [w_attn[0], w_attn[1], w_attn[2], w_attn[3], w_in[0], w_in[1], w_down]
    lower_local = []
    combined = []
    square_parts = []
    for index in range(7):
        rows_here = frozen[index].shape[0]
        piece = lax.dynamic_slice_in_dim(lowers[index], model_index * rows_here, rows_here, 0)
        lower_local.append(piece)
        joined = frozen[index].astype(jnp.float32) + dora_scale * jnp.dot(
            piece.astype(jnp.float32), uppers[index].astype(jnp.float32).T, precision=highest
        )
        combined.append(joined)
        square_parts.append(jnp.sum(joined * joined, axis=0))

    def rows_of(values):
        return lax.dynamic_slice_in_dim(values, share_start, share, 0)

    def split_parts(values, indices, axis):
        pieces = []
        offset = 0
        for index in indices:
            pieces.append(lax.slice_in_dim(values, offset, offset + widths[index], axis=axis))
            offset += widths[index]
        return pieces

    norms = [None] * 7
    mixed_share = [None] * 7
    low_share = [None] * 7
    mixed_full = [None] * 7
    grads = [None] * 7

    def set_scales(indices):
        summed = lax.psum(jnp.concatenate([square_parts[index] for index in indices]), "mp")
        squares = split_parts(summed, indices, 0)
        for index, value in zip(indices, squares):
            norms[index] = jnp.sqrt(value + column_eps)

    def scale(index):
        return magnitudes[index].astype(jnp.float32) / norms[index]

    def local_partials(inputs_local, indices):
        mixed_list = []
        low_list = []
        for index in indices:
            low_part = jnp.dot(inputs_local, lower_local[index], preferred_element_type=jnp.float32)
            mixed = jnp.dot(
                inputs_local, frozen[index], preferred_element_type=jnp.float32
            ) + dora_scale * jnp.dot(
                low_part, uppers[index].astype(jnp.float32).T, precision=highest
            )
            mixed_list.append(mixed)
            low_list.append(low_part)
        return (
            inputs_local,
            jnp.concatenate(mixed_list, axis=1),
            jnp.concatenate(low_list, axis=1),
        )

    def group_partials(inputs_b, indices):
        rows_here = frozen[indices[0]].shape[0]
        inputs_local = lax.dynamic_slice_in_dim(inputs_b, model_index * rows_here, rows_here, 1)
        return local_partials(inputs_local, indices)

    def finish(indices, local_mixed, local_low):
        summed_mixed, summed_low = lax.psum((local_mixed, local_low), "mp")
        pieces = split_parts(summed_mixed, indices, 1)
        for position, index in enumerate(indices):
            mixed_full[index] = pieces[position]
            mixed_share[index] = rows_of(pieces[position])
            low_share[index] = rows_of(summed_low[:, position * RANK : (position + 1) * RANK])
        return pieces

    def gather_inputs(local):
        return lax.all_gather(local, "mp", axis=1, tiled=True)

    xf = tokens.astype(jnp.float32)
    row = segments[0]
    cosine, sine = rotary_tables(segment_positions(row))
    order = jnp.arange(group_rows)
    allowed = (row[:, None] == row[None, :]) & (order[None, :] <= order[:, None])
    features = rms_norm(xf, norm_gains[0]).astype(jnp.bfloat16)
    first_local, first_mixed, first_low = group_partials(features, (0, 1, 2))
    set_scales((0, 1, 2))
    summed_mixed, summed_low = lax.psum((first_mixed, first_low), "mp")
    pieces = split_parts(summed_mixed, (0, 1, 2), 1)
    heads_in = []
    for index in range(3):
        mixed_full[index] = pieces[index]
        mixed_share[index] = rows_of(pieces[index])
        low_share[index] = rows_of(summed_low[:, index * RANK : (index + 1) * RANK])
        projected = (pieces[index] * scale(index)).reshape(group_rows, HEADS, HEAD_DIM)
        if index < 2:
            projected = rotate(projected, cosine, sine)
        heads_in.append(projected.astype(jnp.bfloat16))
    query_b, key_b, value_b = heads_in

    def attention_scores(query_h, key_h):
        scores = (
            jnp.einsum("thd,shd->hts", query_h, key_h, preferred_element_type=jnp.float32)
            * score_scale
        )
        return jnp.where(allowed[None], scores, -1e30)

    scores = attention_scores(query_b, key_b)
    top = jnp.max(scores, axis=-1, keepdims=True)
    expd = jnp.exp(scores - top)
    total = jnp.sum(expd, axis=-1, keepdims=True)
    probs = (expd / total).astype(jnp.bfloat16)
    attended_h = jnp.einsum("hts,shd->thd", probs, value_b, preferred_element_type=jnp.float32)
    attended_h, log_total = (attended_h, top + jnp.log(total))
    attended = attended_h.reshape(group_rows, D).astype(jnp.bfloat16)
    out_local, out_mixed, out_low = group_partials(attended, (3,))
    set_scales((3,))
    x_two = xf + finish((3,), out_mixed, out_low)[0] * scale(3)
    second_features = rms_norm(x_two, norm_gains[1]).astype(jnp.bfloat16)
    ffn_local, ffn_mixed, ffn_low = group_partials(second_features, (4, 5))
    set_scales((4, 5))
    gate_pre, up_pre = finish((4, 5), ffn_mixed, ffn_low)
    gate = gate_pre * scale(4)
    upward = up_pre * scale(5)
    sigmoid_gate = jax.nn.sigmoid(gate)
    act = (gate * sigmoid_gate * upward).astype(jnp.bfloat16)
    down_local, down_mixed, down_low = group_partials(act, (6,))
    set_scales((6,))
    down_pre = finish((6,), down_mixed, down_low)[0]
    layer_out = (x_two + down_pre * scale(6)).astype(jnp.bfloat16)

    def whole_dot(index, grad):
        return jnp.sum(grad * mixed_full[index], axis=0)

    def project_back(index, grad, inputs_local, group_dot):
        norm = norms[index]
        magnitude = magnitudes[index].astype(jnp.float32)
        grad_b = (grad * (magnitude / norm)).astype(jnp.bfloat16)
        share_dot = jnp.sum(rows_of(grad) * mixed_share[index], axis=0)
        grad_full = combined[index] * (-group_dot * magnitude / (norm * norm * norm))[None, :]
        upper_f = uppers[index].astype(jnp.float32)
        lower_f = lower_local[index].astype(jnp.float32)
        through = dora_scale * jnp.dot(grad_b, uppers[index], preferred_element_type=jnp.float32)
        grad_lower = jnp.dot(
            inputs_local.astype(jnp.float32).T, through, precision=highest
        ) + dora_scale * jnp.dot(grad_full, upper_f, precision=highest)
        grad_upper = dora_scale * jnp.dot(
            rows_of(grad_b).astype(jnp.float32).T, low_share[index], precision=highest
        ) + dora_scale * jnp.dot(grad_full.T, lower_f, precision=highest)
        grads[index] = (grad_lower, grad_upper, share_dot / norm)
        return jnp.dot(grad_b, frozen[index].T, preferred_element_type=jnp.float32) + jnp.dot(
            through, lower_f.T, precision=highest
        )

    grad_out = cotangent.astype(jnp.float32)
    grad_act = gather_inputs(project_back(6, grad_out, down_local, whole_dot(6, grad_out)))
    grad_gate = grad_act * upward * sigmoid_gate * (1.0 + gate * (1.0 - sigmoid_gate))
    grad_up = grad_act * gate * sigmoid_gate
    ffn_back = project_back(4, grad_gate, ffn_local, whole_dot(4, grad_gate)) + project_back(
        5, grad_up, ffn_local, whole_dot(5, grad_up)
    )
    grad_two = grad_out + rms_back(x_two, gather_inputs(ffn_back), norm_gains[1])
    grad_att = gather_inputs(project_back(3, grad_two, out_local, whole_dot(3, grad_two)))
    grad_att = grad_att.astype(jnp.bfloat16).reshape(group_rows, HEADS, HEAD_DIM)
    weights = jnp.exp(attention_scores(query_b, key_b) - log_total)
    weights_b = weights.astype(jnp.bfloat16)
    grad_weights = jnp.einsum("thd,shd->hts", grad_att, value_b, preferred_element_type=jnp.float32)
    grad_value = jnp.einsum("hts,thd->shd", weights_b, grad_att, preferred_element_type=jnp.float32)
    centred = jnp.sum(weights * grad_weights, axis=-1, keepdims=True)
    grad_scores = (weights * (grad_weights - centred)).astype(jnp.bfloat16)
    grad_query = (
        jnp.einsum("hts,shd->thd", grad_scores, key_b, preferred_element_type=jnp.float32)
        * score_scale
    )
    grad_key = (
        jnp.einsum("hts,thd->shd", grad_scores, query_b, preferred_element_type=jnp.float32)
        * score_scale
    )
    grad_query, grad_key, grad_value = (
        unrotate(grad_query, cosine, sine),
        unrotate(grad_key, cosine, sine),
        grad_value,
    )
    incoming = [
        grad_query.reshape(group_rows, D),
        grad_key.reshape(group_rows, D),
        grad_value.reshape(group_rows, D),
    ]
    group_dots = [whole_dot(index, incoming[index]) for index in range(3)]
    first_back = project_back(0, incoming[0], first_local, group_dots[0])
    first_back = first_back + project_back(1, incoming[1], first_local, group_dots[1])
    first_back = first_back + project_back(2, incoming[2], first_local, group_dots[2])
    input_grad = grad_two + rms_back(xf, gather_inputs(first_back), norm_gains[0])
    pieces = []
    for index in range(7):
        rows_total = proj_dims()[index][0]
        grad_lower = grads[index][0]
        placed = lax.dynamic_update_slice_in_dim(
            jnp.zeros((rows_total, RANK), jnp.float32),
            grad_lower,
            model_index * grad_lower.shape[0],
            0,
        )
        pieces.append(placed.reshape(-1))
    for index in range(7):
        pieces.append(grads[index][1].reshape(-1))
    for index in range(7):
        pieces.append(grads[index][2])
    blocks = jnp.concatenate(pieces).reshape(-1, BLOCK)
    buffer = jnp.zeros((capacity * everyone, BLOCK), jnp.float32).at[slot_index].set(blocks)
    owned = lax.psum_scatter(buffer, ("dp", "mp"), scatter_dimension=0, tiled=True)
    slot_block = (
        jnp.full((capacity * everyone,), -1, jnp.int32)
        .at[slot_index]
        .set(jnp.arange(blocks.shape[0], dtype=jnp.int32))
    )
    local_blocks = lax.dynamic_slice_in_dim(
        slot_block, lax.axis_index(("dp", "mp")) * capacity, capacity, 0
    )
    new_master, new_first, new_second = adam_update(
        master, owned, first_moment, second_moment, block_rates(local_blocks)
    )
    return (layer_out, input_grad, new_master, new_first, new_second)


f32 = jnp.float32
bf16 = jnp.bfloat16
VM = pl.BlockSpec(memory_space=pltpu.VMEM)
SM = pl.BlockSpec(memory_space=pltpu.SMEM)
ANY = pl.BlockSpec(memory_space=pl.ANY)
HBM = pl.BlockSpec(memory_space=pltpu.HBM)
TILE = 128
CHUNK = 256
N_DP = 4
N_MP = 8
N_Z = 4
WIDE = 768
FILL = 64


def mm(left, right):
    return lax.dot_general(left, right, (((1,), (0,)), ((), ())), preferred_element_type=f32)


def mm_t(left, right):
    return lax.dot_general(left, right, (((1,), (1,)), ((), ())), preferred_element_type=f32)


def mm_f(left, right):
    return lax.dot_general(left, right, (((0,), (0,)), ((), ())), preferred_element_type=f32)


def halves(value):
    high = value.astype(bf16)
    return high, (value - high.astype(f32)).astype(bf16)


def mm2(left, right):
    high, low = halves(left)
    return mm(high, right) + mm(low, right)


def mm2_t(left, right):
    high, low = halves(left)
    return mm_t(high, right) + mm_t(low, right)


def mm2_f(left, right):
    high, low = halves(left)
    return mm_f(high, right) + mm_f(low, right)


def twice(parts):
    return jnp.concatenate([part for one in parts for part in (one, one)], axis=0)


def only(part, position, count):
    zero = jnp.zeros_like(part)
    return twice([part if index == position else zero for index in range(count)])


def high_low(value):
    high = value.astype(bf16).astype(f32)
    lanes = lax.broadcasted_iota(jnp.int32, value.shape, 1)
    return jnp.where(jnp.bitwise_and(lanes, RANK) == 0, high, value - high).astype(bf16)


def swap64(value):
    return pltpu.roll(value, 64, 1)


def low_lanes(rows):
    return lax.broadcasted_iota(jnp.int32, (rows, TILE), 1) < 64


def merge(first, second):
    low = low_lanes(first.shape[0])
    return (
        jnp.where(low, first, swap64(second)),
        jnp.where(low, swap64(first), second),
    )


def tile(value, index):
    return value[:, index * TILE : (index + 1) * TILE]


def to_dp_order(value):
    out = [None] * 16
    for core in range(2):
        for pair in range(2):
            for part in range(2):
                first = 8 * pair + 2 * core + part
                low, high = merge(tile(value, first), tile(value, first + 4))
                out[8 * part + 2 * core + pair] = low
                out[8 * part + 4 + 2 * core + pair] = high
    return jnp.concatenate(out, axis=1)


def to_mp_order(value):
    out = [None] * 16
    for core in range(2):
        for pair in range(2):
            for part in range(2):
                first = 8 * part + 2 * core + pair
                low, high = merge(tile(value, first), tile(value, first + 4))
                out[8 * pair + 2 * core + part] = low
                out[8 * pair + 2 * core + part + 4] = high
    return jnp.concatenate(out, axis=1)


def shape_of(shape, dtype):
    return jax.ShapeDtypeStruct(shape, dtype)


def run(kernel, ins, specs, outs, scratch=(), name=None, after=(), megabytes=4, us=1.0):
    n_in, n_after = len(ins), len(after)

    def body(*refs):
        kernel(*refs[:n_in], *refs[n_in + n_after :])

    kinds = {"s": SM, "v": VM, "h": VM, "r": ANY}
    return pl.pallas_call(
        body,
        out_shape=list(outs),
        in_specs=[kinds[kind] for kind in specs] + [ANY] * n_after,
        out_specs=[VM] * len(outs),
        scratch_shapes=list(scratch),
        compiler_params=pltpu.CompilerParams(vmem_limit_bytes=megabytes * 2**20),
        cost_estimate=pl.CostEstimate(flops=int(us * 10**9), bytes_accessed=int(us * 10**6), transcendentals=0),
        name=name,
    )(*ins, *after)


def at(index, unit):
    return pl.ds(pl.multiple_of(index * unit, unit), unit)


def first_norm_kernel(tokens, gains, out):
    value = tokens[...].astype(f32)
    inverse = lax.rsqrt(jnp.mean(value * value, axis=-1, keepdims=True) + norm_eps)
    out[...] = to_dp_order(value * inverse * gains[0:1, :]).astype(bf16)


def line_kernel(step, where, p0, p1, p2, p3, out, forward):
    width = out.shape[2]
    for index, piece in enumerate((p0, p1, p2, p3)):
        rows = at(jnp.bitwise_xor(where[2], index), 64)
        for result, core in ((out, where[3]), (forward, 1 - where[3])):
            lanes = pl.ds(pl.multiple_of(core * step, TILE), width)
            result[:, rows, :] = piece[:, :, lanes]


def stack_kernel(first, second, out):
    out[0] = first[...]
    out[1] = second[...]


def join_all_kernel(p0, p1, p2, p3, p4, p5, first, second):
    for out, pieces in ((first, (p0, p1, p2)), (second, (p3, p4, p5))):
        begin = 0
        for piece in pieces:
            out[begin : begin + piece.shape[0]] = piece[...]
            begin += piece.shape[0]


def thirds(first, second):
    parts = []
    for value in (first, second):
        for _ in range(3):
            part = value.astype(bf16).astype(f32)
            parts.append(part)
            value = value - part
    parts += [jnp.zeros_like(first)] * 2
    return jnp.concatenate(parts, axis=0).astype(bf16)


def from_thirds(rows):
    value = rows.astype(f32)
    return [value[k : k + 1] + value[k + 1 : k + 2] + value[k + 2 : k + 3] for k in (0, 3)]


def eight(a, ax, y2, b, by, x2):
    return [
        lambda p: a[p],
        lambda p: ax[p],
        lambda p: y2[0, p],
        lambda p: y2[1, p],
        lambda p: b[p],
        lambda p: by[p],
        lambda p: x2[0, p],
        lambda p: x2[1, p],
    ]


def order_matrix():
    rows = lax.broadcasted_iota(jnp.int32, (BLOCK, BLOCK), 0)
    cols = lax.broadcasted_iota(jnp.int32, (BLOCK, BLOCK), 1)
    target = jnp.bitwise_and(rows, RANK - 1) * (BLOCK // RANK) + jnp.right_shift(rows, 4)
    return jnp.where(cols == target, 1.0, 0.0).astype(bf16)


def pick(indices, pieces):
    total = None
    first = 0
    for piece in pieces:
        rows = piece.shape[0]
        lanes = lax.broadcasted_iota(jnp.int32, (indices.shape[0], rows), 1) + first
        part = mm(jnp.where(lanes == indices, 1.0, 0.0).astype(bf16), piece[...])
        total = part if total is None else total + part
        first += rows
    return total


def adapters_kernel(even_at, odd_at, flat_at, *rest):
    pieces, (out, out_m, tiles) = rest[:-3], rest[-3:]
    order = order_matrix()
    even = mm(pick(even_at[...], pieces).astype(bf16), order)
    odd = mm(pick(odd_at[...], pieces).astype(bf16), order)
    for part in range(8):
        low, high = merge(tile(even, part), tile(odd, part))
        tiles[:, part, :] = low
        tiles[:, 8 + part, :] = high
    for index in range(out.shape[1] // TILE):
        out[:, index * TILE : (index + 1) * TILE] = tiles[index].astype(bf16)
    flat = pick(flat_at[...], pieces)
    for index in range(out_m.shape[1] // BLOCK):
        out_m[0:1, index * BLOCK : (index + 1) * BLOCK] = flat[index : index + 1, :]


def column_norm(weights, lowers, uppers):
    joined = weights.astype(f32) + dora_scale * mm_f(lowers, uppers)
    return jnp.sum(joined * joined, axis=0, keepdims=True)


def split_rows(where, part, send, keep, share):
    core = where[3]
    for line in range(N_Z):
        send[line * share : (line + 1) * share] = part[at(2 * line + 1 - core, share)].astype(bf16)
    for line in range(N_Z):
        keep[line * share : (line + 1) * share] = part[at(2 * line + core, share)]


def attention_kernel(spans, where, x, b0, b1, b2, b3, b4, b5, w_out, flat, mags, cos, sin, seg_row, seg_col, squares,
                     send, keep, mixed, qkv, probs, att, low_qkv, low_out, stats, part):
    blocks = eight(b0, b1, b2, b3, b4, b5)
    width = CHUNK
    rows = x.shape[0]
    la = [spans[("A", p)][0] for p in range(3)]
    lb = [spans[("B", p)][0] for p in range(3)]
    allowed = seg_col[...] == seg_row[...]
    t_index = lax.broadcasted_iota(jnp.int32, (rows, rows), 0)
    s_index = lax.broadcasted_iota(jnp.int32, (rows, rows), 1)
    allowed = jnp.logical_and(allowed, s_index <= t_index)
    lows = mm_t(x[...], twice([flat[:, la[p] : la[p] + D] for p in range(3)]))
    low_qkv[...] = lows
    lows = high_low(lows)
    for p in range(3):
        upper = flat[:, lb[p] : lb[p] + width]
        total = dora_scale * mm(lows, only(upper, p, 3))
        square = jnp.zeros((1, width), f32)
        for index, block in enumerate(blocks):
            chunk = where[4 + index]
            weights = block(p)
            total += mm(x[:, at(chunk, CHUNK)], weights)
            lowers = flat[:, pl.ds(pl.multiple_of(la[p] + chunk * CHUNK, TILE), CHUNK)]
            square += column_norm(weights, lowers, upper)
        norm = jnp.sqrt(square + column_eps)
        magnitude = mags[:, pl.ds(pl.multiple_of(p * D + where[1] * width, TILE), width)]
        scale = magnitude / norm
        lanes = slice(p * width, (p + 1) * width)
        mixed[:, lanes] = total
        stats[0:1, lanes] = scale
        stats[1:2, lanes] = norm
        stats[2:3, lanes] = magnitude
        value = total * scale
        for head in range(width // HEAD_DIM):
            one = value[:, head * HEAD_DIM : (head + 1) * HEAD_DIM]
            if p < 2:
                one = one * cos[...] + swap64(one) * sin[...]
            begin = p * width + head * HEAD_DIM
            qkv[:, begin : begin + HEAD_DIM] = one.astype(bf16)
    for head in range(width // HEAD_DIM):
        lanes = slice(head * HEAD_DIM, (head + 1) * HEAD_DIM)
        query = qkv[:, lanes]
        keys = qkv[:, width + head * HEAD_DIM : width + (head + 1) * HEAD_DIM]
        value = qkv[:, 2 * width + head * HEAD_DIM : 2 * width + (head + 1) * HEAD_DIM]
        scores = mm_t(query, keys) * HEAD_DIM ** (-0.5)
        scores = jnp.where(allowed, scores, -1e30)
        expd = jnp.exp(scores - jnp.max(scores, axis=-1, keepdims=True))
        weights = expd / jnp.sum(expd, axis=-1, keepdims=True)
        probs[head] = weights
        att[:, lanes] = mm(weights.astype(bf16), value).astype(bf16)
    a_out, b_out = spans[("A", 3)][0], spans[("B", 3)][0]
    low = mm_t(att[...], flat[:, a_out : a_out + width])
    low_out[...] = low
    part[...] = mm(att[...], w_out[...]) + dora_scale * mm2(low, flat[:, b_out : b_out + D])
    split_rows(where, part, send, keep, keep.shape[0] // N_Z)
    send[keep.shape[0] :] = thirds(squares[0:1], squares[1:2])


def pair_kernel(where, keep, received, p1, p2, p3, own):
    share = own.shape[0]

    def line(index):
        rows = at(index, share)
        return keep[rows] + received[rows].astype(f32)

    own[...] = line(where[2])
    for step, piece in ((1, p1), (2, p2), (3, p3)):
        piece[...] = line(jnp.bitwise_xor(where[2], step)).astype(bf16)


def pair_more_kernel(where, keep, received, squares, p1, p2, p3, own, more):
    share = own.shape[0]

    def line(index):
        rows = at(index, share)
        return keep[rows] + received[rows].astype(f32)

    own[...] = line(where[2])
    first, second = from_thirds(received[keep.shape[0] :])
    first, second = first + squares[0:1], second + squares[1:2]
    more[0:1], more[1:2] = first, second
    rows = thirds(first, second)
    for step, piece in ((1, p1), (2, p2), (3, p3)):
        piece[0:share] = line(jnp.bitwise_xor(where[2], step)).astype(bf16)
        piece[share:] = rows


def total_of(own, r1, r2, r3):
    rows = own.shape[0]
    return own[...] + r1[0:rows].astype(f32) + r2[0:rows].astype(f32) + r3[0:rows].astype(f32)


def pair_grads_kernel(where, keep, received, kept, got, p1, p2, p3, own, own_grads):
    share, unit = own.shape[0], own_grads.shape[0]
    half = unit // 2

    def line(index):
        rows = at(index, share)
        return keep[rows] + received[rows].astype(f32)

    def grads(index):
        rows = at(index, unit)
        return kept[rows] + got[rows].astype(f32)

    own[...] = line(where[2])
    own_grads[...] = grads(where[2])
    for step, piece in ((1, p1), (2, p2), (3, p3)):
        index = jnp.bitwise_xor(where[2], step)
        piece[0:share] = line(index).astype(bf16)
        value = grads(index).astype(bf16)
        piece[share:, 0:BLOCK] = value[0:half]
        piece[share:, BLOCK:] = value[half:]


def second_norm_kernel(own, more, r1, r2, r3, tokens, gains, mags, x_two, mixed, out, scale_o, norm_o, scale_d, norm_d):
    share = own.shape[0]
    total = own[...]
    squares = [more[0:1], more[1:2]]
    for piece in (r1, r2, r3):
        total = total + piece[0:share].astype(f32)
        for row, value in enumerate(from_thirds(piece[share:])):
            squares[row] = squares[row] + value
    for square, begin, scale, norm in (
        (squares[0], 3 * D, scale_o, norm_o),
        (squares[1], 4 * D + 2 * FF, scale_d, norm_d),
    ):
        value = jnp.sqrt(square + column_eps)
        norm[...] = value
        scale[...] = mags[:, begin : begin + D] / value
    mixed[...] = total
    value = tokens[...].astype(f32) + total * scale_o[...]
    x_two[...] = value
    inverse = lax.rsqrt(jnp.mean(value * value, axis=-1, keepdims=True) + norm_eps)
    out[...] = to_dp_order(value * inverse * gains[1:2, :]).astype(bf16)


def join_rows(where, pieces, out):
    share = out.shape[0] // N_MP
    for index, piece in enumerate(pieces):
        line = jnp.bitwise_xor(where[2], index % N_Z)
        core = where[3] if index < N_Z else 1 - where[3]
        out[at(2 * line + core, share)] = piece[0:share].astype(out.dtype)


def join_kernel(where, p0, p1, p2, p3, p4, p5, p6, p7, input_grad, layer_out):
    share = layer_out.shape[0] // N_MP
    pieces = (p0, p1, p2, p3, p4, p5, p6, p7)
    join_rows(where, pieces, input_grad)
    join_rows(where, [piece.at[share : 2 * share] for piece in pieces], layer_out)


def wide_squares(spans, where, blocks, chunks, flat):
    squares = []
    for p in range(2):
        a, b = spans[("A", 4 + p)][0], spans[("B", 4 + p)][0]
        square = jnp.zeros((1, WIDE), f32)
        for index, block in zip(chunks, blocks):
            begin = pl.multiple_of(a + where[4 + index] * CHUNK, TILE)
            square += column_norm(block(p), flat[:, pl.ds(begin, CHUNK)], flat[:, b : b + WIDE])
        squares.append(square)
    return jnp.concatenate(squares, axis=1)


def wide_first_kernel(spans, where, a, ax, b, by, flat, squares):
    blocks = eight(a, ax, None, b, by, None)
    squares[...] = wide_squares(spans, where, [blocks[k] for k in (0, 1, 4, 5)], (0, 1, 4, 5), flat)


def wide_norm_kernel(spans, where, y2, x2, flat, mags, squares, stats):
    blocks = eight(None, None, y2, None, None, x2)
    total = squares[...] + wide_squares(spans, where, [blocks[k] for k in (2, 3, 6, 7)], (2, 3, 6, 7), flat)
    for p in range(2):
        lanes = slice(p * WIDE, (p + 1) * WIDE)
        norm = jnp.sqrt(total[:, lanes] + column_eps)
        first = 4 * D + p * FF + where[2] * (2 * FF // N_MP) + where[3] * (WIDE - TILE)
        magnitude = mags[:, pl.ds(pl.multiple_of(first, TILE), WIDE)]
        stats[0:1, lanes] = magnitude / norm
        stats[1:2, lanes] = norm
        stats[2:3, lanes] = magnitude


def row_norm_kernel(spans, w_out, w_down, flat, squares):
    for row, (p, weights) in enumerate(((3, w_out[...]), (6, w_down[...]))):
        a, size = spans[("A", p)]
        b = spans[("B", p)][0]
        squares[row : row + 1, :] = column_norm(weights, flat[:, a : a + size], flat[:, b : b + D])


def down_back_kernel(spans, where, cotangent, scale, w_down, flat, d_act, grad_b, through, padded):
    a, size = spans[("A", 6)]
    b = spans[("B", 6)][0]
    grad = (cotangent[...].astype(f32) * scale[...]).astype(bf16)
    grad_b[...] = grad
    low = dora_scale * mm_t(grad, flat[:, b : b + D])
    through[...] = low
    padded[...] = jnp.zeros_like(padded)
    padded[:, 0:size] = mm_t(grad, w_down[...]) + mm2(low, flat[:, a : a + size])
    value = padded[...]
    d_act[...] = jnp.where(where[3] == 0, value, pltpu.roll(value, FILL, 1))


def middle_kernel(spans, where, p0, p1, p2, p3, p4, p5, p6, p7, b0, b1, b2, b3, b4, b5, d_act, flat, stats,
                  send, keep, x, act, grads, throughs, lows, dots, part, mixed):
    blocks = eight(b0, b1, b2, b3, b4, b5)
    join_rows(where, (p0, p1, p2, p3, p4, p5, p6, p7), x)
    la = [spans[("A", 4 + p)][0] for p in range(2)]
    lb = [spans[("B", 4 + p)][0] for p in range(2)]
    uppers = [flat[:, b : b + WIDE] for b in lb]
    low = mm_t(x[...], twice([flat[:, a : a + D] for a in la]))
    lows[...] = low
    low = high_low(low)
    for p in range(2):
        total = dora_scale * mm(low, only(uppers[p], p, 2))
        for index, block in enumerate(blocks):
            total += mm(x[:, at(where[4 + index], CHUNK)], block(p))
        mixed[:, p * WIDE : (p + 1) * WIDE] = total
    lanes = lax.broadcasted_iota(jnp.int32, d_act.shape, 1) - where[3] * FILL
    used = jnp.logical_and(lanes >= 0, lanes < WIDE - FILL)
    gate = mixed[:, :WIDE] * stats[0:1, :WIDE]
    upward = mixed[:, WIDE:] * stats[0:1, WIDE:]
    sigmoid_gate = jax.nn.sigmoid(gate)
    silu = gate * sigmoid_gate
    act[...] = jnp.where(used, silu * upward, 0.0).astype(bf16)
    back = jnp.where(used, d_act[...], 0.0)
    grad = back * upward * sigmoid_gate * (1.0 + gate * (1.0 - sigmoid_gate))
    dots[0:1, :WIDE] = jnp.sum(grad * mixed[:, :WIDE], axis=0, keepdims=True)
    grads[:, :WIDE] = (grad * stats[0:1, :WIDE]).astype(bf16)
    grad = back * silu
    dots[0:1, WIDE:] = jnp.sum(grad * mixed[:, WIDE:], axis=0, keepdims=True)
    grads[:, WIDE:] = (grad * stats[0:1, WIDE:]).astype(bf16)
    through = dora_scale * (
        mm_t(grads[:, :WIDE], only(uppers[0], 0, 2)) + mm_t(grads[:, WIDE:], only(uppers[1], 1, 2))
    )
    throughs[...] = through
    through = high_low(through)
    for index, block in enumerate(blocks):
        chunk = where[4 + index]
        lowers = [flat[:, pl.ds(pl.multiple_of(a + chunk * CHUNK, TILE), CHUNK)] for a in la]
        total = mm(through, twice(lowers))
        for p in range(2):
            total += mm_t(grads[:, p * WIDE : (p + 1) * WIDE], block(p))
        part[:, at(chunk, CHUNK)] = total
    split_rows(where, part, send, keep, send.shape[0] // N_Z)


def down_kernel(spans, where, act, w_down, flat, cotangent, send, keep, low_out, dots, part, local):
    a, size = spans[("A", 6)]
    b = spans[("B", 6)][0]
    value = act[...].astype(f32)
    value = jnp.where(where[3] == 0, value, pltpu.roll(value, WIDE - FILL, 1))
    local[...] = value.astype(bf16)
    inputs = local[:, 0:size]
    low = mm_t(inputs, flat[:, a : a + size])
    low_out[...] = low
    part[...] = mm(inputs, w_down[...]) + dora_scale * mm2(low, flat[:, b : b + D])
    split_rows(where, part, send, keep, send.shape[0] // N_Z)
    dots[...] = jnp.sum(cotangent[...].astype(f32) * part[...], axis=0, keepdims=True)


def norm_back(value, grad, gain):
    inverse = lax.rsqrt(jnp.mean(value * value, axis=-1, keepdims=True) + norm_eps)
    scaled = grad * gain
    inner = jnp.mean(scaled * value, axis=-1, keepdims=True)
    return inverse * (scaled - value * inverse * inverse * inner)


def second_back_kernel(own, r1, r2, r3, x_two, mixed, cotangent, gains, scale, dots_d, grad_two, grad_b, dots):
    total = to_mp_order(total_of(own, r1, r2, r3))
    grad = cotangent[...].astype(f32) + norm_back(x_two[...], total, gains[1:2, :])
    grad_two[...] = grad
    grad_b[0 : grad.shape[0]] = (grad * scale[...]).astype(bf16)
    own = jnp.sum(grad * mixed[...], axis=0, keepdims=True)
    dots[...] = own
    grad_b[grad.shape[0] :] = thirds(own, dots_d[...])


def last_rows_kernel(own, r1, r2, r3, tokens, grad_two, gains, own_d, d1, d2, d3, x_two, scale, out):
    share = own.shape[0]
    total = to_mp_order(total_of(own, r1, r2, r3))
    value = tokens[...].astype(f32)
    out[0:share] = (grad_two[...] + norm_back(value, total, gains[0:1, :])).astype(bf16)
    out[share:] = (x_two[...] + total_of(own_d, d1, d2, d3) * scale[...]).astype(bf16)


def attention_back_kernel(spans, where, p0, p1, p2, p3, p4, p5, p6, p7, b0, b1, b2, b3, b4, b5, w_out, flat,
                          cos, sin, mixed, qkv, probs, stats,
                          send, keep, grad_out, grads, throughs, through_out, dots, dots_o, dots_d, part, incoming):
    blocks = eight(b0, b1, b2, b3, b4, b5)
    width = CHUNK
    join_rows(where, (p0, p1, p2, p3, p4, p5, p6, p7), grad_out)
    sums = [jnp.zeros((1, D), f32)] * 2
    for piece in (p0, p1, p2, p3, p4, p5, p6, p7):
        for index, value in enumerate(from_thirds(piece[grad_out.shape[0] // N_MP :])):
            sums[index] = sums[index] + value
    dots_o[...], dots_d[...] = sums
    a, b = spans[("A", 3)][0], spans[("B", 3)][0]
    low = dora_scale * mm_t(grad_out[...], flat[:, b : b + D])
    through_out[...] = low
    grad_att = (mm_t(grad_out[...], w_out[...]) + mm2(low, flat[:, a : a + width])).astype(bf16)
    for head in range(width // HEAD_DIM):
        lanes = [slice(p * width + head * HEAD_DIM, p * width + (head + 1) * HEAD_DIM) for p in range(3)]
        query, keys, value = [qkv[:, one] for one in lanes]
        grad = grad_att[:, head * HEAD_DIM : (head + 1) * HEAD_DIM]
        weights = probs[head]
        grad_weights = mm_t(grad, value)
        incoming[:, lanes[2]] = mm_f(weights.astype(bf16), grad)
        centred = jnp.sum(weights * grad_weights, axis=-1, keepdims=True)
        grad_scores = (weights * (grad_weights - centred)).astype(bf16)
        grad_query = mm(grad_scores, keys) * HEAD_DIM ** (-0.5)
        grad_key = mm_f(grad_scores, query) * HEAD_DIM ** (-0.5)
        incoming[:, lanes[0]] = grad_query * cos[...] - swap64(grad_query) * sin[...]
        incoming[:, lanes[1]] = grad_key * cos[...] - swap64(grad_key) * sin[...]
    dots[...] = jnp.sum(incoming[...] * mixed[...], axis=0, keepdims=True)
    grads[...] = (incoming[...] * stats[0:1, :]).astype(bf16)
    la = [spans[("A", p)][0] for p in range(3)]
    uppers = [flat[:, spans[("B", p)][0] : spans[("B", p)][0] + width] for p in range(3)]
    through = mm_t(grads[:, :width], only(uppers[0], 0, 3))
    for p in (1, 2):
        through += mm_t(grads[:, p * width : (p + 1) * width], only(uppers[p], p, 3))
    through = dora_scale * through
    throughs[...] = through
    through = high_low(through)
    for index, block in enumerate(blocks):
        chunk = where[4 + index]
        lowers = [flat[:, pl.ds(pl.multiple_of(a + chunk * CHUNK, TILE), CHUNK)] for a in la]
        total = mm(through, twice(lowers))
        for p in range(3):
            total += mm_t(grads[:, p * width : (p + 1) * width], block(p))
        part[:, at(chunk, CHUNK)] = total
    split_rows(where, part, send, keep, send.shape[0] // N_Z)


def to_blocks(value, tiles, out, begin):
    pairs = value.shape[1] // TILE
    for index in range(pairs):
        tiles[index] = tile(value, index)
    for part in range(8):
        even, odd = merge(tiles[0:pairs, part, :], tiles[0:pairs, 8 + part, :])
        lanes = slice(part * TILE, (part + 1) * TILE)
        out[begin : begin + pairs, lanes] = even
        out[begin + pairs : begin + 2 * pairs, lanes] = odd


def column_grads_kernel(spans, projections, width, where, x, b0, b1, b2, b3, b4, b5, flat, stats, grads, throughs,
                        lows, dots, out_a, out_b, out_m, tiles, whole):
    blocks = eight(b0, b1, b2, b3, b4, b5)
    for position, p in enumerate(projections):
        a, b = spans[("A", p)][0], spans[("B", p)][0]
        lanes = slice(position * width, (position + 1) * width)
        ranks = slice(2 * position * RANK, (2 * position + 1) * RANK)
        upper = flat[:, b : b + width]
        norm = stats[1:2, lanes]
        inverse = 1.0 / norm
        e = dots[0:1, lanes]
        out_m[0:1, lanes] = e * inverse
        ratio = -e * stats[2:3, lanes] * inverse * inverse * inverse
        scaled = halves(dora_scale * upper.astype(f32) * ratio)
        through = halves(throughs[:, ranks])
        square = dora_scale * (mm_t(scaled[0], upper) + mm_t(scaled[1], upper))
        lower = flat[:, a : a + D]
        whole[...] = mm2(square, lower) + mm_f(through[0], x[...]) + mm_f(through[1], x[...])
        crossed = dora_scale * mm2(mm_t(lower, lower), upper)
        for index, block in enumerate(blocks):
            chunk = where[4 + index]
            weights = block(position)
            whole[:, at(chunk, CHUNK)] += mm_t(scaled[0], weights) + mm_t(scaled[1], weights)
            crossed += mm(flat[:, pl.ds(pl.multiple_of(a + chunk * CHUNK, TILE), CHUNK)], weights)
        to_blocks(whole[...], tiles, out_a, position * D * RANK // BLOCK)
        upper_grad = dora_scale * (mm2_f(lows[:, ranks], grads[:, lanes]) + crossed * ratio)
        to_blocks(upper_grad, tiles, out_b, position * width * RANK // BLOCK)


def row_grads_kernel(spans, p, where, x, weights_ref, flat, scale_row, norm_row, mag_row, grads, through_in, low, dots,
                     out_a, out_b, tiles, local):
    a, size = spans[("A", p)]
    b = spans[("B", p)][0]
    weights = weights_ref[...]
    inputs = x[...]
    if p == 6:
        value = inputs.astype(f32)
        value = jnp.where(where[3] == 0, value, pltpu.roll(value, WIDE - FILL, 1))
        local[...] = value.astype(bf16)
        inputs = local[:, 0:size]
    lower = flat[:, a : a + size]
    upper = flat[:, b : b + D]
    inverse = 1.0 / norm_row[...]
    ratio = -dots[...] * mag_row[...] * inverse * inverse * inverse
    scaled = halves(dora_scale * upper.astype(f32) * ratio)
    square = dora_scale * (mm_t(scaled[0], upper) + mm_t(scaled[1], upper))
    grad = mm2(square, lower) + mm2_f(through_in[...], inputs)
    grad += mm_t(scaled[0], weights) + mm_t(scaled[1], weights)
    if size % TILE:
        grad = jnp.concatenate([grad, jnp.zeros((RANK, TILE - size % TILE), f32)], axis=1)
    to_blocks(grad, tiles, out_a, 0)
    crossed = mm(lower, weights) + dora_scale * mm2(mm_t(lower, lower), upper)
    to_blocks(dora_scale * (mm2_f(low[...], grads[...]) + crossed * ratio), tiles, out_b, 0)


def pack_kernel(where, a_f, a_a, b_d, b_o, m_f, m_a, dots_o, norm_o, dots_d, norm_d, give, keep, rows, flat):
    begin = 0
    for array in (a_f, a_a, b_d, b_o):
        rows[begin : begin + array.shape[0]] = array[...]
        begin += array.shape[0]
    flat[...] = jnp.zeros_like(flat)
    for p in range(3):
        lanes = pl.ds(pl.multiple_of(p * D + where[1] * CHUNK, TILE), CHUNK)
        flat[:, lanes] = m_a[:, p * CHUNK : (p + 1) * CHUNK]
    flat[:, 3 * D : 4 * D] = dots_o[...] / norm_o[...]
    for p in range(2):
        first = 4 * D + p * FF + where[2] * (2 * FF // N_MP) + where[3] * (WIDE - TILE)
        flat[:, pl.ds(pl.multiple_of(first, TILE), WIDE)] = m_f[:, p * WIDE : (p + 1) * WIDE]
    flat[:, 4 * D + 2 * FF :] = dots_d[...] / norm_d[...]
    rows[begin:] = jnp.zeros((rows.shape[0] - begin, BLOCK), f32)
    for index in range(flat.shape[1] // BLOCK):
        rows[begin + index : begin + index + 1] = flat[:, index * BLOCK : (index + 1) * BLOCK]
    unit = rows.shape[0] // N_MP
    for line in range(N_Z):
        give[line * unit : (line + 1) * unit] = rows[at(2 * line + 1 - where[3], unit)].astype(bf16)
        keep[line * unit : (line + 1) * unit] = rows[at(2 * line + where[3], unit)]


def local_kernel(where, own, r1, r2, r3, b_f, b_a, a_d, a_o, mine, p1, p2, p3, rows):
    begin = own.shape[0]
    half = begin // 2
    for index in range(2):
        lanes = slice(index * BLOCK, (index + 1) * BLOCK)
        total = own[index * half : (index + 1) * half]
        for piece in (r1, r2, r3):
            total = total + piece[piece.shape[0] - half :, lanes].astype(f32)
        rows[index * half : (index + 1) * half] = total
    for array in (b_f, b_a, a_d, a_o):
        rows[begin : begin + array.shape[0]] = array[...]
        begin += array.shape[0]
    rows[begin:] = jnp.zeros((rows.shape[0] - begin, BLOCK), f32)
    part = mine.shape[0]
    mine[...] = rows[at(where[0], part)]
    for step, piece in ((1, p1), (2, p2), (3, p3)):
        piece[...] = rows[at(jnp.bitwise_xor(where[0], step), part)].astype(bf16)


def last_sum_kernel(own, r1, r2, r3, out):
    out[...] = total_of(own, r1, r2, r3).astype(bf16)


def update_kernel(index, mine, s0, s1, s2, s3, s4, s5, s6, s7, master, first, second, new_master, new_first, new_second):
    picked = pick(index[...], (s0, s1, s2, s3, s4, s5, s6, s7)).astype(bf16)
    grad = jnp.where(mine[...] >= COUNT_FLAT, picked.astype(f32), mm_t(picked, order_matrix()))
    grad = jnp.where(mine[...] >= 0, grad, 0.0)
    rates = jnp.where(mine[...] < COUNT_FLAT, rate_upper, rate_magnitude)
    rates = jnp.where(mine[...] < COUNT_LOWER, rate_lower, rates)
    rates = jnp.where(mine[...] < 0, 0.0, rates)
    weight = master[...]
    first_new = beta_one * first[...] + (1.0 - beta_one) * grad
    second_new = beta_two * second[...] + (1.0 - beta_two) * grad * grad
    first_hat = first_new / (1.0 - beta_one**STEP)
    second_hat = second_new / (1.0 - beta_two**STEP)
    new_master[...] = weight - rates * (
        first_hat / (jnp.sqrt(second_hat) + adam_eps) + weight_decay * weight
    )
    new_first[...] = first_new
    new_second[...] = second_new


COUNT_LOWER = RANK * (6 * D + FF) // BLOCK
COUNT_FLAT = COUNT_LOWER + RANK * (5 * D + 2 * FF) // BLOCK


def block_starts():
    starts = {}
    total = 0
    for kind, side in (("A", 0), ("B", 1)):
        for index, sizes in enumerate(proj_dims()):
            starts[(kind, index)] = total
            total += sizes[side] * RANK // BLOCK
    return starts


def fast_body(
    tokens,
    cotangent,
    norm_gains,
    w_attn,
    w_in,
    w_down,
    segments,
    owners,
    master,
    first_moment,
    second_moment,
):
    rows = tokens.shape[0]
    mi = lax.axis_index("mp")
    di = lax.axis_index("dp")
    core = mi % 2
    zi = mi // 2
    share = rows // N_MP
    capacity = master.shape[0]
    n_blocks = owners.shape[0]
    width = D // N_MP
    starts = block_starts()

    def mp_swap(values, step):
        return lax.ppermute(values, "mp", [(i, i ^ step) for i in range(N_MP)])

    def dp_swap(values, step):
        return lax.ppermute(values, "dp", [(i, i ^ step) for i in range(N_DP)])

    order = [(0, 0), (1, 0), (2, 0), (3, 0), (0, 1), (2, 1), (1, 1), (3, 1)]
    chunks = [(di ^ t) * 2 + (core ^ h) for t, h in order]
    where = jnp.stack([di, mi, zi, core] + chunks).astype(jnp.int32)

    def stack(first, second, after=()):
        shape = (2,) + first.shape
        return run(
            stack_kernel, [first, second], "hh", [shape_of(shape, bf16)], name="stack", after=after, us=0.01
        )[0]

    def plane_first(a, b):
        return a, dp_swap(a, 1), b, dp_swap(b, 2)

    def plane_second(a, ax, b, by, after=()):
        return [a, ax, dp_swap(stack(a, ax, after), 2), b, by, dp_swap(stack(b, by, after), 1)]

    def plane(a, b):
        return plane_second(*plane_first(a, b))

    sent = master.astype(bf16)
    line = [sent] + [mp_swap(sent, 2 * step) for step in range(1, N_Z)]
    first_b = plane_first(jnp.concatenate(line[:2]), jnp.concatenate(line[2:]))
    owners, segments, w_late, tokens, line_end = lax.optimization_barrier(
        (owners, segments, w_attn, tokens, first_b[2])
    )
    first_b = first_b[:2] + (line_end,) + first_b[3:]
    sheet = plane_second(*first_b)
    sheet = [one.reshape(-1, BLOCK) for one in sheet]
    features = run(
        first_norm_kernel,
        [tokens, norm_gains],
        "hh",
        [shape_of((rows, D), bf16)],
        name="first_norm",
        megabytes=6,
        us=1.2,
        after=[first_b[2]],
    )[0]
    def cut(weights, count, chip):
        pieces = []
        for index in range(N_Z):
            piece = lax.dynamic_slice(weights, (0, di * 64, (zi ^ index) * chip), (count, 64, chip))
            pieces.append(mp_swap(piece, 2 * index) if index else piece)
        return pieces

    def columns_of(pieces, size, step, name, after=()):
        count = pieces[0].shape[0]
        a, forward = run(
            functools.partial(line_kernel, step),
            [where] + pieces,
            "shhhh",
            [shape_of((count, CHUNK, size), bf16)] * 2,
            name=name,
            after=after,
        )
        return plane_first(a, mp_swap(forward, 1))

    first_a = columns_of(cut(w_attn, 3, 2 * width), width, width, "line_a", [features])
    blocks_a = plane_second(*first_a)
    sheet = run(
        join_all_kernel,
        sheet,
        "h" * 6,
        [shape_of((8 * capacity, BLOCK), bf16)] * 2,
        name="adapter_rows",
        after=[first_a[0]],
        us=0.1,
    )
    stacked = list(sheet) + [mp_swap(one, 1) for one in sheet]
    w_in_late, own_a = lax.optimization_barrier((w_in, first_a[0]))
    pieces_f = cut(w_in_late, 2, 2 * FF // N_MP)
    w_out = w_late[3]

    ranks = slot_positions(owners, 0)
    owner_d, owner_m = owners // N_MP, owners % N_MP
    piece_at = (owner_d ^ di) * N_Z + ((owner_m // 2) ^ zi)
    listed = np.array([0, 1, 8, 9, 2, 3, 12, 13, 4, 5, 10, 11, 6, 7, 14, 15], np.int32)
    piece_at = jnp.sum(jnp.where(piece_at[:, None] == np.arange(16), listed, 0), axis=1)
    slot = (((owner_m % 2) ^ core) * 16 + piece_at) * capacity + ranks
    wanted = []
    spans = {}

    def want(name, blocks, size):
        spans[name] = (sum(w.shape[0] for w in wanted) * 64, size)
        wanted.append(blocks)

    by_dp = np.array(
        [(2 * z + c) * 4 + d for d in range(N_DP) for c in range(2) for z in range(N_Z)], np.int32
    )
    all_blocks = np.arange(D * RANK // BLOCK, dtype=np.int32)
    for index in (0, 1, 2, 4, 5):
        want(("A", index), starts[("A", index)] + by_dp, D)
        if index < 3:
            want(("B", index), starts[("B", index)] + mi * 4 + np.arange(4), width)
        else:
            first_block = starts[("B", index)] + zi * 22 + core * 10
            want(("B", index), first_block + np.arange(12), WIDE)
    want(("A", 3), starts[("A", 3)] + mi * 4 + np.arange(4), width)
    want(("B", 3), starts[("B", 3)] + all_blocks, D)
    want(("A", 6), starts[("A", 6)] + mi * 11 + np.minimum(np.arange(12), 10), FF // N_MP)
    want(("B", 6), starts[("B", 6)] + all_blocks, D)
    chosen = jnp.take(slot, jnp.concatenate([jnp.asarray(w, jnp.int32) for w in wanted]))
    n_pairs = chosen.shape[0] // 2
    pairs = chosen.reshape(n_pairs, 2)
    flat, mags = run(
        adapters_kernel,
        [pairs[:, :1], pairs[:, 1:], slot[COUNT_FLAT:, None]] + stacked,
        "vvv" + "h" * len(stacked),
        [shape_of((RANK, n_pairs * TILE), bf16), shape_of((1, (n_blocks - COUNT_FLAT) * BLOCK), f32)],
        [pltpu.VMEM((n_pairs, RANK, TILE), f32)],
        name="adapters", megabytes=13, us=0.3,
    )

    def bind(kernel, *args):
        return functools.partial(kernel, spans, *args)

    def column_grads(projections, size, x, blocks, flat, stats, grads, throughs, lows, dots, after):
        count = len(projections)
        return run(
            bind(column_grads_kernel, projections, size),
            [where, x] + blocks + [flat, stats, grads, throughs, lows, dots],
            "s" + "h" * 13,
            [
                shape_of((count * D * RANK // BLOCK, BLOCK), f32),
                shape_of((count * size * RANK // BLOCK, BLOCK), f32),
                shape_of((1, count * size), f32),
            ],
            [pltpu.VMEM((D // TILE, RANK, TILE), f32), pltpu.VMEM((RANK, D), f32)],
            name="column_grads", megabytes=9, us=1,
            after=after,
        )

    def row_grads(p, x, weights, flat, scale, norm, mag, grads, through, low, dots, after):
        size = spans[("A", p)][1]
        return run(
            bind(row_grads_kernel, p),
            [where, x, weights, flat, scale, norm, mag, grads, through, low, dots],
            "s" + "h" * 10,
            [
                shape_of((-(-size // TILE) * 2, BLOCK), f32),
                shape_of((D * RANK // BLOCK, BLOCK), f32),
            ],
            [pltpu.VMEM((D // TILE, RANK, TILE), f32), pltpu.VMEM((rows, WIDE), bf16)],
            name="row_grads", megabytes=6, us=0.1,
            after=after,
        )

    row = segments[0]
    cosine, sine = rotary_tables(segment_positions(row))
    cosine, sine = cosine[:, 0], sine[:, 0]
    cos_full = jnp.concatenate([cosine, cosine], axis=-1)
    sin_full = jnp.concatenate([-sine, sine], axis=-1)
    tokens_here = lax.dynamic_slice_in_dim(tokens, mi * share, share, 0)
    cotangent_here = lax.dynamic_slice_in_dim(cotangent, mi * share, share, 0)
    half_rows = [shape_of((rows // 2, D), bf16), shape_of((rows // 2, D), f32)]

    def finish_rows(send, keep, after):
        received = mp_swap(send, 1)
        p1, p2, p3, own = run(
            pair_kernel,
            [where, keep, received],
            "shh",
            [shape_of((share, D), bf16)] * 3 + [shape_of((share, D), f32)],
            name="pair_sums", megabytes=4, us=1.2,
            after=after,
        )
        return [own, mp_swap(p1, 2), mp_swap(p2, 4), mp_swap(p3, 6)]

    def gather_rows(value):
        mine = [value] + [mp_swap(value, 2 * step) for step in range(1, N_Z)]
        return mine + [mp_swap(one, 1) for one in mine]

    squares = run(
        bind(row_norm_kernel),
        [w_out, w_down, flat],
        "hhh",
        [shape_of((2, D), f32)],
        name="row_norms",
        us=0.1,
    )[0]
    n_heads = width // HEAD_DIM
    send, keep, mixed_a, qkv, probs, att, low_a, low_o, stats_a = run(
        bind(attention_kernel),
        [where, features] + blocks_a + [w_out, flat, mags, cos_full, sin_full, segments, row[:, None], squares],
        "s" + "h" * 15,
        [shape_of((rows // 2 + 8, D), bf16), half_rows[1]]
        + [
            shape_of((rows, 3 * width), f32),
            shape_of((rows, 3 * width), bf16),
            shape_of((n_heads, rows, rows), f32),
            shape_of((rows, width), bf16),
            shape_of((rows, 6 * RANK), f32),
            shape_of((rows, RANK), f32),
            shape_of((8, 3 * width), f32),
        ],
        [pltpu.VMEM((rows, D), f32)],
        name="attention",
        megabytes=13,
        us=10,
    )

    p1, p2, p3, own_o, more_o = run(
        pair_more_kernel,
        [where, keep, mp_swap(send, 1), squares],
        "shhh",
        [shape_of((share + 8, D), bf16)] * 3 + [shape_of((share, D), f32), shape_of((2, D), f32)],
        name="pair_sums",
        us=1.2,
    )
    sums_o = [mp_swap(p1, 2), mp_swap(p2, 4), mp_swap(p3, 6)]
    first_f = columns_of(pieces_f, WIDE, WIDE - TILE, "line_f")
    blocks_f = plane_second(*first_f, after=sums_o[1:2])
    row_of = shape_of((1, D), f32)
    x_two, mixed_o, features_two, scale_o, norm_o, scale_d, norm_d = run(
        second_norm_kernel,
        [own_o, more_o] + sums_o + [tokens_here, norm_gains, mags],
        "h" * 8,
        [shape_of((share, D), f32)] * 2 + [shape_of((share, D), bf16)] + [row_of] * 4,
        name="second_norm",
        us=0.5,
    )
    mag_o = mags[:, 3 * D : 4 * D]
    mag_d = mags[:, 4 * D + 2 * FF :]
    pieces = gather_rows(features_two)
    squares_f = run(
        bind(wide_first_kernel),
        [where] + [blocks_f[k] for k in (0, 1, 3, 4)] + [flat],
        "s" + "h" * 5,
        [shape_of((1, 2 * WIDE), f32)],
        name="wide_squares", megabytes=8, us=3,
        after=[pieces[1]],
    )[0]
    d_act, grad_d, through_d = run(
        bind(down_back_kernel),
        [where, cotangent, scale_d, w_down, flat],
        "shhhh",
        [shape_of((rows, WIDE), f32), shape_of((rows, D), bf16), shape_of((rows, RANK), f32)],
        [pltpu.VMEM((rows, WIDE), f32)],
        name="down_back", megabytes=7, us=3.5,
        after=[squares_f],
    )
    stats_f = run(
        bind(wide_norm_kernel),
        [where] + [blocks_f[k] for k in (2, 5)] + [flat, mags, squares_f],
        "s" + "h" * 5,
        [shape_of((8, 2 * WIDE), f32)],
        name="wide_norms", megabytes=8, us=3,
        after=[through_d],
    )[0]
    send, keep, x_f, act, grads_f, through_f, low_f, dots_f = run(
        bind(middle_kernel),
        [where] + pieces + blocks_f + [d_act, flat, stats_f],
        "s" + "h" * 17,
        half_rows
        + [
            shape_of((rows, D), bf16),
            shape_of((rows, WIDE), bf16),
            shape_of((rows, 2 * WIDE), bf16),
            shape_of((rows, 4 * RANK), f32),
            shape_of((rows, 4 * RANK), f32),
            shape_of((1, 2 * WIDE), f32),
        ],
        [pltpu.VMEM((rows, D), f32), pltpu.VMEM((rows, 2 * WIDE), f32)],
        name="feed_forward", megabytes=22, us=14,
    )
    send_d, keep_d, low_d, dots_d = run(
        bind(down_kernel),
        [where, act, w_down, flat, cotangent],
        "shhhh",
        half_rows + [shape_of((rows, RANK), f32), shape_of((1, D), f32)],
        [pltpu.VMEM((rows, D), f32), pltpu.VMEM((rows, WIDE), bf16)],
        name="down", megabytes=9, us=3.5,
    )
    sums = finish_rows(send, keep, [low_d])
    a_f, b_f, m_f = column_grads(
        (4, 5), WIDE, x_f, blocks_f, flat, stats_f, grads_f, through_f, low_f, dots_f, [sums[1]]
    )
    grad_two, grad_o_piece, dots_o = run(
        second_back_kernel,
        sums + [x_two, mixed_o, cotangent_here, norm_gains, scale_o, dots_d],
        "h" * 10,
        [shape_of((share, D), f32), shape_of((share + 8, D), bf16), row_of],
        name="second_norm_back", megabytes=3, us=0.5,
        after=[m_f],
    )
    pieces_o = gather_rows(grad_o_piece)
    sums_d = finish_rows(send_d, keep_d, [pieces_o[0], pieces_o[7]])
    send, keep, grad_o, grads_a, through_a, through_o, dots_a, dots_all_o, dots_all_d = run(
        bind(attention_back_kernel),
        [where] + pieces_o + blocks_a + [w_out, flat, cos_full, sin_full, mixed_a, qkv, probs, stats_a],
        "s" + "h" * 22,
        half_rows
        + [
            shape_of((rows, D), bf16),
            shape_of((rows, 3 * width), bf16),
            shape_of((rows, 6 * RANK), f32),
            shape_of((rows, RANK), f32),
            shape_of((1, 3 * width), f32),
            row_of,
            row_of,
        ],
        [pltpu.VMEM((rows, D), f32), pltpu.VMEM((rows, 3 * width), f32)],
        name="attention_back",
        megabytes=10,
        us=0.1,
        after=[sums_d[0]],
    )
    a_o, b_o = row_grads(
        3, att, w_out, flat, scale_o, norm_o, mag_o, grad_o, through_o, low_o, dots_all_o, []
    )
    a_a, b_a, m_a = column_grads(
        (0, 1, 2), width, features, blocks_a, flat, stats_a, grads_a, through_a, low_a, dots_a, sums_d[2:3]
    )
    a_d, b_d = row_grads(
        6, act, w_down, flat, scale_d, norm_d, mag_d, grad_d, through_d, low_d, dots_all_d, [m_a]
    )
    unit, part = 32, 24
    give, kept = run(
        pack_kernel,
        [where, a_f, a_a, b_d, b_o, m_f, m_a, dots_o, norm_o, dots_d, norm_d],
        "s" + "h" * 10,
        [shape_of((N_Z * unit, BLOCK), bf16), shape_of((N_Z * unit, BLOCK), f32)],
        [pltpu.VMEM((N_MP * unit, BLOCK), f32), pltpu.VMEM((1, (n_blocks - COUNT_FLAT) * BLOCK), f32)],
        name="pack",
    )
    p1, p2, p3, own = run(
        pair_kernel,
        [where, kept, mp_swap(give, 1)],
        "shh",
        [shape_of((unit, BLOCK), bf16)] * 3 + [shape_of((unit, BLOCK), f32)],
        name="pack_sums",
        us=0.1,
    )
    p1, p2, p3, own, own_grads = run(
        pair_grads_kernel,
        [where, keep, mp_swap(send, 1), kept, mp_swap(give, 1)],
        "shhhh",
        [shape_of((share + unit // 2, D), bf16)] * 3 + [shape_of((share, D), f32), shape_of((unit, BLOCK), f32)],
        name="pair_grads",
        us=1.2,
    )
    sums = [own, mp_swap(p1, 2), mp_swap(p2, 4), mp_swap(p3, 6)]
    local_own, p1, p2, p3 = run(
        local_kernel,
        [where, own_grads] + sums[1:] + [b_f, b_a, a_d, a_o],
        "s" + "h" * 8,
        [shape_of((part, BLOCK), f32)] + [shape_of((part, BLOCK), bf16)] * 3,
        [pltpu.VMEM((N_DP * part, BLOCK), f32)],
        name="local_sums",
        us=0.1,
    )
    own = run(
        last_sum_kernel,
        [local_own, dp_swap(p1, 1), dp_swap(p2, 2), dp_swap(p3, 3)],
        "hhhh",
        [shape_of((part, BLOCK), bf16)],
        name="last_sums",
        us=0.1,
    )[0]
    last_piece = run(
        last_rows_kernel,
        sums + [tokens_here, grad_two, norm_gains] + sums_d + [x_two, scale_d],
        "h" * 13,
        [shape_of((2 * share, D), bf16)],
        name="last_rows",
        us=20,
    )[0]
    lines = jnp.concatenate([own] + [mp_swap(own, 2 * step) for step in range(1, N_Z)])
    summed = [lines] + [dp_swap(lines, step) for step in range(1, N_DP)]
    summed = summed + [mp_swap(one, 1) for one in summed]

    second = mp_swap(last_piece, 4)
    pieces = [last_piece, mp_swap(last_piece, 2), second, mp_swap(second, 2)]
    pieces = pieces + [mp_swap(one, 1) for one in pieces]
    input_grad, layer_out = run(
        join_kernel,
        [where] + pieces,
        "s" + "h" * 8,
        [shape_of((rows, D), f32), shape_of((rows, D), bf16)],
        name="join_rows",
        megabytes=8,
        us=0.1,
    )

    table = np.zeros((n_blocks,), np.int32)

    def note(block, m, r):
        table[block] = ((r // part) * N_MP + m) * 64 + r % part

    def split_pairs(count, r):
        return r // 2 + (r % 2) * (count // 2)

    def blocks_of(names):
        def listing(count, m):
            each = count // len(names)
            for position, blocks in enumerate(names):
                for k, block in enumerate(blocks(m)):
                    if block is not None:
                        yield position * each + split_pairs(each, k), block

        return listing

    def lower_columns(p):
        return lambda m: [starts[("A", p)] + int(k) for k in by_dp]

    def upper_rows(p):
        return lambda m: [starts[("B", p)] + int(k) for k in all_blocks]

    def lower_rows(p, per):
        return lambda m: [starts[("A", p)] + m * per + k for k in range(per)]

    def upper_columns(p):
        if p < 3:
            return lambda m: [starts[("B", p)] + m * 4 + k for k in range(4)]
        return lambda m: [
            starts[("B", p)] + (m // 2) * 22 + (m % 2) * 10 + k
            if (k < 11 if m % 2 == 0 else k >= 1)
            else None
            for k in range(12)
        ]

    begin = 0
    for listing, count in (
        (blocks_of([lower_columns(4), lower_columns(5)]), a_f.shape[0]),
        (blocks_of([lower_columns(p) for p in range(3)]), a_a.shape[0]),
        (blocks_of([upper_rows(6)]), b_d.shape[0]),
        (blocks_of([upper_rows(3)]), b_o.shape[0]),
        (lambda count, m: [(r, COUNT_FLAT + r) for r in range(count)], n_blocks - COUNT_FLAT),
    ):
        for r, block in listing(count, None):
            note(block, (begin + r) // unit, (begin + r) % unit)
        begin += count
    begin = unit
    for listing, count in (
        (blocks_of([upper_columns(4), upper_columns(5)]), b_f.shape[0]),
        (blocks_of([upper_columns(p) for p in range(3)]), b_a.shape[0]),
        (blocks_of([lower_rows(6, 11)]), a_d.shape[0]),
        (blocks_of([lower_rows(3, 4)]), a_o.shape[0]),
    ):
        for m in range(N_MP):
            for r, block in listing(count, m):
                note(block, m, begin + r)
        begin += count
    me = di * N_MP + mi
    hits = (owners * capacity + ranks)[None, :] == me * capacity + jnp.arange(capacity)[:, None]
    mine = jnp.sum(jnp.where(hits, jnp.arange(n_blocks)[None, :] + 1, 0), axis=1) - 1
    code = jnp.sum(jnp.where(hits, jnp.asarray(table)[None, :], 0), axis=1)
    device, inner = code // 64, code % 64
    d_from, m_from = device // N_MP, device % N_MP
    list_at = (((m_from % 2) ^ core) * N_DP + (d_from ^ di)) * N_Z + ((m_from // 2) ^ zi)
    index = list_at * part + inner
    new_master, new_first, new_second = run(
        update_kernel,
        [index[:, None], mine[:, None]] + summed + [master, first_moment, second_moment],
        "vv" + "h" * 11,
        [shape_of(master.shape, f32)] * 3,
        name="update", megabytes=4, us=2,
    )
    return (layer_out, input_grad, new_master, new_first, new_second)


def solution(mesh):
    fast = mesh.shape["dp"] == 4 and mesh.shape["mp"] == 8
    return jax.shard_map(
        fast_body if fast else body,
        mesh=mesh,
        in_specs=(
            P("dp", None),
            P("dp", None),
            P(),
            P(None, "mp", None),
            P(None, "mp", None),
            P("mp", None),
            P("dp", None),
            P(),
            P(("dp", "mp"), None),
            P(("dp", "mp"), None),
            P(("dp", "mp"), None),
        ),
        out_specs=(
            P("dp", None),
            P("dp", None),
            P(("dp", "mp"), None),
            P(("dp", "mp"), None),
            P(("dp", "mp"), None),
        ),
        check_vma=False,
    )
```
